32 devices in a mesh: fsdp: 16 (over z, x, core), tp: 2 (over y).
Axes of the slice: x: 2, y: 2, z: 4, core: 2. Of those that a mesh axis runs over, the one named last changes fastest.
Arguments:
- clean_patches: float32 [256, 256, 16], P(('fsdp', 'tp')), may hold values from -6 to 6
- noise_patches: float32 [256, 256, 16], P(('fsdp', 'tp'))
- timesteps: int32 [256], P('fsdp'), may hold values from 0 to 999
- labels: int32 [256], P('fsdp'), may hold values from 0 to 31
- qkv_weight: float32 [2, 1024, 3072], P(None, 'fsdp', 'tp'), may hold values from -0.125 to 0.125
- out_weight: float32 [2, 1024, 1024], P(None, 'tp', 'fsdp')
- expand_weight: float32 [2, 1024, 4096], P(None, 'fsdp', 'tp'), may hold values from -0.1875 to 0.1875
- reduce_weight: float32 [2, 4096, 1024], P(None, 'tp', 'fsdp')
- modulate_weight: float32 [1024, 14336], P('fsdp', 'tp'), may hold values from -0.09375 to 0.09375
- embed_weight: float32 [1344, 1024], P(None, ('fsdp', 'tp'))
- bias_vector: float32 [29696], P(('fsdp', 'tp'))
- qkv_first: float32 [2, 1024, 3072], P(None, 'fsdp', 'tp'), may hold values from -9.536743e-06 to 9.536743e-06
- out_first: float32 [2, 1024, 1024], P(None, 'tp', 'fsdp'), may hold values from -9.536743e-06 to 9.536743e-06
- expand_first: float32 [2, 1024, 4096], P(None, 'fsdp', 'tp'), may hold values from -9.536743e-06 to 9.536743e-06
- reduce_first: float32 [2, 4096, 1024], P(None, 'tp', 'fsdp'), may hold values from -9.536743e-06 to 9.536743e-06
- modulate_first: float32 [1024, 14336], P('fsdp', 'tp'), may hold values from -9.536743e-06 to 9.536743e-06
- embed_first: float32 [1344, 1024], P(None, ('fsdp', 'tp')), may hold values from -9.536743e-06 to 9.536743e-06
- bias_first: float32 [29696], P(('fsdp', 'tp')), may hold values from -3.8146973e-05 to 3.8146973e-05
- qkv_second: float32 [2, 1024, 3072], P(None, 'fsdp', 'tp'), may hold values from 2.4241342e-12 to 9.696537e-12
- out_second: float32 [2, 1024, 1024], P(None, 'tp', 'fsdp'), may hold values from 2.4241342e-12 to 9.696537e-12
- expand_second: float32 [2, 1024, 4096], P(None, 'fsdp', 'tp'), may hold values from 2.4241342e-12 to 9.696537e-12
- reduce_second: float32 [2, 4096, 1024], P(None, 'tp', 'fsdp'), may hold values from 2.4241342e-12 to 9.696537e-12
- modulate_second: float32 [1024, 14336], P('fsdp', 'tp'), may hold values from 2.4241342e-12 to 9.696537e-12
- embed_second: float32 [1344, 1024], P(None, ('fsdp', 'tp')), may hold values from 2.4241342e-12 to 9.696537e-12
- bias_second: float32 [29696], P(('fsdp', 'tp')), may hold values from 3.8786148e-11 to 1.5514459e-10
Outputs:
- loss_total: float32 [], replicated
- grad_norm: float32 [], replicated
- qkv_moment: float32 [2, 1024, 3072], P(None, 'fsdp', 'tp')
- qkv_square: float32 [2, 1024, 3072], P(None, 'fsdp', 'tp')
- qkv_master: float32 [2, 1024, 3072], P(None, 'fsdp', 'tp')
- out_moment: float32 [2, 1024, 1024], P(None, 'tp', 'fsdp')
- out_square: float32 [2, 1024, 1024], P(None, 'tp', 'fsdp')
- out_master: float32 [2, 1024, 1024], P(None, 'tp', 'fsdp')
- expand_moment: float32 [2, 1024, 4096], P(None, 'fsdp', 'tp')
- expand_square: float32 [2, 1024, 4096], P(None, 'fsdp', 'tp')
- expand_master: float32 [2, 1024, 4096], P(None, 'fsdp', 'tp')
- reduce_moment: float32 [2, 4096, 1024], P(None, 'tp', 'fsdp')
- reduce_square: float32 [2, 4096, 1024], P(None, 'tp', 'fsdp')
- reduce_master: float32 [2, 4096, 1024], P(None, 'tp', 'fsdp')
- modulate_moment: float32 [1024, 14336], P('fsdp', 'tp')
- modulate_square: float32 [1024, 14336], P('fsdp', 'tp')
- modulate_master: float32 [1024, 14336], P('fsdp', 'tp')
- embed_moment: float32 [1344, 1024], P(None, ('fsdp', 'tp'))
- embed_square: float32 [1344, 1024], P(None, ('fsdp', 'tp'))
- embed_master: float32 [1344, 1024], P(None, ('fsdp', 'tp'))
- bias_moment: float32 [29696], P(('fsdp', 'tp'))
- bias_square: float32 [29696], P(('fsdp', 'tp'))
- bias_master: float32 [29696], P(('fsdp', 'tp'))
- qkv_copy: bfloat16 [2, 1024, 3072], P(None, 'fsdp', 'tp')
- out_copy: bfloat16 [2, 1024, 1024], P(None, 'tp', 'fsdp')
- expand_copy: bfloat16 [2, 1024, 4096], P(None, 'fsdp', 'tp')
- reduce_copy: bfloat16 [2, 4096, 1024], P(None, 'tp', 'fsdp')
- modulate_copy: bfloat16 [1024, 14336], P('fsdp', 'tp')
- embed_copy: bfloat16 [1344, 1024], P(None, ('fsdp', 'tp'))
The draws below stay inside these ranges and needn't reach their ends.
All inputs are finite; a program needn't handle non-finite values.
Results may differ from the reference program's by a relative error of at most 0.0079.
The reference program's roundings to bfloat16 on the way count: a program that leaves them out, or rounds other values in their place, can miss the bound.
Values may be sent and summed in bfloat16 or wider, within the bound.
A program may use at most 640 MiB of HBM per device.

```python
import math
import jax
import jax.numpy as jnp
from jax import lax

D = 1024
HEADS = 16
HEAD = 64
FF = 4096
CH = 16
FREQ = 256
CLASSES = 32
SIDE = 16
LAYERS = 2
MB = 2
STEP = 10
LAT_MB = 8
TOK_LAT = 256
LATENTS = 256
MODS = 14336
EROWS = 1344
BIAS_LEN = 29696
PARAMS = 41251840


def draw_noise_patches(key, part):
    key = jax.random.fold_in(key, 11)
    shape = (LATENTS, TOK_LAT, CH)
    values = jax.random.normal(key, shape, jnp.float32)
    reach = 2.0
    block = LAT_MB * MB
    index = jnp.arange(LATENTS, dtype=jnp.int32)
    outer = index.astype(jnp.float32) / LATENTS
    inner = (index % block).astype(jnp.float32) / block
    level = jnp.sqrt((1.0 + reach * outer) * (1.0 + reach * inner))
    return values * level[:, None, None]


def draw_out_weight(key, part):
    key = jax.random.fold_in(key, 12)
    shape = (LAYERS, D, D)
    values = jax.random.normal(key, shape, jnp.float32)
    reach = 2.0
    ramp = 1.0 + reach * jnp.arange(D, dtype=jnp.float32) / D
    return values * ramp[None, :, None] / math.sqrt(D)


def draw_reduce_weight(key, part):
    key = jax.random.fold_in(key, 13)
    shape = (LAYERS, FF, D)
    values = jax.random.normal(key, shape, jnp.float32)
    reach = 2.0
    ramp = 1.0 + reach * jnp.arange(FF, dtype=jnp.float32) / FF
    return values * ramp[None, :, None] / math.sqrt(FF)


def draw_embed_weight(key, part):
    key = jax.random.fold_in(key, 14)
    shape = (EROWS, D)
    values = jax.random.normal(key, shape, jnp.float32)
    rows = jnp.arange(EROWS, dtype=jnp.int32)
    scale = jnp.where(rows < FREQ, 1.0 / math.sqrt(FREQ), jnp.where(rows < FREQ + D, 1.0 / math.sqrt(D), jnp.where(rows < FREQ + D + CH, 1.0 / math.sqrt(CH), jnp.where(rows < FREQ + D + CH + CLASSES, 0.15, 1.0 / math.sqrt(D)))))
    return values * scale[:, None]


def draw_bias_vector(key, part):
    key = jax.random.fold_in(key, 15)
    values = jax.random.normal(key, (BIAS_LEN,), jnp.float32)
    reach = 2.0
    count = 6 * LAYERS + 2
    head = values[:count * D].reshape(count, D)
    kind = (jnp.arange(count, dtype=jnp.int32) % 6)[:, None]
    ramp = reach * jnp.arange(D, dtype=jnp.float32)[None, :] / D
    head = jnp.where(kind == 1, ramp + 0.1 * head, jnp.where((kind == 2) | (kind == 5), 1.0 + 0.3 * head, 0.3 * head))
    return jnp.concatenate([head.reshape(-1), 0.2 * values[count * D:]])


def touch_ends(entries, rng, smallest, high):
    index_at = [jax.random.randint(jax.random.fold_in(rng, axis), (), 0, length) for axis, length in enumerate(entries.shape)]
    main_axis = entries.shape.index(max(entries.shape))
    neighbour = index_at[:main_axis] + [(index_at[main_axis] + 1) % entries.shape[main_axis]] + index_at[main_axis + 1:]
    return entries.at[tuple(index_at)].set(smallest).at[tuple(neighbour)].set(high)


def block_levels(rng, dims, split, smallest, high):
    loudness, own = 1.0, jax.random.fold_in(rng, 6)
    for position, shards_of in split:
        draws = jnp.exp(jax.random.uniform(jax.random.fold_in(own, position), (shards_of,), jnp.float32, smallest / len(split), high / len(split)))
        loudness = loudness * jnp.repeat(draws, dims[position] // shards_of).reshape([-1 if axis == position else 1 for axis in range(len(dims))])
    return loudness


def bell_draw(rng, extent, scale, most, shards=(), kind=jnp.bfloat16):
    level = block_levels(rng, extent, shards, -0.22, 0.18) if shards else 1.0
    result = jax.random.normal(rng, extent, jnp.float32) * scale * level
    return jnp.minimum(jnp.maximum(result, -most), most).astype(kind)


def setup_inputs(seed: int = 0) -> dict:
    arg_keys = jax.random.split(jax.random.key(seed), 26)
    return {
        "clean_patches": bell_draw(arg_keys[0], (LATENTS, TOK_LAT, CH), 1.0, 6.0, ((0, 32),), jnp.float32),
        "noise_patches": draw_noise_patches(jax.random.fold_in(arg_keys[25], 71), 0),
        "timesteps": touch_ends(jax.random.randint(arg_keys[2], (LATENTS,), 0, 1000), jax.random.fold_in(arg_keys[2], 1), 0, 999).astype(jnp.int32),
        "labels": touch_ends(jax.random.randint(arg_keys[3], (LATENTS,), 0, CLASSES), jax.random.fold_in(arg_keys[3], 1), 0, CLASSES - 1).astype(jnp.int32),
        "qkv_weight": bell_draw(arg_keys[4], (LAYERS, D, 3 * D), (2 * D) ** -0.5, 0.125, ((1, 16), (2, 2)), jnp.float32),
        "out_weight": draw_out_weight(jax.random.fold_in(arg_keys[25], 71), 0),
        "expand_weight": bell_draw(arg_keys[6], (LAYERS, D, FF), D ** -0.5, 0.1875, ((1, 16), (2, 2)), jnp.float32),
        "reduce_weight": draw_reduce_weight(jax.random.fold_in(arg_keys[25], 71), 0),
        "modulate_weight": bell_draw(arg_keys[8], (D, MODS), (4 * D) ** -0.5, 0.09375, ((0, 16), (1, 2)), jnp.float32),
        "embed_weight": draw_embed_weight(jax.random.fold_in(arg_keys[25], 71), 0),
        "bias_vector": draw_bias_vector(jax.random.fold_in(arg_keys[25], 71), 0),
        "qkv_first": bell_draw(arg_keys[11], (LAYERS, D, 3 * D), (1 / (100 * PARAMS ** 0.5)), 9.5367431640625e-06, ((1, 16), (2, 2)), jnp.float32),
        "out_first": bell_draw(arg_keys[12], (LAYERS, D, D), (1 / (100 * PARAMS ** 0.5)), 9.5367431640625e-06, ((1, 2), (2, 16)), jnp.float32),
        "expand_first": bell_draw(arg_keys[13], (LAYERS, D, FF), (1 / (100 * PARAMS ** 0.5)), 9.5367431640625e-06, ((1, 16), (2, 2)), jnp.float32),
        "reduce_first": bell_draw(arg_keys[14], (LAYERS, FF, D), (1 / (100 * PARAMS ** 0.5)), 9.5367431640625e-06, ((1, 2), (2, 16)), jnp.float32),
        "modulate_first": bell_draw(arg_keys[15], (D, MODS), (1 / (100 * PARAMS ** 0.5)), 9.5367431640625e-06, ((0, 16), (1, 2)), jnp.float32),
        "embed_first": bell_draw(arg_keys[16], (EROWS, D), (1 / (100 * PARAMS ** 0.5)), 9.5367431640625e-06, ((1, 32),), jnp.float32),
        "bias_first": bell_draw(arg_keys[17], (BIAS_LEN,), (4 / (100 * PARAMS ** 0.5)), 3.814697265625e-05, ((0, 32),), jnp.float32),
        "qkv_second": jnp.clip(jnp.exp(math.log(9.696536976133707e-12) - 1.3862944 * jax.random.uniform(arg_keys[18], (LAYERS, D, 3 * D), jnp.float32) ** block_levels(arg_keys[18], (LAYERS, D, 3 * D), ((1, 16), (2, 2)), -0.2, 0.2)), 2.424134244033427e-12, 9.696536976133707e-12),
        "out_second": jnp.clip(jnp.exp(math.log(9.696536976133707e-12) - 1.3862944 * jax.random.uniform(arg_keys[19], (LAYERS, D, D), jnp.float32) ** block_levels(arg_keys[19], (LAYERS, D, D), ((1, 2), (2, 16)), -0.2, 0.2)), 2.424134244033427e-12, 9.696536976133707e-12),
        "expand_second": jnp.clip(jnp.exp(math.log(9.696536976133707e-12) - 1.3862944 * jax.random.uniform(arg_keys[20], (LAYERS, D, FF), jnp.float32) ** block_levels(arg_keys[20], (LAYERS, D, FF), ((1, 16), (2, 2)), -0.2, 0.2)), 2.424134244033427e-12, 9.696536976133707e-12),
        "reduce_second": jnp.clip(jnp.exp(math.log(9.696536976133707e-12) - 1.3862944 * jax.random.uniform(arg_keys[21], (LAYERS, FF, D), jnp.float32) ** block_levels(arg_keys[21], (LAYERS, FF, D), ((1, 2), (2, 16)), -0.2, 0.2)), 2.424134244033427e-12, 9.696536976133707e-12),
        "modulate_second": jnp.clip(jnp.exp(math.log(9.696536976133707e-12) - 1.3862944 * jax.random.uniform(arg_keys[22], (D, MODS), jnp.float32) ** block_levels(arg_keys[22], (D, MODS), ((0, 16), (1, 2)), -0.2, 0.2)), 2.424134244033427e-12, 9.696536976133707e-12),
        "embed_second": jnp.clip(jnp.exp(math.log(9.696536976133707e-12) - 1.3862944 * jax.random.uniform(arg_keys[23], (EROWS, D), jnp.float32) ** block_levels(arg_keys[23], (EROWS, D), ((1, 32),), -0.2, 0.2)), 2.424134244033427e-12, 9.696536976133707e-12),
        "bias_second": jnp.clip(jnp.exp(math.log(1.5514459161813932e-10) - 1.3862944 * jax.random.uniform(arg_keys[24], (BIAS_LEN,), jnp.float32) ** block_levels(arg_keys[24], (BIAS_LEN,), ((0, 32),), -0.2, 0.2)), 3.878614790453483e-11, 1.5514459161813932e-10),
    }


CLIP_AT = 0.01
RATE = 0.05
BETA_ONE = 0.5
BETA_TWO = 0.5
DECAY = 0.01
ADAM_EPS = 1e-08
NORM_EPS = 1e-06
EXACT = lax.Precision.HIGHEST

@jax.custom_vjp
def low(v):
    return lax.optimization_barrier(v.astype(jnp.bfloat16)).astype(jnp.float32)

@jax.custom_vjp
def low_back(v):
    return v

def low_keep(v):
    return (low(v), None)

def low_pass(kept, grad):
    return (grad,)

def back_keep(v):
    return (v, None)

def back_low(kept, grad):
    return (low(grad),)
low.defvjp(low_keep, low_pass)
low_back.defvjp(back_keep, back_low)

def product(left, right):
    return jnp.einsum('...i,ij->...j', left, right, precision=EXACT)

def layer_norm(value):
    center = value - lax.optimization_barrier(jnp.mean(value, -1, keepdims=True))
    return center * lax.rsqrt(lax.optimization_barrier(jnp.mean(center * center, -1, keepdims=True)) + NORM_EPS)

def noise_levels(steps):
    angle = (steps.astype(jnp.float32) / 1000.0 + 0.008) / 1.008 * (math.pi / 2)
    return (jnp.cos(angle), jnp.sin(angle))

def step_features(steps):
    half = FREQ // 2
    rates = jnp.exp(-math.log(10000.0) * jnp.arange(half, dtype=jnp.float32) / half)
    phase = steps.astype(jnp.float32)[:, None] * rates[None, :]
    return jnp.concatenate([jnp.cos(phase), jnp.sin(phase)], axis=1)

def place_table():
    quarter = D // 4
    rates = 1.0 / 10000.0 ** (jnp.arange(quarter, dtype=jnp.float32) / quarter)
    index = jnp.arange(TOK_LAT, dtype=jnp.int32)
    rows = (index // SIDE).astype(jnp.float32)[:, None] * rates[None, :]
    columns = (index % SIDE).astype(jnp.float32)[:, None] * rates[None, :]
    return jnp.concatenate([jnp.sin(rows), jnp.cos(rows), jnp.sin(columns), jnp.cos(columns)], axis=1)

def split_embed(embed):
    start = FREQ + D
    return (embed[:FREQ], embed[FREQ:start], embed[start:start + CH], embed[start + CH:start + CH + CLASSES], embed[start + CH + CLASSES:])

def split_bias(bias):
    layers = []
    for layer in range(LAYERS):
        base = MODS + layer * (2 * D + FF)
        layers.append((bias[base:base + D], bias[base + D:base + D + FF], bias[base + D + FF:base + 2 * D + FF]))
    tail = MODS + LAYERS * (2 * D + FF)
    return (bias[:MODS], layers, bias[tail:tail + D], bias[tail + D:tail + 2 * D], bias[tail + 2 * D:tail + 3 * D])

def block(stream, modulation, w_qkv, w_out, w_expand, w_reduce, out_bias, expand_bias, reduce_bias):
    count = stream.shape[0]
    shift_a, scale_a, gate_a, shift_m, scale_m, gate_m = [modulation[:, i, None, :] for i in range(6)]
    seq_a = low(layer_norm(stream) * (1.0 + scale_a) + shift_a)
    qkv = low_back(low(product(seq_a, low(w_qkv)))).reshape(count, TOK_LAT, HEADS, 3, HEAD)
    query, key, value = (qkv[:, :, :, 0], qkv[:, :, :, 1], qkv[:, :, :, 2])
    scores = low_back(jnp.einsum('gqhe,gkhe->ghqk', query, key, precision=EXACT) / math.sqrt(HEAD))
    probs = low(jax.nn.softmax(scores, axis=-1))
    att = jnp.einsum('ghqk,gkhe->gqhe', probs, value, precision=EXACT).reshape(count, TOK_LAT, D)
    att = low_back(low(att))
    branch_a = low_back(product(att, low(w_out)))
    mid = stream + gate_a * (branch_a + out_bias)
    seq_m = low(layer_norm(mid) * (1.0 + scale_m) + shift_m)
    pre = low_back(product(seq_m, low(w_expand)) + expand_bias)
    branch_m = low_back(product(low(jax.nn.gelu(pre, approximate=True)), low(w_reduce)))
    return mid + gate_m * (branch_m + reduce_bias)

def group_loss(params, clean, noise, steps, classes):
    w_qkv, w_out, w_expand, w_reduce, w_mod, embed, bias = params
    step_in, step_out, patch_in, table, patch_out = split_embed(embed)
    ada_bias, layer_bias, step_in_bias, step_out_bias, patch_bias = split_bias(bias)
    signal, spread = noise_levels(steps)
    noisy = signal[:, None, None] * clean + spread[:, None, None] * noise
    hidden = jax.nn.silu(product(low(step_features(steps)), low(step_in)) + step_in_bias)
    onehot = (classes[:, None] == jnp.arange(CLASSES, dtype=jnp.int32)[None, :]).astype(jnp.float32)
    cond = product(low(hidden), low(step_out)) + step_out_bias + product(onehot, low(table))
    mods = low_back(product(low(jax.nn.silu(cond)), low(w_mod)) + ada_bias).reshape(-1, 6 * LAYERS + 2, D)
    stream = low_back(product(low(noisy), low(patch_in)) + patch_bias) + place_table()[None]
    for layer in range(LAYERS):
        out_bias, expand_bias, reduce_bias = layer_bias[layer]
        stream = block(stream, mods[:, 6 * layer:6 * layer + 6], w_qkv[layer], w_out[layer], w_expand[layer], w_reduce[layer], out_bias, expand_bias, reduce_bias)
    final = layer_norm(stream) * (1.0 + mods[:, 6 * LAYERS + 1, None, :]) + mods[:, 6 * LAYERS, None, :]
    pred = low_back(product(low(final), low(patch_out).T))
    error = pred - noise
    return jnp.sum(error * error)

def adam(weight, first, second, grad, factor):
    grad = grad * factor
    new_first = BETA_ONE * first + (1.0 - BETA_ONE) * grad
    new_second = BETA_TWO * second + (1.0 - BETA_TWO) * grad * grad
    first_hat = new_first / (1.0 - BETA_ONE ** STEP)
    second_hat = new_second / (1.0 - BETA_TWO ** STEP)
    new_weight = weight - RATE * (first_hat / (jnp.sqrt(second_hat) + ADAM_EPS) + DECAY * weight)
    return (new_first, new_second, new_weight)

def reference(clean_patches, noise_patches, timesteps, labels, qkv_weight, out_weight, expand_weight, reduce_weight, modulate_weight, embed_weight, bias_vector, qkv_first, out_first, expand_first, reduce_first, modulate_first, embed_first, bias_first, qkv_second, out_second, expand_second, reduce_second, modulate_second, embed_second, bias_second):
    params = tuple((p.astype(jnp.float32) for p in (qkv_weight, out_weight, expand_weight, reduce_weight, modulate_weight, embed_weight, bias_vector)))
    total = LATENTS * TOK_LAT * CH
    data = (clean_patches.reshape(-1, LAT_MB, TOK_LAT, CH), noise_patches.reshape(-1, LAT_MB, TOK_LAT, CH), timesteps.reshape(-1, LAT_MB), labels.reshape(-1, LAT_MB))

    def objective(weights):

        def one_group(carry, batch):
            return (carry + jax.checkpoint(group_loss)(weights, *batch), None)
        loss_sum, _ = lax.scan(one_group, jnp.zeros((), jnp.float32), data)
        return (loss_sum / total, loss_sum)
    _, pullback, loss_total = jax.vjp(objective, params, has_aux=True)
    grads = pullback(jnp.ones((), jnp.float32))[0]
    square = jnp.zeros((), jnp.float32)
    for grad in grads:
        square = square + jnp.sum(grad * grad)
    grad_norm = jnp.sqrt(square)
    factor = CLIP_AT / jnp.maximum(grad_norm, CLIP_AT)
    firsts = (qkv_first, out_first, expand_first, reduce_first, modulate_first, embed_first, bias_first)
    seconds = (qkv_second, out_second, expand_second, reduce_second, modulate_second, embed_second, bias_second)
    news = [adam(w, f, s, g, factor) for w, f, s, g in zip(params, firsts, seconds, grads)]
    qkv_moment, qkv_square, qkv_master = news[0]
    out_moment, out_square, out_master = news[1]
    expand_moment, expand_square, expand_master = news[2]
    reduce_moment, reduce_square, reduce_master = news[3]
    modulate_moment, modulate_square, modulate_master = news[4]
    embed_moment, embed_square, embed_master = news[5]
    bias_moment, bias_square, bias_master = news[6]
    return (loss_total, grad_norm, qkv_moment, qkv_square, qkv_master, out_moment, out_square, out_master, expand_moment, expand_square, expand_master, reduce_moment, reduce_square, reduce_master, modulate_moment, modulate_square, modulate_master, embed_moment, embed_square, embed_master, bias_moment, bias_square, bias_master, qkv_master.astype(jnp.bfloat16), out_master.astype(jnp.bfloat16), expand_master.astype(jnp.bfloat16), reduce_master.astype(jnp.bfloat16), modulate_master.astype(jnp.bfloat16), embed_master.astype(jnp.bfloat16))
```

```python
import functools
import math

import jax
import jax.numpy as jnp
from jax import lax
from jax.experimental import pallas as pl
from jax.experimental.pallas import tpu as pltpu
from jax.sharding import PartitionSpec as P

D = 1024
HEAD = 64
FF = 4096
CH = 16
FREQ = 256
CLASSES = 32
SIDE = 16
LAYERS = 2
STEP = 10
TOK_LAT = 256
MODS = 14336


CLIP_AT = 0.01
RATE = 0.05
BETA_ONE = 0.5
BETA_TWO = 0.5
DECAY = 0.01
ADAM_EPS = 1e-08
NORM_EPS = 1e-06
EXACT = lax.Precision.HIGHEST


def contract(left, right, form):
    return jnp.einsum(form, left, right, preferred_element_type=jnp.float32)


def exact_dot(left, right):
    return jnp.dot(left, right, precision=EXACT)


def layer_norm(value):
    center = value - jnp.mean(value, -1, keepdims=True)
    return center * lax.rsqrt(jnp.mean(center * center, -1, keepdims=True) + NORM_EPS)


def gelu_tanh(value):
    return jax.nn.gelu(value, approximate=True)


def local_back(func, value, grad):
    _, pullback = jax.vjp(func, value)
    return pullback(grad)[0]


def noise_levels(steps):
    angle = (steps.astype(jnp.float32) / 1000.0 + 0.008) / 1.008 * (math.pi / 2)
    return (jnp.cos(angle), jnp.sin(angle))


def step_features(steps):
    half = FREQ // 2
    rates = jnp.exp(-math.log(10000.0) * jnp.arange(half, dtype=jnp.float32) / half)
    phase = steps.astype(jnp.float32)[:, None] * rates[None, :]
    return jnp.concatenate([jnp.cos(phase), jnp.sin(phase)], axis=1)


def place_table():
    quarter = D // 4
    rates = 1.0 / 10000.0 ** (jnp.arange(quarter, dtype=jnp.float32) / quarter)
    index = jnp.arange(TOK_LAT, dtype=jnp.int32)
    rows = (index // SIDE).astype(jnp.float32)[:, None] * rates[None, :]
    columns = (index % SIDE).astype(jnp.float32)[:, None] * rates[None, :]
    return jnp.concatenate(
        [jnp.sin(rows), jnp.cos(rows), jnp.sin(columns), jnp.cos(columns)], axis=1
    )


def split_embed(embed):
    start = FREQ + D
    return (
        embed[:FREQ],
        embed[FREQ:start],
        embed[start : start + CH],
        embed[start + CH : start + CH + CLASSES],
        embed[start + CH + CLASSES :],
    )


def split_bias(bias):
    layers = []
    for layer in range(LAYERS):
        base = MODS + layer * (2 * D + FF)
        layers.append(
            (
                bias[base : base + D],
                bias[base + D : base + D + FF],
                bias[base + D + FF : base + 2 * D + FF],
            )
        )
    tail = MODS + LAYERS * (2 * D + FF)
    return (
        bias[:MODS],
        layers,
        bias[tail : tail + D],
        bias[tail + D : tail + 2 * D],
        bias[tail + 2 * D : tail + 3 * D],
    )


LANES = 128
FSDP, TP = ("fsdp", "tp")
GELU_A = math.sqrt(2.0 / math.pi)
GELU_B = 0.044715
VMEM_BYTES = 60 * 1024 * 1024


def swap(value, flip):
    name, bits = (FSDP, flip[0]) if flip[0] else (TP, flip[1])
    return lax.ppermute(value, name, [(i, i ^ bits) for i in range(lax.axis_size(name))])


def bit_flips(name):
    bits = [1 << i for i in range(lax.axis_size(name).bit_length() - 1)]
    return [(bit, 0) if name == FSDP else (0, bit) for bit in bits]


def far_flips():
    return [(k << 2, 0) for k in range(max(lax.axis_size(FSDP) >> 2, 1))]


def middle_flips(first):
    fsdp, tp = (bit_flips(FSDP)[1:2], bit_flips(TP))
    return fsdp + tp if first == FSDP else tp + fsdp


CORE = (1, 0)


def both(one, other):
    return (one[0] ^ other[0], one[1] ^ other[1])


def gather_far(value):
    flips = far_flips()
    held = [value[None]] + [swap(value, flip)[None] for flip in flips[1:]]
    return jnp.concatenate(held, axis=0), flips


def double(held, flips, flip):
    return jnp.concatenate([held, swap(held, flip)], axis=0), flips + [both(f, flip) for f in flips]


def gather_relative(value, hops):
    held, flips = (value[None], [(0, 0)])
    for flip in hops:
        held, flips = double(held, flips, flip)
    return held, flips


def gather_small(value, axes):
    held, _ = gather_relative(value, [flip for name in reversed(axes) for flip in bit_flips(name)])
    return jnp.take(held, jnp.arange(held.shape[0]) ^ lax.axis_index(axes), axis=0)


def split_bit(value, axis, index):
    return lax.index_in_dim(value, index, axis, keepdims=False)


def scatter_sum(value, axes, axis):
    flips = [flip for name in reversed(axes) for flip in bit_flips(name)][::-1]
    count = 1 << len(flips)
    shape = value.shape
    value = value.reshape(shape[:axis] + (count, shape[axis] // count) + shape[axis + 1 :])
    value = jnp.take(value, jnp.arange(count) ^ lax.axis_index(axes), axis=axis)
    keep = jnp.moveaxis(value, axis, 0).reshape(
        (2,) * len(flips) + shape[:axis] + (shape[axis] // count,) + shape[axis + 1 :]
    )
    dims = list(flips)
    for flip in sorted(flips, key=lambda flip: flip != CORE):
        at = dims.index(flip)
        keep = split_bit(keep, at, 0) + swap(split_bit(keep, at, 1), flip)
        dims = dims[:at] + dims[at + 1 :]
    return keep


def exchange_tp(value):
    count, rank = (lax.axis_size(TP), lax.axis_index(TP))
    value = jnp.take(value, jnp.arange(count) ^ rank, axis=0)
    got = jnp.stack([value[0]] + [swap(value[k], (0, k)) for k in range(1, count)])
    return jnp.take(got, jnp.arange(count) ^ rank, axis=0)


def push_kernel(plans, arrays, *refs):
    ins, outs = (refs[:arrays], refs[arrays : 2 * arrays])
    send, recv = refs[2 * arrays :]
    fsdp, tp = (lax.axis_index(FSDP), lax.axis_index(TP))
    count = lax.axis_size(FSDP) * lax.axis_size(TP)
    me = fsdp * lax.axis_size(TP) + tp

    def partner(k):
        other = lax.rem(me + k, count)
        return (other // lax.axis_size(TP), lax.rem(other, lax.axis_size(TP)))

    barrier = pltpu.get_barrier_semaphore()

    def greet(k, carry):
        pl.semaphore_signal(barrier, inc=1, device_id=partner(k), device_id_type=pl.DeviceIdType.MESH)
        return carry

    lax.fori_loop(1, count, greet, 0)
    pl.semaphore_wait(barrier, count - 1)

    def copies(k):
        other = lax.rem(me + k, count)
        found = []
        for i, (plan, source, target) in enumerate(zip(plans, ins, outs)):
            view = source.at[other] if plan == 1 else source
            found.append(
                pltpu.make_async_remote_copy(
                    src_ref=view,
                    dst_ref=target.at[me],
                    send_sem=send.at[i, k],
                    recv_sem=recv.at[i, k],
                    device_id=partner(k),
                    device_id_type=pl.DeviceIdType.MESH,
                )
            )
        return found

    def start(k, carry):
        for plan, copy in zip(plans, copies(k)):
            if plan > 1:
                pl.when(partner(k)[1] < plan - 1)(copy.start)
            else:
                copy.start()
        return carry

    def finish(k, carry):
        for plan, copy in zip(plans, copies(k)):
            if plan > 1:
                pl.when(partner(k)[1] < plan - 1)(copy.wait_send)
                pl.when(tp < plan - 1)(copy.wait_recv)
            else:
                copy.wait()
        return carry

    lax.fori_loop(1, count, start, 0)
    for plan, source, target in zip(plans, ins, outs):
        target[pl.ds(me, 1)] = source[pl.ds(me, 1)] if plan == 1 else source[...][None]
    lax.fori_loop(1, count, finish, 0)


def push(arrays, plans, identity):
    count = lax.axis_size(FSDP) * lax.axis_size(TP)
    shapes = [array.shape[1:] if plan == 1 else array.shape for array, plan in zip(arrays, plans)]
    block = pl.BlockSpec(memory_space=pltpu.VMEM)
    return pl.pallas_call(
        functools.partial(push_kernel, plans, len(arrays)),
        in_specs=[block] * len(arrays),
        out_specs=[block] * len(arrays),
        out_shape=[
            jax.ShapeDtypeStruct((count,) + shape, array.dtype) for shape, array in zip(shapes, arrays)
        ],
        scratch_shapes=[pltpu.SemaphoreType.DMA((len(arrays), count))] * 2,
        compiler_params=pltpu.CompilerParams(
            collective_id=identity, has_side_effects=True, vmem_limit_bytes=VMEM_BYTES
        ),
        cost_estimate=pl.CostEstimate(flops=int(5e9), bytes_accessed=int(5e7), transcendentals=0),
    )(*arrays)


def flipped(index, bits):
    result, bit = (index, 1)
    while bit <= bits:
        if bits & bit:
            result = result + bit * (1 - 2 * lax.rem(index // bit, 2))
        bit *= 2
    return result


def head_kernel(packed, step_in, cond, modulate, shard, *refs):
    packed_all, step_in_all, cond_all, modulate_all, matrix = refs[:5]
    send, recv, small_send, small_recv, local = refs[5:]
    fsdp, tp = (lax.axis_index(FSDP), lax.axis_index(TP))
    tp_count = lax.axis_size(TP)
    count = lax.axis_size(FSDP) * tp_count
    me = fsdp * tp_count + tp
    slot = lax.rem(fsdp, 4)

    def device(k):
        other = lax.rem(me + k, count)
        return (other // tp_count, lax.rem(other, tp_count))

    barrier = pltpu.get_barrier_semaphore()

    def greet(k, carry):
        pl.semaphore_signal(barrier, inc=1, device_id=device(k), device_id_type=pl.DeviceIdType.MESH)
        return carry

    lax.fori_loop(1, count, greet, 0)
    pl.semaphore_wait(barrier, count - 1)

    made = []

    def remote(source, target, flip):
        copy = pltpu.make_async_remote_copy(
            src_ref=source,
            dst_ref=target,
            send_sem=send.at[len(made)],
            recv_sem=recv.at[len(made)],
            device_id=(flipped(fsdp, flip[0]), flipped(tp, flip[1])),
            device_id_type=pl.DeviceIdType.MESH,
        )
        made.append(copy)
        copy.start()
        return copy

    rows, columns = shard.shape

    def region(flip, cols):
        row = pl.multiple_of(flipped(fsdp, flip[0]) * rows, rows)
        return matrix.at[flipped(tp, flip[1]), pl.ds(row, rows), cols]

    every = slice(0, columns)
    far = far_flips()
    own_copies = [
        pltpu.make_async_copy(modulate, modulate_all.at[slot], local.at[0]),
        pltpu.make_async_copy(shard, region((0, 0), every), local.at[1]),
    ]
    for copy in own_copies:
        copy.start()
    near = [remote(modulate, modulate_all.at[slot], (2, 0))]
    under_way = [remote(shard, region((0, 0), every), flip) for flip in far[1:]]
    plane = [(f, t) for f in range(4) for t in range(tp_count)][1:]
    last = [remote(cond, cond_all.at[slot * tp_count + tp], flip) for flip in plane]

    def small(k):
        pairs = ((packed, packed_all), (step_in, step_in_all))
        return [
            pltpu.make_async_remote_copy(
                src_ref=source,
                dst_ref=target.at[me],
                send_sem=small_send.at[i, k],
                recv_sem=small_recv.at[i, k],
                device_id=device(k),
                device_id_type=pl.DeviceIdType.MESH,
            )
            for i, (source, target) in enumerate(pairs)
        ]

    def start_small(k, carry):
        for copy in small(k):
            copy.start()
        return carry

    def finish_small(k, carry):
        for copy in small(k):
            copy.wait()
        return carry

    lax.fori_loop(1, count, start_small, 0)
    packed_all[pl.ds(me, 1)] = packed[...][None]
    step_in_all[pl.ds(me, 1)] = step_in[...][None]
    cond_all[pl.ds(slot * tp_count + tp, 1)] = cond[...][None]
    for copy in own_copies:
        copy.wait()
    for copy in near:
        copy.wait()
    last.append(remote(modulate, modulate_all.at[slot], CORE))
    partner = flipped(slot, 2)
    last.append(remote(modulate_all.at[partner], modulate_all.at[partner], CORE))
    for copy in under_way:
        copy.wait()
    orders = (middle_flips(FSDP), middle_flips(TP))
    held = [list(far), list(far)]
    halves = (slice(0, columns // 2), slice(columns // 2, columns))
    for step in range(len(orders[0])):
        under_way = []
        for color, cols in enumerate(halves):
            flip = orders[color][step]
            under_way += [remote(region(f, cols), region(f, cols), flip) for f in held[color]]
            held[color] = held[color] + [both(f, flip) for f in held[color]]
        for copy in under_way:
            copy.wait()
    last += [remote(region(f, every), region(f, every), CORE) for f in held[0]]
    lax.fori_loop(1, count, finish_small, 0)
    for copy in last:
        copy.wait()


def run_head(packed, step_in, cond, modulate, shard, identity):
    tp, fsdp = (lax.axis_size(TP), lax.axis_size(FSDP))
    count = fsdp * tp
    rows, columns = shard.shape
    vmem = pl.BlockSpec(memory_space=pltpu.VMEM)
    total = fsdp // 4 + 4 * tp + 2 + 2 * (fsdp // 4) * (2 * tp - 1) + fsdp * tp
    shapes = [
        ((count,) + packed.shape, F32),
        ((count,) + step_in.shape, BF16),
        ((4 * tp,) + cond.shape, BF16),
        ((4,) + modulate.shape, BF16),
        ((tp, rows * fsdp, columns), BF16),
    ]
    return pl.pallas_call(
        head_kernel,
        in_specs=[vmem] * 3 + [ANY] * 2,
        out_specs=[vmem] * 3 + [ANY] * 2,
        out_shape=[jax.ShapeDtypeStruct(shape, dtype) for shape, dtype in shapes],
        scratch_shapes=[pltpu.SemaphoreType.DMA((total,))] * 2
        + [pltpu.SemaphoreType.DMA((2, count))] * 2
        + [pltpu.SemaphoreType.DMA((2,))],
        compiler_params=pltpu.CompilerParams(
            collective_id=identity, has_side_effects=True, vmem_limit_bytes=VMEM_BYTES
        ),
        cost_estimate=pl.CostEstimate(flops=int(4e10), bytes_accessed=int(1e8), transcendentals=0),
    )(packed, step_in, cond, modulate, shard)


def padded(vector):
    return jnp.pad(vector, (0, -vector.shape[0] % (8 * LANES))).reshape(-1, LANES)


class GradientSum:
    def __init__(self, keep, send, first):
        fsdp = bit_flips(FSDP)
        self.dims = bit_flips(TP)[::-1] + fsdp[2:][::-1] + fsdp[1:2]
        self.rows, self.columns = (keep.shape[1] * 2 // lax.axis_size(FSDP), keep.shape[2])
        self.flips = middle_flips(first)[::-1]
        self.keep = keep.reshape((2,) * len(self.dims) + (self.rows, self.columns))
        self.sent = send
        self.next = CORE
        self.far = None

    def step(self):
        got = swap(self.sent, self.next).reshape(self.keep.shape)

        def part(axis, index):
            return split_bit(self.keep, axis, index).astype(F32) + split_bit(got, axis, index).astype(F32)

        if self.flips:
            self.next = self.flips.pop(0)
            axis = self.dims.index(self.next)
            self.sent, self.keep = (part(axis, 1).astype(BF16), part(axis, 0).astype(BF16))
            self.dims = self.dims[:axis] + self.dims[axis + 1 :]
            return [self.sent]
        blocks = (-1, self.rows, self.columns)
        self.keep, got = (self.keep.reshape(blocks), got.reshape(blocks))
        self.far = [part(0, k).astype(BF16) for k in range(1, self.keep.shape[0])]
        self.keep = part(0, 0)
        return self.far

    def finish(self):
        result = self.keep
        for flip, sent in zip(far_flips()[1:], self.far):
            result = result + swap(sent, flip).astype(F32)
        return result


def nt_dot(left, right):
    return lax.dot_general(left, right, (((1,), (1,)), ((), ())), preferred_element_type=jnp.float32)


def nn_dot(left, right):
    return lax.dot_general(left, right, (((1,), (0,)), ((), ())), preferred_element_type=jnp.float32)


def tn_dot(left, right):
    return lax.dot_general(left, right, (((0,), (0,)), ((), ())), preferred_element_type=jnp.float32)


def norm_parts(value):
    center = value - jnp.mean(value, -1, keepdims=True)
    inverse = lax.rsqrt(jnp.mean(center * center, -1, keepdims=True) + NORM_EPS)
    return center * inverse, inverse


def norm_back(normed, inverse, grad):
    mean_grad = jnp.mean(grad, -1, keepdims=True)
    mean_both = jnp.mean(grad * normed, -1, keepdims=True)
    return inverse * (grad - mean_grad - normed * mean_both)


def row_sum(value):
    return jnp.sum(value, axis=0, keepdims=True)


def column_copy(start, ref, target, sem):
    return [pltpu.make_async_copy(ref.at[:, :, pl.ds(start, target.shape[2])], target, sem)]


def run_copies(*groups):
    for group in groups:
        for copy in group:
            copy.start()
    for group in groups:
        for copy in group:
            copy.wait()


def lane_masks(dtype):
    lane = lax.broadcasted_iota(jnp.int32, (1, LANES), 1)
    return [((lane // HEAD) == i).astype(jnp.float32).astype(dtype) for i in range(LANES // HEAD)]


def attn_forward_kernel(info, columns, stream, mods, bias, *rest):
    parts, (seq_a, qkv, lse, att, branch, mid, seq_m, weight, sems) = (rest[0], rest[1:])
    tp = weight.shape[0]
    third = columns // 3

    @pl.when(pl.program_id(0) == 0)
    def _():
        run_copies(column_copy(info, parts, weight, sems))

    value = stream[...]
    normed, _ = norm_parts(value)
    seq_a[...] = (normed * (1.0 + mods[0, 1:2, :]) + mods[0, 0:1, :]).astype(jnp.bfloat16)
    for p in range(tp):
        qkv[:, p * columns : (p + 1) * columns] = nn_dot(
            seq_a[...], weight[p, :, :columns]
        ).astype(jnp.bfloat16)
    masks = lane_masks(jnp.bfloat16)
    for p in range(tp):
        for pair in range(third // LANES):
            base = p * columns + pair * LANES
            query = qkv[:, base : base + LANES]
            key = qkv[:, base + third : base + third + LANES]
            val = qkv[:, base + 2 * third : base + 2 * third + LANES]
            out = None
            for i, mask in enumerate(masks):
                scores = nt_dot(key, query * mask) * (1.0 / math.sqrt(HEAD))
                top = jnp.max(scores, axis=0, keepdims=True)
                raised = jnp.exp(scores - top)
                total = row_sum(raised)
                probs = (raised * (1.0 / total)).astype(jnp.bfloat16)
                head = (p * third + pair * LANES) // HEAD + i
                lse[0, head : head + 1, :] = top + jnp.log(total)
                term = tn_dot(probs, val * mask)
                out = term if out is None else out + term
            att[:, p * third + pair * LANES : p * third + (pair + 1) * LANES] = out.astype(jnp.bfloat16)
    total = None
    for p in range(tp):
        term = nt_dot(att[:, p * third : (p + 1) * third], weight[p, :, columns:])
        total = term if total is None else total + term
    branch[...] = total.astype(jnp.bfloat16)
    after = value + mods[0, 2:3, :] * (total + bias[...])
    mid[...] = after
    normed, _ = norm_parts(after)
    seq_m[...] = (normed * (1.0 + mods[0, 4:5, :]) + mods[0, 3:4, :]).astype(jnp.bfloat16)


def gelu_parts(value):
    square = value * value
    inner = GELU_A * (value + GELU_B * (square * value))
    return jnp.tanh(inner), square


def mlp_forward_kernel(info, chunk, seq_m, mid, mods, expand_bias, reduce_bias, *rest):
    parts_e, parts_r, pre, acted, branch, stream, w_expand, w_reduce, sems = rest
    tp, _, columns = w_expand.shape

    @pl.when(pl.program_id(0) == 0)
    def _():
        run_copies(
            column_copy(info[0], parts_e, w_expand, sems.at[0]),
            column_copy(info[1], parts_r, w_reduce, sems.at[1]),
        )

    total = None
    for p in range(tp):
        for start in range(0, columns, chunk):
            cols = slice(p * columns + start, p * columns + start + chunk)
            value = nn_dot(seq_m[...], w_expand[p, :, start : start + chunk]) + expand_bias[:, cols]
            pre[:, cols] = value
            bent, _ = gelu_parts(value)
            hidden = (0.5 * value * (1.0 + bent)).astype(jnp.bfloat16)
            acted[:, cols] = hidden
            term = nt_dot(hidden, w_reduce[p, :, start : start + chunk])
            total = term if total is None else total + term
    branch[...] = total.astype(jnp.bfloat16)
    stream[...] = mid[...] + mods[0, 5:6, :] * (total + reduce_bias[...])


def mlp_backward_kernel(info, chunk, grad_out, branch_m, pre, mid, branch_a, mods, reduce_bias, out_bias, *rest):
    parts_e, parts_r, seq_grad_m, grad_pre, grad_mid, seq_grad_a = rest[:6]
    mod_grads, d_out, d_expand, d_reduce, w_expand, w_reduce, sems = rest[6:]
    tp, _, columns = w_expand.shape

    @pl.when(pl.program_id(0) == 0)
    def _():
        run_copies(
            column_copy(info[0], parts_e, w_expand, sems.at[0]),
            column_copy(info[1], parts_r, w_reduce, sems.at[1]),
        )
        d_out[...] = jnp.zeros_like(d_out)
        d_expand[...] = jnp.zeros_like(d_expand)
        d_reduce[...] = jnp.zeros_like(d_reduce)

    grad = grad_out[...]
    carried = mods[0, 5:6, :] * grad
    d_reduce[...] += row_sum(carried)
    mod_grads[0, 5:6, :] = row_sum(grad * (branch_m[...].astype(jnp.float32) + reduce_bias[...]))
    seq_grad_m[...] = carried.astype(jnp.bfloat16)
    total = None
    for p in range(tp):
        for start in range(0, columns, chunk):
            cols = slice(p * columns + start, p * columns + start + chunk)
            back = nn_dot(seq_grad_m[...], w_reduce[p, :, start : start + chunk])
            value = pre[:, cols]
            bent, square = gelu_parts(value)
            slope = 0.5 * (1.0 + bent) + (0.5 * GELU_A) * value * (1.0 - bent * bent) * (
                1.0 + (3.0 * GELU_B) * square
            )
            low = (back * slope).astype(jnp.bfloat16)
            grad_pre[:, cols] = low
            d_expand[:, cols] += row_sum(low.astype(jnp.float32))
            term = nt_dot(low, w_expand[p, :, start : start + chunk])
            total = term if total is None else total + term
    normed, inverse = norm_parts(mid[...])
    mod_grads[0, 3:4, :] = row_sum(total)
    mod_grads[0, 4:5, :] = row_sum(total * normed)
    after = grad_out[...] + norm_back(normed, inverse, total * (1.0 + mods[0, 4:5, :]))
    grad_mid[...] = after
    mod_grads[0, 2:3, :] = row_sum(after * (branch_a[...].astype(jnp.float32) + out_bias[...]))
    carried = mods[0, 2:3, :] * after
    d_out[...] += row_sum(carried)
    seq_grad_a[...] = carried.astype(jnp.bfloat16)
    mod_grads[0, 0:2, :] = jnp.zeros((2, mod_grads.shape[2]), jnp.float32)


def attn_backward_kernel(info, columns, seq_grad, qkv, lse, stream, grad_mid, mods, *rest):
    parts, (grad_qkv, grad_in, mod_grads, back, weight, sems) = (rest[0], rest[1:])
    tp = weight.shape[0]
    third = columns // 3

    @pl.when(pl.program_id(0) == 0)
    def _():
        run_copies(column_copy(info, parts, weight, sems))

    masks = lane_masks(jnp.bfloat16)
    for p in range(tp):
        back[:, p * third : (p + 1) * third] = nn_dot(
            seq_grad[...], weight[p, :, columns:]
        ).astype(jnp.bfloat16)
    scale = 1.0 / math.sqrt(HEAD)
    for p in range(tp):
        for pair in range(third // LANES):
            base = p * columns + pair * LANES
            query = qkv[:, base : base + LANES]
            key = qkv[:, base + third : base + third + LANES]
            val = qkv[:, base + 2 * third : base + 2 * third + LANES]
            grad = back[:, p * third + pair * LANES : p * third + (pair + 1) * LANES]
            d_query, d_key, d_val = (None, None, None)
            for i, mask in enumerate(masks):
                head = (p * third + pair * LANES) // HEAD + i
                query_i, key_i, grad_i = (query * mask, key * mask, grad * mask)
                scores = nt_dot(key, query_i) * scale
                probs = jnp.exp(scores - lse[0, head : head + 1, :])
                d_probs = nt_dot(val, grad_i)
                d_scores = probs * (d_probs - row_sum(d_probs * probs))
                d_scores = d_scores.astype(jnp.bfloat16)
                terms = (
                    tn_dot(d_scores, key_i),
                    nn_dot(d_scores, query_i),
                    nn_dot(probs.astype(jnp.bfloat16), grad_i),
                )
                if i == 0:
                    d_query, d_key, d_val = terms
                else:
                    d_query, d_key, d_val = (d_query + terms[0], d_key + terms[1], d_val + terms[2])
            grad_qkv[:, base : base + LANES] = (d_query * scale).astype(jnp.bfloat16)
            grad_qkv[:, base + third : base + third + LANES] = (d_key * scale).astype(jnp.bfloat16)
            grad_qkv[:, base + 2 * third : base + 2 * third + LANES] = d_val.astype(jnp.bfloat16)
    total = None
    for p in range(tp):
        term = nt_dot(grad_qkv[:, p * columns : (p + 1) * columns], weight[p, :, :columns])
        total = term if total is None else total + term
    normed, inverse = norm_parts(stream[...])
    mod_grads[0, 0:1, :] = row_sum(total)
    mod_grads[0, 1:2, :] = row_sum(total * normed)
    grad_in[...] = grad_mid[...] + norm_back(normed, inverse, total * (1.0 + mods[0, 1:2, :]))


def final_kernel(scale_pred, stream, mods, noise, patch_out, grad_stream, mod_grads, d_patch, loss):
    @pl.when(pl.program_id(0) == 0)
    def _():
        d_patch[...] = jnp.zeros_like(d_patch)
        loss[...] = jnp.zeros_like(loss)

    normed, inverse = norm_parts(stream[...])
    final = (normed * (1.0 + mods[0, 1:2, :]) + mods[0, 0:1, :]).astype(jnp.bfloat16)
    error = nt_dot(final, patch_out[...]) - noise[0]
    loss[...] += row_sum(error * error)
    grad_pred = (error * scale_pred).astype(jnp.bfloat16)
    d_patch[...] += tn_dot(grad_pred, final)
    grad_final = nn_dot(grad_pred, patch_out[...])
    mod_grads[0, 0:1, :] = row_sum(grad_final)
    mod_grads[0, 1:2, :] = row_sum(grad_final * normed)
    grad_stream[...] = norm_back(normed, inverse, grad_final * (1.0 + mods[0, 1:2, :]))


def weight_grad_kernel(count, groups, place, left, right, *refs):
    turned = refs[-1]
    depth = turned.shape[0]
    rows = depth // count

    @pl.when((pl.program_id(0) == 0) & (pl.program_id(1) == 0))
    def _():
        for start in range(0, depth, LANES):
            block = jnp.transpose(left[:, start : start + LANES])
            for i in range(LANES // rows):
                k = place[0] ^ (start // rows + i)
                slot = (k % 2) * (count // 2) + k // 2
                turned[pl.ds(pl.multiple_of(slot * rows, rows), rows), :] = block[i * rows : (i + 1) * rows]

    half = depth // 2
    steps = pl.num_programs(1) // groups
    for group in range(groups):
        keep, send = refs[2 * group : 2 * group + 2]

        @pl.when(pl.program_id(1) // steps == group)
        def _():
            send[0] = nn_dot(turned[half:, :], right[...]).astype(jnp.bfloat16)
            keep[0] = nn_dot(turned[:half, :], right[...]).astype(jnp.bfloat16)


def params(semantics=1):
    return pltpu.CompilerParams(
        dimension_semantics=("arbitrary",) * semantics, vmem_limit_bytes=VMEM_BYTES
    )


ANY = pl.BlockSpec(memory_space=pl.ANY)
F32, BF16 = (jnp.float32, jnp.bfloat16)


def cost(flops, nbytes):
    return pl.CostEstimate(flops=int(flops), bytes_accessed=int(nbytes), transcendentals=0)


def hold(value, *after):
    def body(*refs):
        pass

    return pl.pallas_call(
        body,
        in_specs=[ANY] * (1 + len(after)),
        out_specs=ANY,
        out_shape=jax.ShapeDtypeStruct(value.shape, value.dtype),
        input_output_aliases={0: 0},
        cost_estimate=cost(0, 0),
    )(value, *after)


def token_rows(width, dtype):
    return ("token", (width,), dtype)


def latent_rows(dims, dtype):
    return ("latent", dims, dtype)


def one_sum(width):
    return ("sum", (1, width), F32)


def call_part(kernel, part, parts, latents, ins, anys, outs, scratch, estimate, after, before):
    count = latents // parts
    first = part * count

    def spec(kind, dims):
        if kind == "token":
            return pl.BlockSpec((TOK_LAT, dims[-1]), lambda i: (i + first, 0))
        if kind == "latent":
            return pl.BlockSpec((1,) + dims, lambda i: (i + first,) + (0,) * len(dims))
        return pl.BlockSpec(dims, lambda i: (0,) * len(dims))

    def dims_of(kind, array):
        return array.shape[1:] if kind == "latent" else array.shape

    out_shape = []
    for kind, dims, dtype in outs:
        lead = {"token": (latents * TOK_LAT,), "latent": (latents,), "sum": ()}[kind]
        out_shape.append(jax.ShapeDtypeStruct(lead + dims, dtype))
    filled = [i for i, (kind, _, _) in enumerate(outs) if kind != "sum"] if before else []
    head = len(ins) + len(anys)
    unused = len(filled) + len(after)

    def body(*refs):
        kernel(*refs[:head], *refs[head + unused :])

    return pl.pallas_call(
        body,
        grid=(count,),
        in_specs=[spec(kind, dims_of(kind, array)) for kind, array in ins] + [ANY] * (len(anys) + unused),
        out_specs=[spec(kind, dims) for kind, dims, _ in outs],
        out_shape=out_shape,
        scratch_shapes=scratch,
        input_output_aliases={head + j: i for j, i in enumerate(filled)},
        compiler_params=params(),
        cost_estimate=cost(estimate[0] / parts, estimate[1] / parts),
    )(*[array for _, array in ins], *anys, *[before[i] for i in filled], *after)


def call_parts(kernel, latents, ins, anys, outs, scratch, estimate, afters):
    parts = 2 if afters and latents % 2 == 0 else 1
    afters = afters or [list, list]
    result, sums = (None, None)
    for part in range(parts):
        after = afters[part]() if parts > 1 else afters[0]() + afters[1]()
        result = call_part(
            kernel, part, parts, latents, ins, anys, outs, scratch, estimate, after, result
        )
        own = [value for value, (kind, _, _) in zip(result, outs) if kind == "sum"]
        sums = own if sums is None else [a + b for a, b in zip(sums, own)]
    sums = iter(sums)
    return [next(sums) if kind == "sum" else value for value, (kind, _, _) in zip(result, outs)]


def run_attn_forward(stream, mods, out_bias, pieces, columns, afters):
    total, depth = stream.shape
    latents = total // TOK_LAT
    tp = lax.axis_size(TP)
    third = columns // 3
    width = columns + third
    return call_parts(
        functools.partial(attn_forward_kernel, pieces[1], columns),
        latents,
        [("token", stream), ("latent", mods), ("whole", out_bias)],
        [pieces[0]],
        [
            token_rows(depth, BF16),
            token_rows(tp * columns, BF16),
            latent_rows((tp * third // HEAD, TOK_LAT), F32),
            token_rows(tp * third, BF16),
            token_rows(depth, BF16),
            token_rows(depth, F32),
            token_rows(depth, BF16),
        ],
        [pltpu.VMEM((tp, depth, width), BF16), pltpu.SemaphoreType.DMA],
        (2 * total * depth * width * tp * 2.5, total * depth * 24),
        afters,
    )


def mlp_scratch(pieces_e, pieces_r, depth):
    tp = lax.axis_size(TP)
    columns = pieces_e[2]
    return [
        pltpu.VMEM((tp, depth, columns), BF16),
        pltpu.VMEM((tp, depth, columns), BF16),
        pltpu.SemaphoreType.DMA((2,)),
    ]


def run_mlp_forward(seq_m, mid, mods, expand_bias, reduce_bias, pieces_e, pieces_r, afters):
    total, depth = mid.shape
    hidden = expand_bias.shape[1]
    chunk = min(hidden // lax.axis_size(TP), 512)
    return call_parts(
        functools.partial(mlp_forward_kernel, (pieces_e[1], pieces_r[1]), chunk),
        total // TOK_LAT,
        [("token", seq_m), ("token", mid), ("latent", mods), ("whole", expand_bias), ("whole", reduce_bias)],
        [pieces_e[0], pieces_r[0]],
        [
            token_rows(hidden, F32),
            token_rows(hidden, BF16),
            token_rows(depth, BF16),
            token_rows(depth, F32),
        ],
        mlp_scratch(pieces_e, pieces_r, depth),
        (6 * total * depth * hidden, total * hidden * 6),
        afters,
    )


def run_mlp_backward(
    grad_out, branch_m, pre, mid, branch_a, mods, reduce_bias, out_bias, pieces_e, pieces_r, afters
):
    total, depth = mid.shape
    hidden = pre.shape[1]
    chunk = min(hidden // lax.axis_size(TP), 512)
    return call_parts(
        functools.partial(mlp_backward_kernel, (pieces_e[1], pieces_r[1]), chunk),
        total // TOK_LAT,
        [
            ("token", grad_out),
            ("token", branch_m),
            ("token", pre),
            ("token", mid),
            ("token", branch_a),
            ("latent", mods),
            ("whole", reduce_bias),
            ("whole", out_bias),
        ],
        [pieces_e[0], pieces_r[0]],
        [
            token_rows(depth, BF16),
            token_rows(hidden, BF16),
            token_rows(depth, F32),
            token_rows(depth, BF16),
            latent_rows((6, depth), F32),
            one_sum(depth),
            one_sum(hidden),
            one_sum(depth),
        ],
        mlp_scratch(pieces_e, pieces_r, depth),
        (6 * total * depth * hidden, total * hidden * 6),
        afters,
    )


def run_attn_backward(seq_grad, qkv, lse, stream, grad_mid, mods, pieces, columns, afters):
    total, depth = stream.shape
    tp = lax.axis_size(TP)
    third = columns // 3
    width = columns + third
    return call_parts(
        functools.partial(attn_backward_kernel, pieces[1], columns),
        total // TOK_LAT,
        [
            ("token", seq_grad),
            ("token", qkv),
            ("latent", lse),
            ("token", stream),
            ("token", grad_mid),
            ("latent", mods),
        ],
        [pieces[0]],
        [token_rows(tp * columns, BF16), token_rows(depth, F32), latent_rows((2, depth), F32)],
        [
            pltpu.VMEM((TOK_LAT, tp * third), BF16),
            pltpu.VMEM((tp, depth, width), BF16),
            pltpu.SemaphoreType.DMA,
        ],
        (2 * total * depth * width * tp * 3, total * depth * 24),
        afters,
    )


def run_final(stream, mods, noise, patch_out, scale_pred):
    total, depth = stream.shape
    return call_part(
        functools.partial(final_kernel, scale_pred),
        0,
        1,
        total // TOK_LAT,
        [("token", stream), ("latent", mods), ("latent", noise), ("whole", patch_out)],
        [],
        [
            token_rows(depth, F32),
            latent_rows((2, depth), F32),
            ("sum", (CH, depth), F32),
            one_sum(CH),
        ],
        [],
        (6 * total * depth * LANES, total * depth * 8),
        [],
        None,
    )


def start_sums(left, right, columns, firsts, after):
    total, depth = left.shape
    tp, count = (lax.axis_size(TP), lax.axis_size(FSDP))
    groups = len(firsts)
    width = columns // groups
    chunk = next(size for size in (768, 512, 384, 256, 128) if width % size == 0)
    steps = columns // chunk
    each = width // chunk
    place = jnp.stack([lax.axis_index(FSDP), lax.axis_index(TP)]).astype(jnp.int32)

    def out(group):
        return pl.BlockSpec(
            (1, depth // 2, chunk),
            lambda p, j, place: (p, 0, jnp.clip(j - group * each, 0, each - 1)),
        )

    def body(place, left, right, *rest):
        weight_grad_kernel(count, groups, place, left, right, *rest[len(after) :])

    results = pl.pallas_call(
        body,
        grid_spec=pltpu.PrefetchScalarGridSpec(
            num_scalar_prefetch=1,
            grid=(tp, steps),
            in_specs=[
                pl.BlockSpec((total, depth), lambda p, j, place: (0, 0)),
                pl.BlockSpec((total, chunk), lambda p, j, place: (0, (p ^ place[1]) * steps + j)),
            ]
            + [ANY] * len(after),
            out_specs=[out(i // 2) for i in range(2 * groups)],
            scratch_shapes=[pltpu.VMEM((depth, total), BF16)],
        ),
        out_shape=[jax.ShapeDtypeStruct((tp, depth // 2, width), BF16)] * (2 * groups),
        compiler_params=params(2),
        cost_estimate=cost(2.5 * total * depth * columns * tp, total * (depth + columns * tp) * 2),
    )(place, left, right, *after)
    return [GradientSum(*results[2 * i : 2 * i + 2], first) for i, first in enumerate(firsts)]


def heads_apart(matrix):
    rows, columns = matrix.shape
    return matrix.reshape(rows, columns // (3 * HEAD), 3, HEAD).swapaxes(1, 2).reshape(rows, columns)


def heads_together(matrix):
    rows, columns = matrix.shape
    return matrix.reshape(rows, 3, columns // (3 * HEAD), HEAD).swapaxes(1, 2).reshape(rows, columns)


def adam(weight, first, second, grad, factor):
    grad = grad * factor
    new_first = BETA_ONE * first + (1.0 - BETA_ONE) * grad
    new_second = BETA_TWO * second + (1.0 - BETA_TWO) * grad * grad
    first_hat = new_first / (1.0 - BETA_ONE**STEP)
    second_hat = new_second / (1.0 - BETA_TWO**STEP)
    new_weight = weight - RATE * (first_hat / (jnp.sqrt(second_hat) + ADAM_EPS) + DECAY * weight)
    return (new_first, new_second, new_weight)


def per_device(
    clean_patches,
    noise_patches,
    timesteps,
    labels,
    qkv_weight,
    out_weight,
    expand_weight,
    reduce_weight,
    modulate_weight,
    embed_weight,
    bias_vector,
    qkv_first,
    out_first,
    expand_first,
    reduce_first,
    modulate_first,
    embed_first,
    bias_first,
    qkv_second,
    out_second,
    expand_second,
    reduce_second,
    modulate_second,
    embed_second,
    bias_second,
):
    tp_count, fsdp_count = (lax.axis_size(TP), lax.axis_size(FSDP))
    tp_rank, fsdp_rank = (lax.axis_index(TP), lax.axis_index(FSDP))
    everywhere = (FSDP, TP)
    rank = lax.axis_index(everywhere)
    own, length, _ = clean_patches.shape
    latents = own * fsdp_count * tp_count
    depth, columns = (embed_weight.shape[0] - FREQ - 2 * CH - CLASSES, embed_weight.shape[1])
    cols_qkv = qkv_weight.shape[2]

    step_in_own, step_out_own, patch_in_own, table_own, patch_out_own = split_embed(
        embed_weight.astype(BF16)
    )
    group = timesteps.shape[0]
    vector = jnp.concatenate(
        [
            timesteps.astype(F32),
            labels.astype(F32),
            bias_vector,
            patch_in_own.astype(F32).reshape(-1),
            patch_out_own.astype(F32).reshape(-1),
        ]
    )
    def shard(name, layer):
        if name == "attn":
            parts = [heads_apart(qkv_weight[layer].astype(BF16)), out_weight[layer].T.astype(BF16)]
            return jnp.concatenate(parts, axis=1)
        if name == "expand":
            return expand_weight[layer].astype(BF16)
        return reduce_weight[layer].T.astype(BF16)

    low_modulate = modulate_weight.astype(BF16)
    cond_columns = jnp.concatenate([step_out_own, table_own], axis=0).reshape(-1, LANES)
    cond_rows = cond_columns.shape[0]
    cond_columns = jnp.pad(cond_columns, ((0, -cond_rows % 16), (0, 0)))
    packed, step_in, near_columns, near_modulate, matrix = run_head(
        padded(vector), step_in_own.reshape(-1, LANES), cond_columns, low_modulate, shard("attn", 0), 0
    )
    near_modulate = near_modulate.reshape(-1, modulate_weight.shape[1])
    near_columns = near_columns[:, :cond_rows].reshape(-1, depth + CLASSES, columns)
    near_columns = near_columns.swapaxes(0, 1).reshape(depth + CLASSES, -1)
    packed = packed.reshape(packed.shape[0], -1)[:, : vector.shape[0]]
    step_in = step_in.reshape(-1, FREQ, columns)
    first_of_tp = packed.reshape(fsdp_count, tp_count, -1)[:, 0]
    steps_all = first_of_tp[:, :group].reshape(-1).astype(jnp.int32)
    labels_all = first_of_tp[:, group : 2 * group].reshape(-1).astype(jnp.int32)
    at = 2 * group + bias_vector.shape[0]
    bias = packed[:, 2 * group : at].reshape(-1)

    def rows_of(block):
        return block.reshape(-1, CH, columns).swapaxes(0, 1).reshape(CH, -1).astype(BF16)

    patch_in_low = rows_of(packed[:, at : at + CH * columns])
    patch_out_low = rows_of(packed[:, at + CH * columns :])
    step_in_low = step_in.swapaxes(0, 1).reshape(FREQ, -1)
    ada_bias, layer_bias, step_in_bias, step_out_bias, patch_bias = split_bias(bias)

    def gather(shards):
        packed = jnp.concatenate(shards, axis=1)
        whole = lax.all_gather(packed, (TP, FSDP), axis=0, tiled=True)
        return whole.reshape(tp_count, -1, packed.shape[1])

    hidden = expand_weight.shape[2]
    width = hidden + cols_qkv + out_weight.shape[1]
    first_half = gather([shard("expand", 0), shard("reduce", 0)])
    rest = jnp.concatenate([shard(name, 1) for name in ("attn", "expand", "reduce")], axis=1)
    second_half = gather([hold(rest, matrix)])
    attn_width = width - hidden
    pieces = {
        ("attn", 0): (matrix, 0, attn_width),
        ("expand", 0): (first_half, 0, hidden),
        ("reduce", 0): (first_half, hidden, hidden),
        ("attn", 1): (second_half, 0, attn_width),
        ("expand", 1): (second_half, attn_width, hidden),
        ("reduce", 1): (second_half, width, hidden),
    }

    features = step_features(steps_all).astype(BF16)
    step_pre = contract(features, step_in_low, "gf,fd->gd") + step_in_bias
    step_hidden = jax.nn.silu(step_pre).astype(BF16)
    onehot = (labels_all[:, None] == jnp.arange(CLASSES, dtype=jnp.int32)[None, :]).astype(F32)
    wide = tp_count * columns
    near_bias = jnp.take(
        step_out_bias.reshape(-1, 4 * wide), fsdp_rank // 4, axis=0
    )
    cond_near = (
        contract(step_hidden, near_columns[:depth], "gd,de->ge")
        + near_bias
        + contract(onehot.astype(BF16), near_columns[depth:], "gc,cd->gd")
    )
    place = (fsdp_rank % 4) * wide
    act_near = jax.nn.silu(cond_near).astype(BF16)
    act_own = lax.dynamic_slice_in_dim(act_near, place, wide, axis=1)
    far = far_flips()
    far_order = jnp.array([flip[0] for flip in far]) ^ fsdp_rank
    act_far = jnp.take(act_near.reshape(fsdp_count, group, -1), far_order, axis=0)
    mod_part = contract(
        act_far.reshape(len(far) * group, -1), near_modulate, "gd,de->ge"
    ).reshape(len(far), group, -1)
    mod_sum = mod_part[0]
    for k, flip in list(enumerate(far))[1:]:
        mod_sum = mod_sum + swap(mod_part[k].astype(BF16), flip).astype(F32)
    mods = exchange_tp(mod_sum.reshape(tp_count, own, -1)).swapaxes(0, 1).reshape(own, -1) + ada_bias
    mods = mods.reshape(own, 6 * LAYERS + 2, -1)
    steps_own = lax.dynamic_slice_in_dim(timesteps, tp_rank * own, own)
    signal, spread_level = noise_levels(steps_own)
    noisy = (
        signal[:, None, None] * clean_patches + spread_level[:, None, None] * noise_patches
    ).astype(BF16)
    stream = contract(noisy, patch_in_low, "gtc,cd->gtd") + patch_bias + place_table()[None]
    stream = stream.reshape(-1, depth)
    kept = [None] * LAYERS

    for layer in range(LAYERS):
        modulation = mods[:, 6 * layer : 6 * layer + 6]
        out_bias, expand_bias, reduce_bias = [value[None] for value in layer_bias[layer]]
        seq_a, qkv, lse, att, branch_a, mid, seq_m = run_attn_forward(
            stream, modulation, out_bias, pieces["attn", layer], cols_qkv, None
        )
        pre, acted, branch_m, after = run_mlp_forward(
            seq_m,
            mid,
            modulation,
            expand_bias,
            reduce_bias,
            pieces["expand", layer],
            pieces["reduce", layer],
            None,
        )
        kept[layer] = (stream, seq_a, qkv, lse, att, branch_a, mid, seq_m, pre, acted, branch_m)
        stream = after
    cond_matrix = jnp.concatenate([step_out_own, table_own], axis=0).T
    cond_matrix = lax.all_gather(hold(cond_matrix, seq_m), everywhere, axis=0, tiled=True)
    total = float(latents * length * CH)
    grad_stream, grad_final_mod, grad_patch_out, loss_rows = run_final(
        stream, mods[:, 6 * LAYERS :], noise_patches, patch_out_low, 2.0 / total
    )
    loss_local = jnp.sum(loss_rows)

    sums, reduced = ({}, {})

    def step(*wanted):
        return lambda: [sent for key in wanted for sent in sums[key].step()]

    def mlp_backward(layer, grad, afters):
        stream, seq_a, qkv, lse, att, branch_a, mid, seq_m, pre, acted, branch_m = kept[layer]
        out_bias, expand_bias, reduce_bias = [value[None] for value in layer_bias[layer]]
        return run_mlp_backward(
            grad,
            branch_m,
            pre,
            mid,
            branch_a,
            mods[:, 6 * layer : 6 * layer + 6],
            reduce_bias,
            out_bias,
            pieces["expand", layer],
            pieces["reduce", layer],
            afters,
        )

    mod_grads = [None] * LAYERS
    layer_bias_grads = [None] * LAYERS
    cols_out = out_weight.shape[1]
    halves = 2 if cols_qkv // 2 % LANES == 0 else 1
    qkv_keys = [[("qkv", layer, i) for i in range(halves)] for layer in range(LAYERS)]
    rest_keys = [[("reduce", layer, 0), ("expand", layer, 0), ("out", layer, 0)] for layer in range(LAYERS)]
    mlp_afters = [(step(*rest_keys[1]), step(*qkv_keys[1])), (step(), step())]
    grad_afters = [[step(), step(*qkv_keys[1]), step(*qkv_keys[1])], [step()] * 3]

    attn_afters = [
        (step(*rest_keys[0][:2]), step(*rest_keys[0])),
        (step(*rest_keys[1][:2]), step(*rest_keys[1][2:])),
    ]

    def start(name, layer, left, right, width, firsts, after):
        started = start_sums(left, right, width, firsts, list(after))
        for i, total_sum in enumerate(started):
            sums[name, layer, i] = total_sum

    for layer in reversed(range(LAYERS)):
        stream, seq_a, qkv, lse, att, branch_a, mid, seq_m, pre, acted, branch_m = kept[layer]
        seq_grad_m, grad_pre, grad_mid, seq_grad_a, mod_late, d_out, d_expand, d_reduce = mlp_backward(
            layer, grad_stream, mlp_afters[layer]
        )
        after = grad_afters[layer]
        if layer == 0:
            mod_known = [jnp.zeros_like(mod_late[:, :2]), mod_late[:, 2:]] + mod_grads[1:]
            mod_known = jnp.concatenate(mod_known + [grad_final_mod], axis=1).reshape(own, -1)
            mod_known = mod_known.astype(BF16)
            known_columns = mod_known.reshape(own, tp_count, -1).swapaxes(0, 1)
            known_columns = exchange_tp(known_columns).reshape(group, -1)
            known_columns = lax.all_gather(known_columns, FSDP, axis=0, tiled=True)
        start("reduce", layer, seq_grad_m, acted, hidden, [FSDP], after[0]())
        start("expand", layer, seq_m, grad_pre, hidden, [TP], after[1]())
        start("out", layer, seq_grad_a, att, cols_out, [FSDP], after[2]())
        grad_qkv, grad_stream, mod_early = run_attn_backward(
            seq_grad_a,
            qkv,
            lse,
            stream,
            grad_mid,
            mods[:, 6 * layer : 6 * layer + 6],
            pieces["attn", layer],
            cols_qkv,
            attn_afters[layer],
        )
        after = step(*rest_keys[layer])()
        start("qkv", layer, seq_a, grad_qkv, cols_qkv, [TP, FSDP][:halves], after)
        mod_grads[layer] = jnp.concatenate([mod_early, mod_late[:, 2:]], axis=1)
        layer_bias_grads[layer] = (d_out[0], d_expand[0], d_reduce[0])
    last_sent = sums["qkv", 0, 0].sent
    mod_columns = modulate_weight.shape[1]
    mod_early = hold(mod_early, last_sent)
    mod_last = mod_early.reshape(own, -1).astype(BF16)
    last_columns = push([mod_last.reshape(-1, LANES)], [-(-mod_last.shape[1] // mod_columns) + 1], 3)[0]
    last_columns = last_columns.reshape(latents, -1)
    for total_sum in sums.values():
        while total_sum.far is None:
            last_sent = total_sum.step()[0]
    for (name, layer, i), total_sum in sums.items():
        reduced.setdefault((name, layer), []).append(total_sum.finish())
    reduced = {key: jnp.concatenate(parts, axis=1) for key, parts in reduced.items()}
    for layer in range(LAYERS):
        reduced["qkv", layer] = heads_together(reduced["qkv", layer])
    grad_stream = hold(grad_stream, sums["qkv", 0, 0].far[0])
    grad_embedded = grad_stream.astype(BF16)
    grad_patch_in = contract(noisy.reshape(-1, CH), grad_embedded, "tc,td->cd")
    grad_patch_bias = jnp.sum(grad_embedded.astype(F32), axis=0)

    last_columns = jnp.pad(last_columns, ((0, 0), (0, modulate_weight.shape[1] * tp_count - last_columns.shape[1])))
    grad_columns = known_columns + lax.dynamic_slice_in_dim(
        last_columns, tp_rank * modulate_weight.shape[1], modulate_weight.shape[1], axis=1
    )
    grad_ada = contract(act_own, grad_columns, "gd,ge->de")
    act_part = contract(grad_columns, low_modulate, "ge,de->gd").reshape(-1, own, low_modulate.shape[0])
    act_part = jnp.pad(act_part, ((0, 0), (0, -own % 8), (0, -act_part.shape[2] % LANES)))
    act_part = push([act_part], [1], 4)[0][:, :own, : low_modulate.shape[0]]
    act_part = jnp.sum(act_part.reshape(fsdp_count, tp_count, own, -1), axis=1).swapaxes(0, 1).reshape(own, -1)

    def of_own(value):
        return lax.dynamic_slice_in_dim(value, rank * own, own)

    cond_mine = (
        contract(of_own(step_hidden), cond_matrix[:, :depth], "gd,ed->ge")
        + step_out_bias
        + contract(of_own(onehot).astype(BF16), cond_matrix[:, depth:], "gc,dc->gd")
    )
    grad_cond = local_back(jax.nn.silu, cond_mine, act_part)
    grad_hidden = exact_dot(grad_cond, cond_matrix[:, :depth].astype(F32))
    grad_step_pre = local_back(jax.nn.silu, of_own(step_pre), grad_hidden)
    both_grads = jnp.concatenate([grad_cond, grad_step_pre], axis=0).reshape(2 * own, -1, columns)
    both_grads = jnp.pad(
        both_grads.swapaxes(0, 1), ((0, 0), (0, -2 * own % 8), (0, -columns % LANES))
    )

    pieces_bias = [
        jnp.sum(mod_known.astype(F32), axis=0)
        + jnp.pad(jnp.sum(mod_last.astype(F32), axis=0), (0, mod_known.shape[1] - mod_last.shape[1]))
    ]
    for layer in range(LAYERS):
        pieces_bias += layer_bias_grads[layer]
    pieces_bias += [jnp.zeros((2 * depth,), F32), grad_patch_bias]
    chunk = bias_vector.shape[0]
    small = jnp.concatenate(
        [
            jnp.concatenate(pieces_bias).reshape(-1, chunk),
            jnp.concatenate([grad_patch_in, grad_patch_out])
            .reshape(2 * CH, -1, columns)
            .swapaxes(0, 1)
            .reshape(-1, 2 * CH * columns),
        ],
        axis=1,
    )
    width = small.shape[1]
    small = jnp.pad(small, ((0, 0), (0, -width % (8 * LANES)))).reshape(small.shape[0], -1, LANES)
    small, both_grads = push([hold(small, sums["qkv", 0, 0].far[0]), both_grads], [1, 1], 1)
    small = jnp.sum(small, axis=0).reshape(-1)[:width]
    grad_cond = both_grads[:, :own, :columns].reshape(latents, columns)
    grad_step_pre = both_grads[:, own : 2 * own, :columns].reshape(latents, columns)
    grad_table = exact_dot(onehot.T, grad_cond)
    grad_step_out = exact_dot(step_hidden.astype(F32).T, grad_cond)
    grad_step_in = exact_dot(features.astype(F32).T, grad_step_pre)
    step_bias_grads = jnp.concatenate([jnp.sum(grad_step_pre, axis=0), jnp.sum(grad_cond, axis=0)])
    bias_grad = small[:chunk]
    patch_grads = small[chunk:].reshape(2 * CH, columns)
    embed_grad = jnp.concatenate(
        [grad_step_in, grad_step_out, patch_grads[:CH], grad_table, patch_grads[CH:]], axis=0
    )
    grads = (
        jnp.stack([reduced["qkv", i] for i in range(LAYERS)]),
        jnp.stack([reduced["out", i].T for i in range(LAYERS)]),
        jnp.stack([reduced["expand", i] for i in range(LAYERS)]),
        jnp.stack([reduced["reduce", i].T for i in range(LAYERS)]),
        grad_ada,
        embed_grad,
        bias_grad,
    )
    square = jnp.zeros((), jnp.float32)
    for grad in grads:
        square = square + jnp.sum(grad * grad)
    square = square + jnp.sum(step_bias_grads * step_bias_grads)
    last = push([padded(jnp.concatenate([square[None], loss_local[None], step_bias_grads]))], [0], 2)[0]
    last = last.reshape(last.shape[0], -1)
    square, loss_total = jnp.sum(last[:, 0]), jnp.sum(last[:, 1])
    step_biases = [last[:, 2 : 2 + columns].reshape(-1), last[:, 2 + columns : 2 + 2 * columns].reshape(-1)]
    before = jnp.zeros((bias.shape[0] - 3 * depth,), F32)
    step_biases = jnp.concatenate([before] + step_biases + [jnp.zeros((depth,), F32)])
    bias_grad = bias_grad + lax.dynamic_slice_in_dim(step_biases, rank * chunk, chunk)
    grads = grads[:-1] + (bias_grad,)
    grad_norm = jnp.sqrt(square)
    factor = CLIP_AT / jnp.maximum(grad_norm, CLIP_AT)
    params = (
        qkv_weight,
        out_weight,
        expand_weight,
        reduce_weight,
        modulate_weight,
        embed_weight,
        bias_vector,
    )
    firsts = (
        qkv_first,
        out_first,
        expand_first,
        reduce_first,
        modulate_first,
        embed_first,
        bias_first,
    )
    seconds = (
        qkv_second,
        out_second,
        expand_second,
        reduce_second,
        modulate_second,
        embed_second,
        bias_second,
    )
    news = [adam(w, f, s, g, factor) for w, f, s, g in zip(params, firsts, seconds, grads)]
    qkv_moment, qkv_square, qkv_master = news[0]
    out_moment, out_square, out_master = news[1]
    expand_moment, expand_square, expand_master = news[2]
    reduce_moment, reduce_square, reduce_master = news[3]
    modulate_moment, modulate_square, modulate_master = news[4]
    embed_moment, embed_square, embed_master = news[5]
    bias_moment, bias_square, bias_master = news[6]
    return (
        loss_total,
        grad_norm,
        qkv_moment,
        qkv_square,
        qkv_master,
        out_moment,
        out_square,
        out_master,
        expand_moment,
        expand_square,
        expand_master,
        reduce_moment,
        reduce_square,
        reduce_master,
        modulate_moment,
        modulate_square,
        modulate_master,
        embed_moment,
        embed_square,
        embed_master,
        bias_moment,
        bias_square,
        bias_master,
        qkv_master.astype(jnp.bfloat16),
        out_master.astype(jnp.bfloat16),
        expand_master.astype(jnp.bfloat16),
        reduce_master.astype(jnp.bfloat16),
        modulate_master.astype(jnp.bfloat16),
        embed_master.astype(jnp.bfloat16),
    )


def solution(mesh):
    return jax.shard_map(
        per_device,
        mesh=mesh,
        in_specs=(
            P((FSDP, TP), None, None),
            P((FSDP, TP), None, None),
            P(FSDP),
            P(FSDP),
            P(None, FSDP, TP),
            P(None, TP, FSDP),
            P(None, FSDP, TP),
            P(None, TP, FSDP),
            P(FSDP, TP),
            P(None, (FSDP, TP)),
            P((FSDP, TP)),
            P(None, FSDP, TP),
            P(None, TP, FSDP),
            P(None, FSDP, TP),
            P(None, TP, FSDP),
            P(FSDP, TP),
            P(None, (FSDP, TP)),
            P((FSDP, TP)),
            P(None, FSDP, TP),
            P(None, TP, FSDP),
            P(None, FSDP, TP),
            P(None, TP, FSDP),
            P(FSDP, TP),
            P(None, (FSDP, TP)),
            P((FSDP, TP)),
        ),
        out_specs=(
            P(),
            P(),
            P(None, FSDP, TP),
            P(None, FSDP, TP),
            P(None, FSDP, TP),
            P(None, TP, FSDP),
            P(None, TP, FSDP),
            P(None, TP, FSDP),
            P(None, FSDP, TP),
            P(None, FSDP, TP),
            P(None, FSDP, TP),
            P(None, TP, FSDP),
            P(None, TP, FSDP),
            P(None, TP, FSDP),
            P(FSDP, TP),
            P(FSDP, TP),
            P(FSDP, TP),
            P(None, (FSDP, TP)),
            P(None, (FSDP, TP)),
            P(None, (FSDP, TP)),
            P((FSDP, TP)),
            P((FSDP, TP)),
            P((FSDP, TP)),
            P(None, FSDP, TP),
            P(None, TP, FSDP),
            P(None, FSDP, TP),
            P(None, TP, FSDP),
            P(FSDP, TP),
            P(None, (FSDP, TP)),
        ),
        check_vma=False,
    )
```

```python
import functools
import math

import jax
import jax.numpy as jnp
from jax import lax
from jax.experimental import pallas as pl
from jax.experimental.pallas import tpu as pltpu
from jax.sharding import PartitionSpec as P

D = 1024
HEAD = 64
FF = 4096
CH = 16
FREQ = 256
CLASSES = 32
SIDE = 16
LAYERS = 2
STEP = 10
TOK_LAT = 256
MODS = 14336


CLIP_AT = 0.01
RATE = 0.05
BETA_ONE = 0.5
BETA_TWO = 0.5
DECAY = 0.01
ADAM_EPS = 1e-08
NORM_EPS = 1e-06
EXACT = lax.Precision.HIGHEST


def contract(left, right, form):
    return jnp.einsum(form, left, right, preferred_element_type=jnp.float32)


def exact_dot(left, right):
    return jnp.dot(left, right, precision=EXACT)


def layer_norm(value):
    center = value - jnp.mean(value, -1, keepdims=True)
    return center * lax.rsqrt(jnp.mean(center * center, -1, keepdims=True) + NORM_EPS)


def gelu_tanh(value):
    return jax.nn.gelu(value, approximate=True)


def local_back(func, value, grad):
    _, pullback = jax.vjp(func, value)
    return pullback(grad)[0]


def noise_levels(steps):
    angle = (steps.astype(jnp.float32) / 1000.0 + 0.008) / 1.008 * (math.pi / 2)
    return (jnp.cos(angle), jnp.sin(angle))


def step_features(steps):
    half = FREQ // 2
    rates = jnp.exp(-math.log(10000.0) * jnp.arange(half, dtype=jnp.float32) / half)
    phase = steps.astype(jnp.float32)[:, None] * rates[None, :]
    return jnp.concatenate([jnp.cos(phase), jnp.sin(phase)], axis=1)


def place_table():
    quarter = D // 4
    rates = 1.0 / 10000.0 ** (jnp.arange(quarter, dtype=jnp.float32) / quarter)
    index = jnp.arange(TOK_LAT, dtype=jnp.int32)
    rows = (index // SIDE).astype(jnp.float32)[:, None] * rates[None, :]
    columns = (index % SIDE).astype(jnp.float32)[:, None] * rates[None, :]
    return jnp.concatenate(
        [jnp.sin(rows), jnp.cos(rows), jnp.sin(columns), jnp.cos(columns)], axis=1
    )


def split_embed(embed):
    start = FREQ + D
    return (
        embed[:FREQ],
        embed[FREQ:start],
        embed[start : start + CH],
        embed[start + CH : start + CH + CLASSES],
        embed[start + CH + CLASSES :],
    )


def split_bias(bias):
    layers = []
    for layer in range(LAYERS):
        base = MODS + layer * (2 * D + FF)
        layers.append(
            (
                bias[base : base + D],
                bias[base + D : base + D + FF],
                bias[base + D + FF : base + 2 * D + FF],
            )
        )
    tail = MODS + LAYERS * (2 * D + FF)
    return (
        bias[:MODS],
        layers,
        bias[tail : tail + D],
        bias[tail + D : tail + 2 * D],
        bias[tail + 2 * D : tail + 3 * D],
    )


LANES = 128
FSDP, TP = ("fsdp", "tp")
GELU_A = math.sqrt(2.0 / math.pi)
GELU_B = 0.044715
VMEM_BYTES = 60 * 1024 * 1024


def swap(value, flip):
    name, bits = (FSDP, flip[0]) if flip[0] else (TP, flip[1])
    return lax.ppermute(value, name, [(i, i ^ bits) for i in range(lax.axis_size(name))])


def bit_flips(name):
    bits = [1 << i for i in range(lax.axis_size(name).bit_length() - 1)]
    return [(bit, 0) if name == FSDP else (0, bit) for bit in bits]


def far_flips():
    return [(k << 2, 0) for k in range(max(lax.axis_size(FSDP) >> 2, 1))]


def middle_flips(first):
    fsdp, tp = (bit_flips(FSDP)[1:2], bit_flips(TP))
    return fsdp + tp if first == FSDP else tp + fsdp


CORE = (1, 0)


def both(one, other):
    return (one[0] ^ other[0], one[1] ^ other[1])


def gather_far(value):
    flips = far_flips()
    held = [value[None]] + [swap(value, flip)[None] for flip in flips[1:]]
    return jnp.concatenate(held, axis=0), flips


def double(held, flips, flip):
    return jnp.concatenate([held, swap(held, flip)], axis=0), flips + [both(f, flip) for f in flips]


def gather_relative(value, hops):
    held, flips = (value[None], [(0, 0)])
    for flip in hops:
        held, flips = double(held, flips, flip)
    return held, flips


def gather_small(value, axes):
    held, _ = gather_relative(value, [flip for name in reversed(axes) for flip in bit_flips(name)])
    return jnp.take(held, jnp.arange(held.shape[0]) ^ lax.axis_index(axes), axis=0)


def split_bit(value, axis, index):
    return lax.index_in_dim(value, index, axis, keepdims=False)


def scatter_sum(value, axes, axis):
    flips = [flip for name in reversed(axes) for flip in bit_flips(name)][::-1]
    count = 1 << len(flips)
    shape = value.shape
    value = value.reshape(shape[:axis] + (count, shape[axis] // count) + shape[axis + 1 :])
    value = jnp.take(value, jnp.arange(count) ^ lax.axis_index(axes), axis=axis)
    keep = jnp.moveaxis(value, axis, 0).reshape(
        (2,) * len(flips) + shape[:axis] + (shape[axis] // count,) + shape[axis + 1 :]
    )
    dims = list(flips)
    for flip in sorted(flips, key=lambda flip: flip != CORE):
        at = dims.index(flip)
        keep = split_bit(keep, at, 0) + swap(split_bit(keep, at, 1), flip)
        dims = dims[:at] + dims[at + 1 :]
    return keep


def exchange_tp(value):
    count, rank = (lax.axis_size(TP), lax.axis_index(TP))
    value = jnp.take(value, jnp.arange(count) ^ rank, axis=0)
    got = jnp.stack([value[0]] + [swap(value[k], (0, k)) for k in range(1, count)])
    return jnp.take(got, jnp.arange(count) ^ rank, axis=0)


def push_kernel(plans, arrays, *refs):
    ins, outs = (refs[:arrays], refs[arrays : 2 * arrays])
    send, recv = refs[2 * arrays :]
    fsdp, tp = (lax.axis_index(FSDP), lax.axis_index(TP))
    count = lax.axis_size(FSDP) * lax.axis_size(TP)
    me = fsdp * lax.axis_size(TP) + tp

    def partner(k):
        other = lax.rem(me + k, count)
        return (other // lax.axis_size(TP), lax.rem(other, lax.axis_size(TP)))

    barrier = pltpu.get_barrier_semaphore()

    def greet(k, carry):
        pl.semaphore_signal(barrier, inc=1, device_id=partner(k), device_id_type=pl.DeviceIdType.MESH)
        return carry

    lax.fori_loop(1, count, greet, 0)
    pl.semaphore_wait(barrier, count - 1)

    def copies(k):
        other = lax.rem(me + k, count)
        found = []
        for i, (plan, source, target) in enumerate(zip(plans, ins, outs)):
            view = source.at[other] if plan == 1 else source
            found.append(
                pltpu.make_async_remote_copy(
                    src_ref=view,
                    dst_ref=target.at[me],
                    send_sem=send.at[i, k],
                    recv_sem=recv.at[i, k],
                    device_id=partner(k),
                    device_id_type=pl.DeviceIdType.MESH,
                )
            )
        return found

    def start(k, carry):
        for plan, copy in zip(plans, copies(k)):
            if plan > 1:
                pl.when(partner(k)[1] < plan - 1)(copy.start)
            else:
                copy.start()
        return carry

    def finish(k, carry):
        for plan, copy in zip(plans, copies(k)):
            if plan > 1:
                pl.when(partner(k)[1] < plan - 1)(copy.wait_send)
                pl.when(tp < plan - 1)(copy.wait_recv)
            else:
                copy.wait()
        return carry

    lax.fori_loop(1, count, start, 0)
    for plan, source, target in zip(plans, ins, outs):
        target[pl.ds(me, 1)] = source[pl.ds(me, 1)] if plan == 1 else source[...][None]
    lax.fori_loop(1, count, finish, 0)


def push(arrays, plans, identity):
    count = lax.axis_size(FSDP) * lax.axis_size(TP)
    shapes = [array.shape[1:] if plan == 1 else array.shape for array, plan in zip(arrays, plans)]
    block = pl.BlockSpec(memory_space=pltpu.VMEM)
    return pl.pallas_call(
        functools.partial(push_kernel, plans, len(arrays)),
        in_specs=[block] * len(arrays),
        out_specs=[block] * len(arrays),
        out_shape=[
            jax.ShapeDtypeStruct((count,) + shape, array.dtype) for shape, array in zip(shapes, arrays)
        ],
        scratch_shapes=[pltpu.SemaphoreType.DMA((len(arrays), count))] * 2,
        compiler_params=pltpu.CompilerParams(
            collective_id=identity, has_side_effects=True, vmem_limit_bytes=VMEM_BYTES
        ),
        cost_estimate=pl.CostEstimate(flops=int(5e9), bytes_accessed=int(5e7), transcendentals=0),
    )(*arrays)


def flipped(index, bits):
    result, bit = (index, 1)
    while bit <= bits:
        if bits & bit:
            result = result + bit * (1 - 2 * lax.rem(index // bit, 2))
        bit *= 2
    return result


def head_kernel(packed, step_in, cond, modulate, shard, *refs):
    packed_all, step_in_all, cond_all, modulate_all, matrix = refs[:5]
    send, recv, small_send, small_recv, local = refs[5:]
    fsdp, tp = (lax.axis_index(FSDP), lax.axis_index(TP))
    tp_count = lax.axis_size(TP)
    count = lax.axis_size(FSDP) * tp_count
    me = fsdp * tp_count + tp
    slot = lax.rem(fsdp, 4)

    def device(k):
        other = lax.rem(me + k, count)
        return (other // tp_count, lax.rem(other, tp_count))

    barrier = pltpu.get_barrier_semaphore()

    def greet(k, carry):
        pl.semaphore_signal(barrier, inc=1, device_id=device(k), device_id_type=pl.DeviceIdType.MESH)
        return carry

    lax.fori_loop(1, count, greet, 0)
    pl.semaphore_wait(barrier, count - 1)

    made = []

    def remote(source, target, flip):
        copy = pltpu.make_async_remote_copy(
            src_ref=source,
            dst_ref=target,
            send_sem=send.at[len(made)],
            recv_sem=recv.at[len(made)],
            device_id=(flipped(fsdp, flip[0]), flipped(tp, flip[1])),
            device_id_type=pl.DeviceIdType.MESH,
        )
        made.append(copy)
        copy.start()
        return copy

    rows, columns = shard.shape

    def region(flip, cols):
        row = pl.multiple_of(flipped(fsdp, flip[0]) * rows, rows)
        return matrix.at[flipped(tp, flip[1]), pl.ds(row, rows), cols]

    every = slice(0, columns)
    far = far_flips()
    own_copies = [
        pltpu.make_async_copy(modulate, modulate_all.at[slot], local.at[0]),
        pltpu.make_async_copy(shard, region((0, 0), every), local.at[1]),
    ]
    for copy in own_copies:
        copy.start()
    near = [remote(modulate, modulate_all.at[slot], (2, 0))]
    under_way = [remote(shard, region((0, 0), every), flip) for flip in far[1:]]
    plane = [(f, t) for f in range(4) for t in range(tp_count)][1:]
    last = [remote(cond, cond_all.at[slot * tp_count + tp], flip) for flip in plane]

    def small(k):
        pairs = ((packed, packed_all), (step_in, step_in_all))
        return [
            pltpu.make_async_remote_copy(
                src_ref=source,
                dst_ref=target.at[me],
                send_sem=small_send.at[i, k],
                recv_sem=small_recv.at[i, k],
                device_id=device(k),
                device_id_type=pl.DeviceIdType.MESH,
            )
            for i, (source, target) in enumerate(pairs)
        ]

    def start_small(k, carry):
        for copy in small(k):
            copy.start()
        return carry

    def finish_small(k, carry):
        for copy in small(k):
            copy.wait()
        return carry

    lax.fori_loop(1, count, start_small, 0)
    packed_all[pl.ds(me, 1)] = packed[...][None]
    step_in_all[pl.ds(me, 1)] = step_in[...][None]
    cond_all[pl.ds(slot * tp_count + tp, 1)] = cond[...][None]
    for copy in own_copies:
        copy.wait()
    for copy in near:
        copy.wait()
    last.append(remote(modulate, modulate_all.at[slot], CORE))
    partner = flipped(slot, 2)
    last.append(remote(modulate_all.at[partner], modulate_all.at[partner], CORE))
    for copy in under_way:
        copy.wait()
    orders = (middle_flips(FSDP), middle_flips(TP))
    held = [list(far), list(far)]
    halves = (slice(0, columns // 2), slice(columns // 2, columns))
    for step in range(len(orders[0])):
        under_way = []
        for color, cols in enumerate(halves):
            flip = orders[color][step]
            under_way += [remote(region(f, cols), region(f, cols), flip) for f in held[color]]
            held[color] = held[color] + [both(f, flip) for f in held[color]]
        for copy in under_way:
            copy.wait()
    last += [remote(region(f, every), region(f, every), CORE) for f in held[0]]
    lax.fori_loop(1, count, finish_small, 0)
    for copy in last:
        copy.wait()


def run_head(packed, step_in, cond, modulate, shard, identity):
    tp, fsdp = (lax.axis_size(TP), lax.axis_size(FSDP))
    count = fsdp * tp
    rows, columns = shard.shape
    vmem = pl.BlockSpec(memory_space=pltpu.VMEM)
    total = fsdp // 4 + 4 * tp + 2 + 2 * (fsdp // 4) * (2 * tp - 1) + fsdp * tp
    shapes = [
        ((count,) + packed.shape, F32),
        ((count,) + step_in.shape, BF16),
        ((4 * tp,) + cond.shape, BF16),
        ((4,) + modulate.shape, BF16),
        ((tp, rows * fsdp, columns), BF16),
    ]
    return pl.pallas_call(
        head_kernel,
        in_specs=[vmem] * 3 + [ANY] * 2,
        out_specs=[vmem] * 3 + [ANY] * 2,
        out_shape=[jax.ShapeDtypeStruct(shape, dtype) for shape, dtype in shapes],
        scratch_shapes=[pltpu.SemaphoreType.DMA((total,))] * 2
        + [pltpu.SemaphoreType.DMA((2, count))] * 2
        + [pltpu.SemaphoreType.DMA((2,))],
        compiler_params=pltpu.CompilerParams(
            collective_id=identity, has_side_effects=True, vmem_limit_bytes=VMEM_BYTES
        ),
        cost_estimate=pl.CostEstimate(flops=int(4e10), bytes_accessed=int(1e8), transcendentals=0),
    )(packed, step_in, cond, modulate, shard)


def padded(vector):
    return jnp.pad(vector, (0, -vector.shape[0] % (8 * LANES))).reshape(-1, LANES)


class GradientSum:
    def __init__(self, keep, send, first):
        fsdp = bit_flips(FSDP)
        self.dims = bit_flips(TP)[::-1] + fsdp[2:][::-1] + fsdp[1:2]
        self.rows, self.columns = (keep.shape[1] * 2 // lax.axis_size(FSDP), keep.shape[2])
        self.flips = middle_flips(first)[::-1]
        self.keep = keep.reshape((2,) * len(self.dims) + (self.rows, self.columns))
        self.sent = send
        self.next = CORE
        self.far, self.total = (None, None)

    def step(self):
        got = swap(self.sent, self.next).reshape(self.keep.shape)

        def part(axis, index):
            return split_bit(self.keep, axis, index).astype(F32) + split_bit(got, axis, index).astype(F32)

        if self.flips:
            self.next = self.flips.pop(0)
            axis = self.dims.index(self.next)
            self.sent, self.keep = (part(axis, 1).astype(BF16), part(axis, 0).astype(BF16))
            self.dims = self.dims[:axis] + self.dims[axis + 1 :]
            return [self.sent]
        blocks = (-1, self.rows, self.columns)
        self.keep, got = (self.keep.reshape(blocks), got.reshape(blocks))
        self.far = [part(0, k).astype(BF16) for k in range(1, self.keep.shape[0])]
        self.keep = part(0, 0)
        return self.far

    def finish(self):
        if self.total is not None:
            return self.total
        while self.far is None:
            self.step()
        result = self.keep
        for flip, sent in zip(far_flips()[1:], self.far):
            result = result + swap(sent, flip).astype(F32)
        self.total = result
        return result


def nt_dot(left, right):
    return lax.dot_general(left, right, (((1,), (1,)), ((), ())), preferred_element_type=jnp.float32)


def nn_dot(left, right):
    return lax.dot_general(left, right, (((1,), (0,)), ((), ())), preferred_element_type=jnp.float32)


def tn_dot(left, right):
    return lax.dot_general(left, right, (((0,), (0,)), ((), ())), preferred_element_type=jnp.float32)


def norm_parts(value):
    center = value - jnp.mean(value, -1, keepdims=True)
    inverse = lax.rsqrt(jnp.mean(center * center, -1, keepdims=True) + NORM_EPS)
    return center * inverse, inverse


def norm_back(normed, inverse, grad):
    mean_grad = jnp.mean(grad, -1, keepdims=True)
    mean_both = jnp.mean(grad * normed, -1, keepdims=True)
    return inverse * (grad - mean_grad - normed * mean_both)


def row_sum(value):
    return jnp.sum(value, axis=0, keepdims=True)


def column_copy(start, ref, target, sem):
    return [pltpu.make_async_copy(ref.at[:, :, pl.ds(start, target.shape[2])], target, sem)]


def run_copies(*groups):
    for group in groups:
        for copy in group:
            copy.start()
    for group in groups:
        for copy in group:
            copy.wait()


def lane_masks(dtype):
    lane = lax.broadcasted_iota(jnp.int32, (1, LANES), 1)
    return [((lane // HEAD) == i).astype(jnp.float32).astype(dtype) for i in range(LANES // HEAD)]


def attn_forward_kernel(info, columns, stream, mods, bias, *rest):
    parts, (seq_a, qkv, lse, att, branch, mid, seq_m, weight, sems) = (rest[0], rest[1:])
    tp = weight.shape[0]
    third = columns // 3

    @pl.when(pl.program_id(0) == 0)
    def _():
        run_copies(column_copy(info, parts, weight, sems))

    value = stream[...]
    normed, _ = norm_parts(value)
    seq_a[...] = (normed * (1.0 + mods[0, 1:2, :]) + mods[0, 0:1, :]).astype(jnp.bfloat16)
    for p in range(tp):
        qkv[:, p * columns : (p + 1) * columns] = nn_dot(
            seq_a[...], weight[p, :, :columns]
        ).astype(jnp.bfloat16)
    masks = lane_masks(jnp.bfloat16)
    for p in range(tp):
        for pair in range(third // LANES):
            base = p * columns + pair * LANES
            query = qkv[:, base : base + LANES]
            key = qkv[:, base + third : base + third + LANES]
            val = qkv[:, base + 2 * third : base + 2 * third + LANES]
            out = None
            for i, mask in enumerate(masks):
                scores = nt_dot(key, query * mask) * (1.0 / math.sqrt(HEAD))
                top = jnp.max(scores, axis=0, keepdims=True)
                raised = jnp.exp(scores - top)
                total = row_sum(raised)
                probs = (raised * (1.0 / total)).astype(jnp.bfloat16)
                head = (p * third + pair * LANES) // HEAD + i
                lse[0, head : head + 1, :] = top + jnp.log(total)
                term = tn_dot(probs, val * mask)
                out = term if out is None else out + term
            att[:, p * third + pair * LANES : p * third + (pair + 1) * LANES] = out.astype(jnp.bfloat16)
    total = None
    for p in range(tp):
        term = nt_dot(att[:, p * third : (p + 1) * third], weight[p, :, columns:])
        total = term if total is None else total + term
    branch[...] = total.astype(jnp.bfloat16)
    after = value + mods[0, 2:3, :] * (total + bias[...])
    mid[...] = after
    normed, _ = norm_parts(after)
    seq_m[...] = (normed * (1.0 + mods[0, 4:5, :]) + mods[0, 3:4, :]).astype(jnp.bfloat16)


def gelu_parts(value):
    square = value * value
    inner = GELU_A * (value + GELU_B * (square * value))
    return jnp.tanh(inner), square


def mlp_forward_kernel(info, chunk, seq_m, mid, mods, expand_bias, reduce_bias, *rest):
    parts_e, parts_r, pre, acted, branch, stream, w_expand, w_reduce, sems = rest
    tp, _, columns = w_expand.shape

    @pl.when(pl.program_id(0) == 0)
    def _():
        run_copies(
            column_copy(info[0], parts_e, w_expand, sems.at[0]),
            column_copy(info[1], parts_r, w_reduce, sems.at[1]),
        )

    for p in range(tp):
        for start in range(0, columns, chunk):
            cols = slice(p * columns + start, p * columns + start + chunk)
            value = nn_dot(seq_m[...], w_expand[p, :, start : start + chunk]) + expand_bias[:, cols]
            pre[:, cols] = value
            bent, _ = gelu_parts(value)
            acted[:, cols] = (0.5 * value * (1.0 + bent)).astype(jnp.bfloat16)
    total = None
    for p in range(tp):
        term = nt_dot(acted[:, p * columns : (p + 1) * columns], w_reduce[p])
        total = term if total is None else total + term
    branch[...] = total.astype(jnp.bfloat16)
    stream[...] = mid[...] + mods[0, 5:6, :] * (total + reduce_bias[...])


def mlp_backward_kernel(info, chunk, grad_out, branch_m, pre, mid, branch_a, mods, reduce_bias, out_bias, *rest):
    parts_e, parts_r, seq_grad_m, grad_pre, grad_mid, seq_grad_a = rest[:6]
    mod_grads, d_out, d_expand, d_reduce, w_expand, w_reduce, sems = rest[6:]
    tp, _, columns = w_expand.shape

    @pl.when(pl.program_id(0) == 0)
    def _():
        run_copies(
            column_copy(info[0], parts_e, w_expand, sems.at[0]),
            column_copy(info[1], parts_r, w_reduce, sems.at[1]),
        )
        d_out[...] = jnp.zeros_like(d_out)
        d_expand[...] = jnp.zeros_like(d_expand)
        d_reduce[...] = jnp.zeros_like(d_reduce)

    grad = grad_out[...]
    carried = mods[0, 5:6, :] * grad
    d_reduce[...] += row_sum(carried)
    mod_grads[0, 5:6, :] = row_sum(grad * (branch_m[...].astype(jnp.float32) + reduce_bias[...]))
    seq_grad_m[...] = carried.astype(jnp.bfloat16)
    spans = [(p, start) for p in range(tp) for start in range(0, columns, chunk)]

    def product(p, start):
        return nn_dot(seq_grad_m[...], w_reduce[p, :, start : start + chunk])

    total = None
    ahead = product(*spans[0])
    for i, (p, start) in enumerate(spans):
        back = ahead
        if i + 1 < len(spans):
            ahead = product(*spans[i + 1])
        cols = slice(p * columns + start, p * columns + start + chunk)
        value = pre[:, cols]
        bent, square = gelu_parts(value)
        slope = 0.5 * (1.0 + bent) + (0.5 * GELU_A) * value * (1.0 - bent * bent) * (
            1.0 + (3.0 * GELU_B) * square
        )
        low = (back * slope).astype(jnp.bfloat16)
        grad_pre[:, cols] = low
        d_expand[:, cols] += row_sum(low.astype(jnp.float32))
        term = nt_dot(low, w_expand[p, :, start : start + chunk])
        total = term if total is None else total + term
    normed, inverse = norm_parts(mid[...])
    mod_grads[0, 3:4, :] = row_sum(total)
    mod_grads[0, 4:5, :] = row_sum(total * normed)
    after = grad_out[...] + norm_back(normed, inverse, total * (1.0 + mods[0, 4:5, :]))
    grad_mid[...] = after
    mod_grads[0, 2:3, :] = row_sum(after * (branch_a[...].astype(jnp.float32) + out_bias[...]))
    carried = mods[0, 2:3, :] * after
    d_out[...] += row_sum(carried)
    seq_grad_a[...] = carried.astype(jnp.bfloat16)
    mod_grads[0, 0:2, :] = jnp.zeros((2, mod_grads.shape[2]), jnp.float32)


def attn_backward_kernel(info, columns, seq_grad, qkv, lse, stream, grad_mid, mods, *rest):
    parts, (grad_qkv, grad_in, mod_grads, back, weight, sems) = (rest[0], rest[1:])
    tp = weight.shape[0]
    third = columns // 3

    @pl.when(pl.program_id(0) == 0)
    def _():
        run_copies(column_copy(info, parts, weight, sems))

    masks = lane_masks(jnp.bfloat16)
    for p in range(tp):
        back[:, p * third : (p + 1) * third] = nn_dot(
            seq_grad[...], weight[p, :, columns:]
        ).astype(jnp.bfloat16)
    scale = 1.0 / math.sqrt(HEAD)
    for p in range(tp):
        for pair in range(third // LANES):
            base = p * columns + pair * LANES
            query = qkv[:, base : base + LANES]
            key = qkv[:, base + third : base + third + LANES]
            val = qkv[:, base + 2 * third : base + 2 * third + LANES]
            grad = back[:, p * third + pair * LANES : p * third + (pair + 1) * LANES]
            d_query, d_key, d_val = (None, None, None)
            for i, mask in enumerate(masks):
                head = (p * third + pair * LANES) // HEAD + i
                query_i, key_i, grad_i = (query * mask, key * mask, grad * mask)
                scores = nt_dot(key, query_i) * scale
                probs = jnp.exp(scores - lse[0, head : head + 1, :])
                d_probs = nt_dot(val, grad_i)
                d_scores = probs * (d_probs - row_sum(d_probs * probs))
                d_scores = d_scores.astype(jnp.bfloat16)
                terms = (
                    tn_dot(d_scores, key_i),
                    nn_dot(d_scores, query_i),
                    nn_dot(probs.astype(jnp.bfloat16), grad_i),
                )
                if i == 0:
                    d_query, d_key, d_val = terms
                else:
                    d_query, d_key, d_val = (d_query + terms[0], d_key + terms[1], d_val + terms[2])
            grad_qkv[:, base : base + LANES] = (d_query * scale).astype(jnp.bfloat16)
            grad_qkv[:, base + third : base + third + LANES] = (d_key * scale).astype(jnp.bfloat16)
            grad_qkv[:, base + 2 * third : base + 2 * third + LANES] = d_val.astype(jnp.bfloat16)
    total = None
    for p in range(tp):
        term = nt_dot(grad_qkv[:, p * columns : (p + 1) * columns], weight[p, :, :columns])
        total = term if total is None else total + term
    normed, inverse = norm_parts(stream[...])
    mod_grads[0, 0:1, :] = row_sum(total)
    mod_grads[0, 1:2, :] = row_sum(total * normed)
    grad_in[...] = grad_mid[...] + norm_back(normed, inverse, total * (1.0 + mods[0, 1:2, :]))


def final_kernel(scale_pred, stream, mods, noise, patch_out, grad_stream, mod_grads, d_patch, loss):
    @pl.when(pl.program_id(0) == 0)
    def _():
        d_patch[...] = jnp.zeros_like(d_patch)
        loss[...] = jnp.zeros_like(loss)

    normed, inverse = norm_parts(stream[...])
    final = (normed * (1.0 + mods[0, 1:2, :]) + mods[0, 0:1, :]).astype(jnp.bfloat16)
    error = nt_dot(final, patch_out[...]) - noise[0]
    loss[...] += row_sum(error * error)
    grad_pred = (error * scale_pred).astype(jnp.bfloat16)
    d_patch[...] += tn_dot(grad_pred, final)
    grad_final = nn_dot(grad_pred, patch_out[...])
    mod_grads[0, 0:1, :] = row_sum(grad_final)
    mod_grads[0, 1:2, :] = row_sum(grad_final * normed)
    grad_stream[...] = norm_back(normed, inverse, grad_final * (1.0 + mods[0, 1:2, :]))


def weight_grad_kernel(count, groups, place, left, right, *refs):
    turned = refs[-1]
    depth = turned.shape[0]
    rows = depth // count

    @pl.when((pl.program_id(0) == 0) & (pl.program_id(1) == 0))
    def _():
        for start in range(0, depth, LANES):
            block = jnp.transpose(left[:, start : start + LANES])
            for i in range(LANES // rows):
                k = place[0] ^ (start // rows + i)
                slot = (k % 2) * (count // 2) + k // 2
                turned[pl.ds(pl.multiple_of(slot * rows, rows), rows), :] = block[i * rows : (i + 1) * rows]

    half = depth // 2
    steps = pl.num_programs(1) // groups
    for group in range(groups):
        keep, send = refs[2 * group : 2 * group + 2]

        @pl.when(pl.program_id(1) // steps == group)
        def _():
            send[0] = nn_dot(turned[half:, :], right[...]).astype(jnp.bfloat16)
            keep[0] = nn_dot(turned[:half, :], right[...]).astype(jnp.bfloat16)


def params(semantics=1):
    return pltpu.CompilerParams(
        dimension_semantics=("arbitrary",) * semantics, vmem_limit_bytes=VMEM_BYTES
    )


ANY = pl.BlockSpec(memory_space=pl.ANY)
F32, BF16 = (jnp.float32, jnp.bfloat16)


def cost(flops, nbytes):
    return pl.CostEstimate(flops=int(flops), bytes_accessed=int(nbytes), transcendentals=0)


def hold(value, *after):
    def body(*refs):
        pass

    return pl.pallas_call(
        body,
        in_specs=[ANY] * (1 + len(after)),
        out_specs=ANY,
        out_shape=jax.ShapeDtypeStruct(value.shape, value.dtype),
        input_output_aliases={0: 0},
        cost_estimate=cost(0, 0),
    )(value, *after)


def token_rows(width, dtype):
    return ("token", (width,), dtype)


def latent_rows(dims, dtype):
    return ("latent", dims, dtype)


def one_sum(width):
    return ("sum", (1, width), F32)


def call_part(kernel, part, parts, latents, ins, anys, outs, scratch, estimate, after, before):
    count = latents // parts
    first = part * count

    def spec(kind, dims):
        if kind == "token":
            return pl.BlockSpec((TOK_LAT, dims[-1]), lambda i: (i + first, 0))
        if kind == "latent":
            return pl.BlockSpec((1,) + dims, lambda i: (i + first,) + (0,) * len(dims))
        return pl.BlockSpec(dims, lambda i: (0,) * len(dims))

    def dims_of(kind, array):
        return array.shape[1:] if kind == "latent" else array.shape

    out_shape = []
    for kind, dims, dtype in outs:
        lead = {"token": (latents * TOK_LAT,), "latent": (latents,), "sum": ()}[kind]
        out_shape.append(jax.ShapeDtypeStruct(lead + dims, dtype))
    filled = [i for i, (kind, _, _) in enumerate(outs) if kind != "sum"] if before else []
    head = len(ins) + len(anys)
    unused = len(filled) + len(after)

    def body(*refs):
        kernel(*refs[:head], *refs[head + unused :])

    return pl.pallas_call(
        body,
        grid=(count,),
        in_specs=[spec(kind, dims_of(kind, array)) for kind, array in ins] + [ANY] * (len(anys) + unused),
        out_specs=[spec(kind, dims) for kind, dims, _ in outs],
        out_shape=out_shape,
        scratch_shapes=scratch,
        input_output_aliases={head + j: i for j, i in enumerate(filled)},
        compiler_params=params(),
        cost_estimate=cost(estimate[0] / parts, estimate[1] / parts),
    )(*[array for _, array in ins], *anys, *[before[i] for i in filled], *after)


def call_parts(kernel, latents, ins, anys, outs, scratch, estimate, afters):
    parts = 2 if afters and latents % 2 == 0 else 1
    afters = afters or [lambda done: []] * 2
    result, sums = (None, None)
    for part in range(parts):
        after = afters[part](result) if parts > 1 else afters[0](None) + afters[1](None)
        result = call_part(
            kernel, part, parts, latents, ins, anys, outs, scratch, estimate, after, result
        )
        own = [value for value, (kind, _, _) in zip(result, outs) if kind == "sum"]
        sums = own if sums is None else [a + b for a, b in zip(sums, own)]
    sums = iter(sums)
    return [next(sums) if kind == "sum" else value for value, (kind, _, _) in zip(result, outs)]


def run_attn_forward(stream, mods, out_bias, pieces, columns, afters):
    total, depth = stream.shape
    latents = total // TOK_LAT
    tp = lax.axis_size(TP)
    third = columns // 3
    width = columns + third
    return call_parts(
        functools.partial(attn_forward_kernel, pieces[1], columns),
        latents,
        [("token", stream), ("latent", mods), ("whole", out_bias)],
        [pieces[0]],
        [
            token_rows(depth, BF16),
            token_rows(tp * columns, BF16),
            latent_rows((tp * third // HEAD, TOK_LAT), F32),
            token_rows(tp * third, BF16),
            token_rows(depth, BF16),
            token_rows(depth, F32),
            token_rows(depth, BF16),
        ],
        [pltpu.VMEM((tp, depth, width), BF16), pltpu.SemaphoreType.DMA],
        (2 * total * depth * width * tp * 2.5, total * depth * 24),
        afters,
    )


def mlp_scratch(pieces_e, pieces_r, depth):
    tp = lax.axis_size(TP)
    columns = pieces_e[2]
    return [
        pltpu.VMEM((tp, depth, columns), BF16),
        pltpu.VMEM((tp, depth, columns), BF16),
        pltpu.SemaphoreType.DMA((2,)),
    ]


def run_mlp_forward(seq_m, mid, mods, expand_bias, reduce_bias, pieces_e, pieces_r, afters):
    total, depth = mid.shape
    hidden = expand_bias.shape[1]
    chunk = hidden // lax.axis_size(TP)
    return call_parts(
        functools.partial(mlp_forward_kernel, (pieces_e[1], pieces_r[1]), chunk),
        total // TOK_LAT,
        [("token", seq_m), ("token", mid), ("latent", mods), ("whole", expand_bias), ("whole", reduce_bias)],
        [pieces_e[0], pieces_r[0]],
        [
            token_rows(hidden, F32),
            token_rows(hidden, BF16),
            token_rows(depth, BF16),
            token_rows(depth, F32),
        ],
        mlp_scratch(pieces_e, pieces_r, depth),
        (6 * total * depth * hidden, total * hidden * 6),
        afters,
    )


def run_mlp_backward(
    grad_out, branch_m, pre, mid, branch_a, mods, reduce_bias, out_bias, pieces_e, pieces_r, afters
):
    total, depth = mid.shape
    hidden = pre.shape[1]
    chunk = min(hidden // lax.axis_size(TP), 256)
    return call_parts(
        functools.partial(mlp_backward_kernel, (pieces_e[1], pieces_r[1]), chunk),
        total // TOK_LAT,
        [
            ("token", grad_out),
            ("token", branch_m),
            ("token", pre),
            ("token", mid),
            ("token", branch_a),
            ("latent", mods),
            ("whole", reduce_bias),
            ("whole", out_bias),
        ],
        [pieces_e[0], pieces_r[0]],
        [
            token_rows(depth, BF16),
            token_rows(hidden, BF16),
            token_rows(depth, F32),
            token_rows(depth, BF16),
            latent_rows((6, depth), F32),
            one_sum(depth),
            one_sum(hidden),
            one_sum(depth),
        ],
        mlp_scratch(pieces_e, pieces_r, depth),
        (6 * total * depth * hidden, total * hidden * 6),
        afters,
    )


def run_attn_backward(seq_grad, qkv, lse, stream, grad_mid, mods, pieces, columns, afters):
    total, depth = stream.shape
    tp = lax.axis_size(TP)
    third = columns // 3
    width = columns + third
    return call_parts(
        functools.partial(attn_backward_kernel, pieces[1], columns),
        total // TOK_LAT,
        [
            ("token", seq_grad),
            ("token", qkv),
            ("latent", lse),
            ("token", stream),
            ("token", grad_mid),
            ("latent", mods),
        ],
        [pieces[0]],
        [token_rows(tp * columns, BF16), token_rows(depth, F32), latent_rows((2, depth), F32)],
        [
            pltpu.VMEM((TOK_LAT, tp * third), BF16),
            pltpu.VMEM((tp, depth, width), BF16),
            pltpu.SemaphoreType.DMA,
        ],
        (2 * total * depth * width * tp * 3, total * depth * 24),
        afters,
    )


def run_final(stream, mods, noise, patch_out, scale_pred):
    total, depth = stream.shape
    return call_part(
        functools.partial(final_kernel, scale_pred),
        0,
        1,
        total // TOK_LAT,
        [("token", stream), ("latent", mods), ("latent", noise), ("whole", patch_out)],
        [],
        [
            token_rows(depth, F32),
            latent_rows((2, depth), F32),
            ("sum", (CH, depth), F32),
            one_sum(CH),
        ],
        [],
        (6 * total * depth * LANES, total * depth * 8),
        [],
        None,
    )


def start_sums(left, right, columns, firsts, after):
    total, depth = left.shape
    tp, count = (lax.axis_size(TP), lax.axis_size(FSDP))
    groups = len(firsts)
    width = columns // groups
    chunk = next(size for size in (768, 512, 384, 256, 128) if width % size == 0)
    steps = columns // chunk
    each = width // chunk
    place = jnp.stack([lax.axis_index(FSDP), lax.axis_index(TP)]).astype(jnp.int32)

    def out(group):
        return pl.BlockSpec(
            (1, depth // 2, chunk),
            lambda p, j, place: (p, 0, jnp.clip(j - group * each, 0, each - 1)),
        )

    def body(place, left, right, *rest):
        weight_grad_kernel(count, groups, place, left, right, *rest[len(after) :])

    results = pl.pallas_call(
        body,
        grid_spec=pltpu.PrefetchScalarGridSpec(
            num_scalar_prefetch=1,
            grid=(tp, steps),
            in_specs=[
                pl.BlockSpec((total, depth), lambda p, j, place: (0, 0)),
                pl.BlockSpec((total, chunk), lambda p, j, place: (0, (p ^ place[1]) * steps + j)),
            ]
            + [ANY] * len(after),
            out_specs=[out(i // 2) for i in range(2 * groups)],
            scratch_shapes=[pltpu.VMEM((depth, total), BF16)],
        ),
        out_shape=[jax.ShapeDtypeStruct((tp, depth // 2, width), BF16)] * (2 * groups),
        compiler_params=params(2),
        cost_estimate=cost(2.5 * total * depth * columns * tp, total * (depth + columns * tp) * 2),
    )(place, left, right, *after)
    return [GradientSum(*results[2 * i : 2 * i + 2], first) for i, first in enumerate(firsts)]


def heads_apart(matrix):
    rows, columns = matrix.shape
    return matrix.reshape(rows, columns // (3 * HEAD), 3, HEAD).swapaxes(1, 2).reshape(rows, columns)


def heads_together(matrix):
    rows, columns = matrix.shape
    return matrix.reshape(rows, 3, columns // (3 * HEAD), HEAD).swapaxes(1, 2).reshape(rows, columns)


def adam(weight, first, second, grad, factor):
    grad = grad * factor
    new_first = BETA_ONE * first + (1.0 - BETA_ONE) * grad
    new_second = BETA_TWO * second + (1.0 - BETA_TWO) * grad * grad
    first_hat = new_first / (1.0 - BETA_ONE**STEP)
    second_hat = new_second / (1.0 - BETA_TWO**STEP)
    new_weight = weight - RATE * (first_hat / (jnp.sqrt(second_hat) + ADAM_EPS) + DECAY * weight)
    return (new_first, new_second, new_weight)


def per_device(
    clean_patches,
    noise_patches,
    timesteps,
    labels,
    qkv_weight,
    out_weight,
    expand_weight,
    reduce_weight,
    modulate_weight,
    embed_weight,
    bias_vector,
    qkv_first,
    out_first,
    expand_first,
    reduce_first,
    modulate_first,
    embed_first,
    bias_first,
    qkv_second,
    out_second,
    expand_second,
    reduce_second,
    modulate_second,
    embed_second,
    bias_second,
):
    tp_count, fsdp_count = (lax.axis_size(TP), lax.axis_size(FSDP))
    tp_rank, fsdp_rank = (lax.axis_index(TP), lax.axis_index(FSDP))
    everywhere = (FSDP, TP)
    rank = lax.axis_index(everywhere)
    own, length, _ = clean_patches.shape
    latents = own * fsdp_count * tp_count
    depth, columns = (embed_weight.shape[0] - FREQ - 2 * CH - CLASSES, embed_weight.shape[1])
    cols_qkv = qkv_weight.shape[2]

    step_in_own, step_out_own, patch_in_own, table_own, patch_out_own = split_embed(
        embed_weight.astype(BF16)
    )
    group = timesteps.shape[0]
    vector = jnp.concatenate(
        [
            timesteps.astype(F32),
            labels.astype(F32),
            bias_vector,
            patch_in_own.astype(F32).reshape(-1),
            patch_out_own.astype(F32).reshape(-1),
        ]
    )
    def shard(name, layer):
        if name == "attn":
            parts = [heads_apart(qkv_weight[layer].astype(BF16)), out_weight[layer].T.astype(BF16)]
            return jnp.concatenate(parts, axis=1)
        if name == "expand":
            return expand_weight[layer].astype(BF16)
        return reduce_weight[layer].T.astype(BF16)

    low_modulate = modulate_weight.astype(BF16)
    cond_columns = jnp.concatenate([step_out_own, table_own], axis=0).reshape(-1, LANES)
    cond_rows = cond_columns.shape[0]
    cond_columns = jnp.pad(cond_columns, ((0, -cond_rows % 16), (0, 0)))
    packed, step_in, near_columns, near_modulate, matrix = run_head(
        padded(vector), step_in_own.reshape(-1, LANES), cond_columns, low_modulate, shard("attn", 0), 0
    )
    near_modulate = near_modulate.reshape(-1, modulate_weight.shape[1])
    near_columns = near_columns[:, :cond_rows].reshape(-1, depth + CLASSES, columns)
    near_columns = near_columns.swapaxes(0, 1).reshape(depth + CLASSES, -1)
    packed = packed.reshape(packed.shape[0], -1)[:, : vector.shape[0]]
    step_in = step_in.reshape(-1, FREQ, columns)
    first_of_tp = packed.reshape(fsdp_count, tp_count, -1)[:, 0]
    steps_all = first_of_tp[:, :group].reshape(-1).astype(jnp.int32)
    labels_all = first_of_tp[:, group : 2 * group].reshape(-1).astype(jnp.int32)
    at = 2 * group + bias_vector.shape[0]
    bias = packed[:, 2 * group : at].reshape(-1)

    def rows_of(block):
        return block.reshape(-1, CH, columns).swapaxes(0, 1).reshape(CH, -1).astype(BF16)

    patch_in_low = rows_of(packed[:, at : at + CH * columns])
    patch_out_low = rows_of(packed[:, at + CH * columns :])
    step_in_low = step_in.swapaxes(0, 1).reshape(FREQ, -1)
    ada_bias, layer_bias, step_in_bias, step_out_bias, patch_bias = split_bias(bias)

    def gather(shards):
        packed = jnp.concatenate(shards, axis=1)
        whole = lax.all_gather(packed, (TP, FSDP), axis=0, tiled=True)
        return whole.reshape(tp_count, -1, packed.shape[1])

    hidden = expand_weight.shape[2]
    width = hidden + cols_qkv + out_weight.shape[1]
    first_half = gather([shard("expand", 0), shard("reduce", 0)])
    second_attn = gather([hold(shard("attn", 1), matrix)])
    attn_width = width - hidden
    pieces = {
        ("attn", 0): (matrix, 0, attn_width),
        ("expand", 0): (first_half, 0, hidden),
        ("reduce", 0): (first_half, hidden, hidden),
        ("attn", 1): (second_attn, 0, attn_width),
    }

    features = step_features(steps_all).astype(BF16)
    step_pre = contract(features, step_in_low, "gf,fd->gd") + step_in_bias
    step_hidden = jax.nn.silu(step_pre).astype(BF16)
    onehot = (labels_all[:, None] == jnp.arange(CLASSES, dtype=jnp.int32)[None, :]).astype(F32)
    wide = tp_count * columns
    near_bias = jnp.take(
        step_out_bias.reshape(-1, 4 * wide), fsdp_rank // 4, axis=0
    )
    cond_near = (
        contract(step_hidden, near_columns[:depth], "gd,de->ge")
        + near_bias
        + contract(onehot.astype(BF16), near_columns[depth:], "gc,cd->gd")
    )
    place = (fsdp_rank % 4) * wide
    act_near = jax.nn.silu(cond_near).astype(BF16)
    act_own = lax.dynamic_slice_in_dim(act_near, place, wide, axis=1)
    far = far_flips()
    far_order = jnp.array([flip[0] for flip in far]) ^ fsdp_rank
    act_far = jnp.take(act_near.reshape(fsdp_count, group, -1), far_order, axis=0)
    mod_part = contract(
        act_far.reshape(len(far) * group, -1), near_modulate, "gd,de->ge"
    ).reshape(len(far), group, -1)
    mod_sum = mod_part[0]
    for k, flip in list(enumerate(far))[1:]:
        mod_sum = mod_sum + swap(mod_part[k].astype(BF16), flip).astype(F32)
    mods = exchange_tp(mod_sum.reshape(tp_count, own, -1)).swapaxes(0, 1).reshape(own, -1) + ada_bias
    mods = mods.reshape(own, 6 * LAYERS + 2, -1)
    steps_own = lax.dynamic_slice_in_dim(timesteps, tp_rank * own, own)
    signal, spread_level = noise_levels(steps_own)
    noisy = (
        signal[:, None, None] * clean_patches + spread_level[:, None, None] * noise_patches
    ).astype(BF16)
    stream = contract(noisy, patch_in_low, "gtc,cd->gtd") + patch_bias + place_table()[None]
    stream = stream.reshape(-1, depth)
    kept = [None] * LAYERS

    for layer in range(LAYERS):
        modulation = mods[:, 6 * layer : 6 * layer + 6]
        out_bias, expand_bias, reduce_bias = [value[None] for value in layer_bias[layer]]
        seq_a, qkv, lse, att, branch_a, mid, seq_m = run_attn_forward(
            stream, modulation, out_bias, pieces["attn", layer], cols_qkv, None
        )
        pre, acted, branch_m, after = run_mlp_forward(
            seq_m,
            mid,
            modulation,
            expand_bias,
            reduce_bias,
            pieces["expand", layer],
            pieces["reduce", layer],
            None,
        )
        if layer == 0:
            second_half = jnp.concatenate([shard("expand", 1), shard("reduce", 1)], axis=1)
            second_half = gather([hold(second_half, att)])
            pieces["expand", 1] = (second_half, 0, hidden)
            pieces["reduce", 1] = (second_half, hidden, hidden)
        kept[layer] = (stream, seq_a, qkv, lse, att, branch_a, mid, seq_m, pre, acted, branch_m)
        stream = after
    cond_matrix = jnp.concatenate([step_out_own, table_own], axis=0).T
    cond_matrix = lax.all_gather(hold(cond_matrix, seq_m), everywhere, axis=0, tiled=True)
    total = float(latents * length * CH)
    grad_stream, grad_final_mod, grad_patch_out, loss_rows = run_final(
        stream, mods[:, 6 * LAYERS :], noise_patches, patch_out_low, 2.0 / total
    )
    loss_local = jnp.sum(loss_rows)

    sums, reduced = ({}, {})

    def step(*wanted):
        return lambda done=None: [sent for key in wanted for sent in sums[key].step()]

    def finish(keys, array):
        if array is not None:
            wait_for(keys, array)
        return [sums[key].finish() for key in keys]

    def in_turn(steps, finished):
        return lambda done=None: steps() + finish(finished, None if done is None else done[0])

    def mlp_backward(layer, grad, afters):
        stream, seq_a, qkv, lse, att, branch_a, mid, seq_m, pre, acted, branch_m = kept[layer]
        out_bias, expand_bias, reduce_bias = [value[None] for value in layer_bias[layer]]
        return run_mlp_backward(
            grad,
            branch_m,
            pre,
            mid,
            branch_a,
            mods[:, 6 * layer : 6 * layer + 6],
            reduce_bias,
            out_bias,
            pieces["expand", layer],
            pieces["reduce", layer],
            afters,
        )

    mod_grads = [None] * LAYERS
    layer_bias_grads = [None] * LAYERS
    cols_out = out_weight.shape[1]
    halves = 2 if cols_qkv // 2 % LANES == 0 else 1
    qkv_keys = [[("qkv", layer, i) for i in range(halves)] for layer in range(LAYERS)]
    rest_keys = [[("reduce", layer, 0), ("expand", layer, 0), ("out", layer, 0)] for layer in range(LAYERS)]
    mlp_afters = [
        (step(*rest_keys[1]), in_turn(step(*qkv_keys[1], *rest_keys[1][1:]), rest_keys[1][:1])),
        None,
    ]
    grad_afters = [[step(), step(*qkv_keys[1]), step(*qkv_keys[1])], [step()] * 3]

    attn_afters = [
        (step(*rest_keys[0][:2]), in_turn(step(rest_keys[0][2]), qkv_keys[1])),
        (step(rest_keys[1][0]), step(rest_keys[1][1])),
    ]

    def wait_for(keys, array):
        for key in keys:
            sums[key].keep = hold(sums[key].keep, array)

    def start(name, layer, left, right, width, firsts, after):
        started = start_sums(left, right, width, firsts, list(after))
        for i, total_sum in enumerate(started):
            sums[name, layer, i] = total_sum

    for layer in reversed(range(LAYERS)):
        stream, seq_a, qkv, lse, att, branch_a, mid, seq_m, pre, acted, branch_m = kept[layer]
        seq_grad_m, grad_pre, grad_mid, seq_grad_a, mod_late, d_out, d_expand, d_reduce = mlp_backward(
            layer, grad_stream, mlp_afters[layer]
        )
        after = grad_afters[layer]
        if layer == 0:
            mod_known = [jnp.zeros_like(mod_late[:, :2]), mod_late[:, 2:]] + mod_grads[1:]
            mod_known = jnp.concatenate(mod_known + [grad_final_mod], axis=1).reshape(own, -1)
            mod_known = mod_known.astype(BF16)
            known_columns = mod_known.reshape(own, tp_count, -1).swapaxes(0, 1)
            known_columns = exchange_tp(known_columns).reshape(group, -1)
            known_columns = lax.all_gather(known_columns, FSDP, axis=0, tiled=True)
        start("reduce", layer, seq_grad_m, acted, hidden, [FSDP], after[0]())
        first = [sums["reduce", layer, 0].sent]
        start("expand", layer, seq_m, grad_pre, hidden, [TP], after[1]() + first)
        first = [sums["expand", layer, 0].sent]
        if layer == 0:
            first += finish(rest_keys[1][1:], first[0])
        start("out", layer, seq_grad_a, att, cols_out, [FSDP], after[2]() + first)
        grad_qkv, grad_stream, mod_early = run_attn_backward(
            seq_grad_a,
            qkv,
            lse,
            stream,
            grad_mid,
            mods[:, 6 * layer : 6 * layer + 6],
            pieces["attn", layer],
            cols_qkv,
            attn_afters[layer],
        )
        after = step(*(rest_keys[layer] if layer == 0 else rest_keys[layer][::2]))()
        start("qkv", layer, seq_a, grad_qkv, cols_qkv, [TP, FSDP][:halves], after)
        mod_grads[layer] = jnp.concatenate([mod_early, mod_late[:, 2:]], axis=1)
        layer_bias_grads[layer] = (d_out[0], d_expand[0], d_reduce[0])
    last_sent = [sums[key].sent for key in qkv_keys[0]]
    mod_columns = modulate_weight.shape[1]
    mod_early, grad_stream = (hold(mod_early, *last_sent), hold(grad_stream, *last_sent))
    mod_last = mod_early.reshape(own, -1).astype(BF16)
    last_columns = push([mod_last.reshape(-1, LANES)], [-(-mod_last.shape[1] // mod_columns) + 1], 3)[0]
    wait_for(qkv_keys[0] + rest_keys[0], last_columns)
    step(*qkv_keys[0], *rest_keys[0])()
    last_columns = last_columns.reshape(latents, -1)
    grad_embedded = grad_stream.astype(BF16)
    grad_patch_in = contract(noisy.reshape(-1, CH), grad_embedded, "tc,td->cd")
    grad_patch_bias = jnp.sum(grad_embedded.astype(F32), axis=0)

    last_columns = jnp.pad(last_columns, ((0, 0), (0, modulate_weight.shape[1] * tp_count - last_columns.shape[1])))
    grad_columns = known_columns + lax.dynamic_slice_in_dim(
        last_columns, tp_rank * modulate_weight.shape[1], modulate_weight.shape[1], axis=1
    )
    grad_ada = contract(act_own, grad_columns, "gd,ge->de")
    act_part = contract(grad_columns, low_modulate, "ge,de->gd").reshape(-1, own, low_modulate.shape[0])
    act_part = jnp.pad(act_part, ((0, 0), (0, -own % 8), (0, -act_part.shape[2] % LANES)))
    act_part = push([act_part], [1], 4)[0]
    act_part = act_part[:, :own, : low_modulate.shape[0]]
    act_part = jnp.sum(act_part.reshape(fsdp_count, tp_count, own, -1), axis=1).swapaxes(0, 1).reshape(own, -1)

    def of_own(value):
        return lax.dynamic_slice_in_dim(value, rank * own, own)

    cond_mine = (
        contract(of_own(step_hidden), cond_matrix[:, :depth], "gd,ed->ge")
        + step_out_bias
        + contract(of_own(onehot).astype(BF16), cond_matrix[:, depth:], "gc,dc->gd")
    )
    grad_cond = local_back(jax.nn.silu, cond_mine, act_part)
    grad_hidden = exact_dot(grad_cond, cond_matrix[:, :depth].astype(F32))
    grad_step_pre = local_back(jax.nn.silu, of_own(step_pre), grad_hidden)
    both_grads = jnp.concatenate([grad_cond, grad_step_pre], axis=0).reshape(2 * own, -1, columns)
    both_grads = jnp.pad(
        both_grads.swapaxes(0, 1), ((0, 0), (0, -2 * own % 8), (0, -columns % LANES))
    )

    pieces_bias = [
        jnp.sum(mod_known.astype(F32), axis=0)
        + jnp.pad(jnp.sum(mod_last.astype(F32), axis=0), (0, mod_known.shape[1] - mod_last.shape[1]))
    ]
    for layer in range(LAYERS):
        pieces_bias += layer_bias_grads[layer]
    pieces_bias += [jnp.zeros((2 * depth,), F32), grad_patch_bias]
    chunk = bias_vector.shape[0]
    small = jnp.concatenate(
        [
            jnp.concatenate(pieces_bias).reshape(-1, chunk),
            jnp.concatenate([grad_patch_in, grad_patch_out])
            .reshape(2 * CH, -1, columns)
            .swapaxes(0, 1)
            .reshape(-1, 2 * CH * columns),
        ],
        axis=1,
    )
    width = small.shape[1]
    small = jnp.pad(small, ((0, 0), (0, -width % (8 * LANES)))).reshape(small.shape[0], -1, LANES)
    small, both_grads = push([small, both_grads], [1, 1], 1)
    for (name, layer, i), total_sum in sums.items():
        reduced.setdefault((name, layer), []).append(total_sum.finish())
    reduced = {key: jnp.concatenate(parts, axis=1) for key, parts in reduced.items()}
    for layer in range(LAYERS):
        reduced["qkv", layer] = heads_together(reduced["qkv", layer])
    small = jnp.sum(small, axis=0).reshape(-1)[:width]
    grad_cond = both_grads[:, :own, :columns].reshape(latents, columns)
    grad_step_pre = both_grads[:, own : 2 * own, :columns].reshape(latents, columns)
    grad_table = exact_dot(onehot.T, grad_cond)
    grad_step_out = exact_dot(step_hidden.astype(F32).T, grad_cond)
    grad_step_in = exact_dot(features.astype(F32).T, grad_step_pre)
    step_bias_grads = jnp.concatenate([jnp.sum(grad_step_pre, axis=0), jnp.sum(grad_cond, axis=0)])
    bias_grad = small[:chunk]
    patch_grads = small[chunk:].reshape(2 * CH, columns)
    embed_grad = jnp.concatenate(
        [grad_step_in, grad_step_out, patch_grads[:CH], grad_table, patch_grads[CH:]], axis=0
    )
    grads = (
        jnp.stack([reduced["qkv", i] for i in range(LAYERS)]),
        jnp.stack([reduced["out", i].T for i in range(LAYERS)]),
        jnp.stack([reduced["expand", i] for i in range(LAYERS)]),
        jnp.stack([reduced["reduce", i].T for i in range(LAYERS)]),
        grad_ada,
        embed_grad,
        bias_grad,
    )
    square = jnp.zeros((), jnp.float32)
    for grad in grads:
        square = square + jnp.sum(grad * grad)
    square = square + jnp.sum(step_bias_grads * step_bias_grads)
    last = push([padded(jnp.concatenate([square[None], loss_local[None], step_bias_grads]))], [0], 2)[0]
    last = last.reshape(last.shape[0], -1)
    square, loss_total = jnp.sum(last[:, 0]), jnp.sum(last[:, 1])
    step_biases = [last[:, 2 : 2 + columns].reshape(-1), last[:, 2 + columns : 2 + 2 * columns].reshape(-1)]
    before = jnp.zeros((bias.shape[0] - 3 * depth,), F32)
    step_biases = jnp.concatenate([before] + step_biases + [jnp.zeros((depth,), F32)])
    bias_grad = bias_grad + lax.dynamic_slice_in_dim(step_biases, rank * chunk, chunk)
    grads = grads[:-1] + (bias_grad,)
    grad_norm = jnp.sqrt(square)
    factor = CLIP_AT / jnp.maximum(grad_norm, CLIP_AT)
    params = (
        qkv_weight,
        out_weight,
        expand_weight,
        reduce_weight,
        modulate_weight,
        embed_weight,
        bias_vector,
    )
    firsts = (
        qkv_first,
        out_first,
        expand_first,
        reduce_first,
        modulate_first,
        embed_first,
        bias_first,
    )
    seconds = (
        qkv_second,
        out_second,
        expand_second,
        reduce_second,
        modulate_second,
        embed_second,
        bias_second,
    )
    news = [adam(w, f, s, g, factor) for w, f, s, g in zip(params, firsts, seconds, grads)]
    qkv_moment, qkv_square, qkv_master = news[0]
    out_moment, out_square, out_master = news[1]
    expand_moment, expand_square, expand_master = news[2]
    reduce_moment, reduce_square, reduce_master = news[3]
    modulate_moment, modulate_square, modulate_master = news[4]
    embed_moment, embed_square, embed_master = news[5]
    bias_moment, bias_square, bias_master = news[6]
    return (
        loss_total,
        grad_norm,
        qkv_moment,
        qkv_square,
        qkv_master,
        out_moment,
        out_square,
        out_master,
        expand_moment,
        expand_square,
        expand_master,
        reduce_moment,
        reduce_square,
        reduce_master,
        modulate_moment,
        modulate_square,
        modulate_master,
        embed_moment,
        embed_square,
        embed_master,
        bias_moment,
        bias_square,
        bias_master,
        qkv_master.astype(jnp.bfloat16),
        out_master.astype(jnp.bfloat16),
        expand_master.astype(jnp.bfloat16),
        reduce_master.astype(jnp.bfloat16),
        modulate_master.astype(jnp.bfloat16),
        embed_master.astype(jnp.bfloat16),
    )


def solution(mesh):
    return jax.shard_map(
        per_device,
        mesh=mesh,
        in_specs=(
            P((FSDP, TP), None, None),
            P((FSDP, TP), None, None),
            P(FSDP),
            P(FSDP),
            P(None, FSDP, TP),
            P(None, TP, FSDP),
            P(None, FSDP, TP),
            P(None, TP, FSDP),
            P(FSDP, TP),
            P(None, (FSDP, TP)),
            P((FSDP, TP)),
            P(None, FSDP, TP),
            P(None, TP, FSDP),
            P(None, FSDP, TP),
            P(None, TP, FSDP),
            P(FSDP, TP),
            P(None, (FSDP, TP)),
            P((FSDP, TP)),
            P(None, FSDP, TP),
            P(None, TP, FSDP),
            P(None, FSDP, TP),
            P(None, TP, FSDP),
            P(FSDP, TP),
            P(None, (FSDP, TP)),
            P((FSDP, TP)),
        ),
        out_specs=(
            P(),
            P(),
            P(None, FSDP, TP),
            P(None, FSDP, TP),
            P(None, FSDP, TP),
            P(None, TP, FSDP),
            P(None, TP, FSDP),
            P(None, TP, FSDP),
            P(None, FSDP, TP),
            P(None, FSDP, TP),
            P(None, FSDP, TP),
            P(None, TP, FSDP),
            P(None, TP, FSDP),
            P(None, TP, FSDP),
            P(FSDP, TP),
            P(FSDP, TP),
            P(FSDP, TP),
            P(None, (FSDP, TP)),
            P(None, (FSDP, TP)),
            P(None, (FSDP, TP)),
            P((FSDP, TP)),
            P((FSDP, TP)),
            P((FSDP, TP)),
            P(None, FSDP, TP),
            P(None, TP, FSDP),
            P(None, FSDP, TP),
            P(None, TP, FSDP),
            P(FSDP, TP),
            P(None, (FSDP, TP)),
        ),
        check_vma=False,
    )
```

```python
import functools
import math

import jax
import jax.numpy as jnp
from jax import lax
from jax.experimental import pallas as pl
from jax.experimental.pallas import tpu as pltpu
from jax.sharding import PartitionSpec as P

D = 1024
HEAD = 64
FF = 4096
CH = 16
FREQ = 256
CLASSES = 32
SIDE = 16
LAYERS = 2
STEP = 10
TOK_LAT = 256
MODS = 14336


CLIP_AT = 0.01
RATE = 0.05
BETA_ONE = 0.5
BETA_TWO = 0.5
DECAY = 0.01
ADAM_EPS = 1e-08
NORM_EPS = 1e-06
EXACT = lax.Precision.HIGHEST


def contract(left, right, form):
    return jnp.einsum(form, left, right, preferred_element_type=jnp.float32)


def exact_dot(left, right):
    return jnp.dot(left, right, precision=EXACT)


def layer_norm(value):
    center = value - jnp.mean(value, -1, keepdims=True)
    return center * lax.rsqrt(jnp.mean(center * center, -1, keepdims=True) + NORM_EPS)


def gelu_tanh(value):
    return jax.nn.gelu(value, approximate=True)


def local_back(func, value, grad):
    _, pullback = jax.vjp(func, value)
    return pullback(grad)[0]


def noise_levels(steps):
    angle = (steps.astype(jnp.float32) / 1000.0 + 0.008) / 1.008 * (math.pi / 2)
    return (jnp.cos(angle), jnp.sin(angle))


def step_features(steps):
    half = FREQ // 2
    rates = jnp.exp(-math.log(10000.0) * jnp.arange(half, dtype=jnp.float32) / half)
    phase = steps.astype(jnp.float32)[:, None] * rates[None, :]
    return jnp.concatenate([jnp.cos(phase), jnp.sin(phase)], axis=1)


def place_table():
    quarter = D // 4
    rates = 1.0 / 10000.0 ** (jnp.arange(quarter, dtype=jnp.float32) / quarter)
    index = jnp.arange(TOK_LAT, dtype=jnp.int32)
    rows = (index // SIDE).astype(jnp.float32)[:, None] * rates[None, :]
    columns = (index % SIDE).astype(jnp.float32)[:, None] * rates[None, :]
    return jnp.concatenate(
        [jnp.sin(rows), jnp.cos(rows), jnp.sin(columns), jnp.cos(columns)], axis=1
    )


def split_embed(embed):
    start = FREQ + D
    return (
        embed[:FREQ],
        embed[FREQ:start],
        embed[start : start + CH],
        embed[start + CH : start + CH + CLASSES],
        embed[start + CH + CLASSES :],
    )


def split_bias(bias):
    layers = []
    for layer in range(LAYERS):
        base = MODS + layer * (2 * D + FF)
        layers.append(
            (
                bias[base : base + D],
                bias[base + D : base + D + FF],
                bias[base + D + FF : base + 2 * D + FF],
            )
        )
    tail = MODS + LAYERS * (2 * D + FF)
    return (
        bias[:MODS],
        layers,
        bias[tail : tail + D],
        bias[tail + D : tail + 2 * D],
        bias[tail + 2 * D : tail + 3 * D],
    )


LANES = 128
FSDP, TP = ("fsdp", "tp")
GELU_A = math.sqrt(2.0 / math.pi)
GELU_B = 0.044715
VMEM_BYTES = 60 * 1024 * 1024


def swap(value, flip):
    name, bits = (FSDP, flip[0]) if flip[0] else (TP, flip[1])
    return lax.ppermute(value, name, [(i, i ^ bits) for i in range(lax.axis_size(name))])


def bit_flips(name):
    bits = [1 << i for i in range(lax.axis_size(name).bit_length() - 1)]
    return [(bit, 0) if name == FSDP else (0, bit) for bit in bits]


def far_flips():
    return [(k << 2, 0) for k in range(max(lax.axis_size(FSDP) >> 2, 1))]


def middle_flips(first):
    fsdp, tp = (bit_flips(FSDP)[1:2], bit_flips(TP))
    return fsdp + tp if first == FSDP else tp + fsdp


CORE = (1, 0)


def both(one, other):
    return (one[0] ^ other[0], one[1] ^ other[1])


def gather_far(value):
    flips = far_flips()
    held = [value[None]] + [swap(value, flip)[None] for flip in flips[1:]]
    return jnp.concatenate(held, axis=0), flips


def double(held, flips, flip):
    return jnp.concatenate([held, swap(held, flip)], axis=0), flips + [both(f, flip) for f in flips]


def gather_relative(value, hops):
    held, flips = (value[None], [(0, 0)])
    for flip in hops:
        held, flips = double(held, flips, flip)
    return held, flips


def gather_small(value, axes):
    held, _ = gather_relative(value, [flip for name in reversed(axes) for flip in bit_flips(name)])
    return jnp.take(held, jnp.arange(held.shape[0]) ^ lax.axis_index(axes), axis=0)


def split_bit(value, axis, index):
    return lax.index_in_dim(value, index, axis, keepdims=False)


def scatter_sum(value, axes, axis):
    flips = [flip for name in reversed(axes) for flip in bit_flips(name)][::-1]
    count = 1 << len(flips)
    shape = value.shape
    value = value.reshape(shape[:axis] + (count, shape[axis] // count) + shape[axis + 1 :])
    value = jnp.take(value, jnp.arange(count) ^ lax.axis_index(axes), axis=axis)
    keep = jnp.moveaxis(value, axis, 0).reshape(
        (2,) * len(flips) + shape[:axis] + (shape[axis] // count,) + shape[axis + 1 :]
    )
    dims = list(flips)
    for flip in sorted(flips, key=lambda flip: flip != CORE):
        at = dims.index(flip)
        keep = split_bit(keep, at, 0) + swap(split_bit(keep, at, 1), flip)
        dims = dims[:at] + dims[at + 1 :]
    return keep


def exchange_tp(value):
    count, rank = (lax.axis_size(TP), lax.axis_index(TP))
    value = jnp.take(value, jnp.arange(count) ^ rank, axis=0)
    got = jnp.stack([value[0]] + [swap(value[k], (0, k)) for k in range(1, count)])
    return jnp.take(got, jnp.arange(count) ^ rank, axis=0)


def push_kernel(plans, arrays, *refs):
    ins, outs = (refs[:arrays], refs[arrays : 2 * arrays])
    send, recv = refs[2 * arrays :]
    fsdp, tp = (lax.axis_index(FSDP), lax.axis_index(TP))
    count = lax.axis_size(FSDP) * lax.axis_size(TP)
    me = fsdp * lax.axis_size(TP) + tp

    def partner(k):
        other = lax.rem(me + k, count)
        return (other // lax.axis_size(TP), lax.rem(other, lax.axis_size(TP)))

    barrier = pltpu.get_barrier_semaphore()

    def greet(k, carry):
        pl.semaphore_signal(barrier, inc=1, device_id=partner(k), device_id_type=pl.DeviceIdType.MESH)
        return carry

    lax.fori_loop(1, count, greet, 0)
    pl.semaphore_wait(barrier, count - 1)

    def copies(k):
        other = lax.rem(me + k, count)
        found = []
        for i, (plan, source, target) in enumerate(zip(plans, ins, outs)):
            view = source.at[other] if plan == 1 else source
            found.append(
                pltpu.make_async_remote_copy(
                    src_ref=view,
                    dst_ref=target.at[me],
                    send_sem=send.at[i, k],
                    recv_sem=recv.at[i, k],
                    device_id=partner(k),
                    device_id_type=pl.DeviceIdType.MESH,
                )
            )
        return found

    def start(k, carry):
        for plan, copy in zip(plans, copies(k)):
            if plan > 1:
                pl.when(partner(k)[1] < plan - 1)(copy.start)
            else:
                copy.start()
        return carry

    def finish(k, carry):
        for plan, copy in zip(plans, copies(k)):
            if plan > 1:
                pl.when(partner(k)[1] < plan - 1)(copy.wait_send)
                pl.when(tp < plan - 1)(copy.wait_recv)
            else:
                copy.wait()
        return carry

    lax.fori_loop(1, count, start, 0)
    for plan, source, target in zip(plans, ins, outs):
        target[pl.ds(me, 1)] = source[pl.ds(me, 1)] if plan == 1 else source[...][None]
    lax.fori_loop(1, count, finish, 0)


def push(arrays, plans, identity):
    count = lax.axis_size(FSDP) * lax.axis_size(TP)
    shapes = [array.shape[1:] if plan == 1 else array.shape for array, plan in zip(arrays, plans)]
    block = pl.BlockSpec(memory_space=pltpu.VMEM)
    return pl.pallas_call(
        functools.partial(push_kernel, plans, len(arrays)),
        in_specs=[block] * len(arrays),
        out_specs=[block] * len(arrays),
        out_shape=[
            jax.ShapeDtypeStruct((count,) + shape, array.dtype) for shape, array in zip(shapes, arrays)
        ],
        scratch_shapes=[pltpu.SemaphoreType.DMA((len(arrays), count))] * 2,
        compiler_params=pltpu.CompilerParams(
            collective_id=identity, has_side_effects=True, vmem_limit_bytes=VMEM_BYTES
        ),
        cost_estimate=pl.CostEstimate(flops=int(5e9), bytes_accessed=int(5e7), transcendentals=0),
    )(*arrays)


def flipped(index, bits):
    result, bit = (index, 1)
    while bit <= bits:
        if bits & bit:
            result = result + bit * (1 - 2 * lax.rem(index // bit, 2))
        bit *= 2
    return result


def head_kernel(packed, step_in, cond, modulate, shard, *refs):
    packed_all, step_in_all, cond_all, modulate_all, matrix = refs[:5]
    send, recv, small_send, small_recv, local = refs[5:]
    fsdp, tp = (lax.axis_index(FSDP), lax.axis_index(TP))
    tp_count = lax.axis_size(TP)
    count = lax.axis_size(FSDP) * tp_count
    me = fsdp * tp_count + tp
    slot = lax.rem(fsdp, 4)

    def device(k):
        other = lax.rem(me + k, count)
        return (other // tp_count, lax.rem(other, tp_count))

    barrier = pltpu.get_barrier_semaphore()

    def greet(k, carry):
        pl.semaphore_signal(barrier, inc=1, device_id=device(k), device_id_type=pl.DeviceIdType.MESH)
        return carry

    lax.fori_loop(1, count, greet, 0)
    pl.semaphore_wait(barrier, count - 1)

    made = []

    def remote(source, target, flip):
        copy = pltpu.make_async_remote_copy(
            src_ref=source,
            dst_ref=target,
            send_sem=send.at[len(made)],
            recv_sem=recv.at[len(made)],
            device_id=(flipped(fsdp, flip[0]), flipped(tp, flip[1])),
            device_id_type=pl.DeviceIdType.MESH,
        )
        made.append(copy)
        copy.start()
        return copy

    rows, columns = shard.shape

    def region(flip, cols):
        row = pl.multiple_of(flipped(fsdp, flip[0]) * rows, rows)
        return matrix.at[flipped(tp, flip[1]), pl.ds(row, rows), cols]

    every = slice(0, columns)
    far = far_flips()
    own_copies = [
        pltpu.make_async_copy(modulate, modulate_all.at[slot], local.at[0]),
        pltpu.make_async_copy(shard, region((0, 0), every), local.at[1]),
    ]
    for copy in own_copies:
        copy.start()
    near = [remote(modulate, modulate_all.at[slot], (2, 0))]
    under_way = [remote(shard, region((0, 0), every), flip) for flip in far[1:]]
    plane = [(f, t) for f in range(4) for t in range(tp_count)][1:]
    last = [remote(cond, cond_all.at[slot * tp_count + tp], flip) for flip in plane]

    def small(k):
        pairs = ((packed, packed_all), (step_in, step_in_all))
        return [
            pltpu.make_async_remote_copy(
                src_ref=source,
                dst_ref=target.at[me],
                send_sem=small_send.at[i, k],
                recv_sem=small_recv.at[i, k],
                device_id=device(k),
                device_id_type=pl.DeviceIdType.MESH,
            )
            for i, (source, target) in enumerate(pairs)
        ]

    def start_small(k, carry):
        for copy in small(k):
            copy.start()
        return carry

    def finish_small(k, carry):
        for copy in small(k):
            copy.wait()
        return carry

    lax.fori_loop(1, count, start_small, 0)
    packed_all[pl.ds(me, 1)] = packed[...][None]
    step_in_all[pl.ds(me, 1)] = step_in[...][None]
    cond_all[pl.ds(slot * tp_count + tp, 1)] = cond[...][None]
    for copy in own_copies:
        copy.wait()
    for copy in near:
        copy.wait()
    last.append(remote(modulate, modulate_all.at[slot], CORE))
    partner = flipped(slot, 2)
    last.append(remote(modulate_all.at[partner], modulate_all.at[partner], CORE))
    for copy in under_way:
        copy.wait()
    orders = (middle_flips(FSDP), middle_flips(TP))
    held = [list(far), list(far)]
    halves = (slice(0, columns // 2), slice(columns // 2, columns))
    for step in range(len(orders[0])):
        under_way = []
        for color, cols in enumerate(halves):
            flip = orders[color][step]
            under_way += [remote(region(f, cols), region(f, cols), flip) for f in held[color]]
            held[color] = held[color] + [both(f, flip) for f in held[color]]
        for copy in under_way:
            copy.wait()
    last += [remote(region(f, every), region(f, every), CORE) for f in held[0]]
    lax.fori_loop(1, count, finish_small, 0)
    for copy in last:
        copy.wait()


def run_head(packed, step_in, cond, modulate, shard, identity):
    tp, fsdp = (lax.axis_size(TP), lax.axis_size(FSDP))
    count = fsdp * tp
    rows, columns = shard.shape
    vmem = pl.BlockSpec(memory_space=pltpu.VMEM)
    total = fsdp // 4 + 4 * tp + 2 + 2 * (fsdp // 4) * (2 * tp - 1) + fsdp * tp
    shapes = [
        ((count,) + packed.shape, F32),
        ((count,) + step_in.shape, BF16),
        ((4 * tp,) + cond.shape, BF16),
        ((4,) + modulate.shape, BF16),
        ((tp, rows * fsdp, columns), BF16),
    ]
    return pl.pallas_call(
        head_kernel,
        in_specs=[vmem] * 3 + [ANY] * 2,
        out_specs=[vmem] * 3 + [ANY] * 2,
        out_shape=[jax.ShapeDtypeStruct(shape, dtype) for shape, dtype in shapes],
        scratch_shapes=[pltpu.SemaphoreType.DMA((total,))] * 2
        + [pltpu.SemaphoreType.DMA((2, count))] * 2
        + [pltpu.SemaphoreType.DMA((2,))],
        compiler_params=pltpu.CompilerParams(
            collective_id=identity, has_side_effects=True, vmem_limit_bytes=VMEM_BYTES
        ),
        cost_estimate=pl.CostEstimate(flops=int(4e10), bytes_accessed=int(1e8), transcendentals=0),
    )(packed, step_in, cond, modulate, shard)


def padded(vector):
    return jnp.pad(vector, (0, -vector.shape[0] % (8 * LANES))).reshape(-1, LANES)


class GradientSum:
    def __init__(self, keep, send, first):
        fsdp = bit_flips(FSDP)
        self.dims = bit_flips(TP)[::-1] + fsdp[2:][::-1] + fsdp[1:2]
        self.rows, self.columns = (keep.shape[1] * 2 // lax.axis_size(FSDP), keep.shape[2])
        self.flips = middle_flips(first)[::-1]
        self.keep = keep.reshape((2,) * len(self.dims) + (self.rows, self.columns))
        self.sent = send
        self.next = CORE
        self.far, self.total = (None, None)

    def step(self):
        got = swap(self.sent, self.next).reshape(self.keep.shape)

        def part(axis, index):
            return split_bit(self.keep, axis, index).astype(F32) + split_bit(got, axis, index).astype(F32)

        if self.flips:
            self.next = self.flips.pop(0)
            axis = self.dims.index(self.next)
            self.sent, self.keep = (part(axis, 1).astype(BF16), part(axis, 0).astype(BF16))
            self.dims = self.dims[:axis] + self.dims[axis + 1 :]
            return [self.sent]
        blocks = (-1, self.rows, self.columns)
        self.keep, got = (self.keep.reshape(blocks), got.reshape(blocks))
        self.far = [part(0, k).astype(BF16) for k in range(1, self.keep.shape[0])]
        self.keep = part(0, 0)
        return self.far

    def finish(self):
        if self.total is not None:
            return self.total
        while self.far is None:
            self.step()
        result = self.keep
        for flip, sent in zip(far_flips()[1:], self.far):
            result = result + swap(sent, flip).astype(F32)
        self.total = result
        return result


def nt_dot(left, right):
    return lax.dot_general(left, right, (((1,), (1,)), ((), ())), preferred_element_type=jnp.float32)


def nn_dot(left, right):
    return lax.dot_general(left, right, (((1,), (0,)), ((), ())), preferred_element_type=jnp.float32)


def tn_dot(left, right):
    return lax.dot_general(left, right, (((0,), (0,)), ((), ())), preferred_element_type=jnp.float32)


def norm_parts(value):
    center = value - jnp.mean(value, -1, keepdims=True)
    inverse = lax.rsqrt(jnp.mean(center * center, -1, keepdims=True) + NORM_EPS)
    return center * inverse, inverse


def norm_back(normed, inverse, grad):
    mean_grad = jnp.mean(grad, -1, keepdims=True)
    mean_both = jnp.mean(grad * normed, -1, keepdims=True)
    return inverse * (grad - mean_grad - normed * mean_both)


def row_sum(value):
    return jnp.sum(value, axis=0, keepdims=True)


def column_copy(start, ref, target, sem):
    return [pltpu.make_async_copy(ref.at[:, :, pl.ds(start, target.shape[2])], target, sem)]


def run_copies(*groups):
    for group in groups:
        for copy in group:
            copy.start()
    for group in groups:
        for copy in group:
            copy.wait()


def lane_masks(dtype):
    lane = lax.broadcasted_iota(jnp.int32, (1, LANES), 1)
    return [((lane // HEAD) == i).astype(jnp.float32).astype(dtype) for i in range(LANES // HEAD)]


def attn_forward_kernel(info, columns, stream, mods, bias, *rest):
    parts, (seq_a, qkv, lse, att, branch, mid, seq_m, weight, sems) = (rest[0], rest[1:])
    tp = weight.shape[0]
    third = columns // 3

    @pl.when(pl.program_id(0) == 0)
    def _():
        run_copies(column_copy(info, parts, weight, sems))

    value = stream[...]
    normed, _ = norm_parts(value)
    seq_a[...] = (normed * (1.0 + mods[0, 1:2, :]) + mods[0, 0:1, :]).astype(jnp.bfloat16)
    for p in range(tp):
        qkv[:, p * columns : (p + 1) * columns] = nn_dot(
            seq_a[...], weight[p, :, :columns]
        ).astype(jnp.bfloat16)
    masks = lane_masks(jnp.bfloat16)
    for p in range(tp):
        for pair in range(third // LANES):
            base = p * columns + pair * LANES
            query = qkv[:, base : base + LANES]
            key = qkv[:, base + third : base + third + LANES]
            val = qkv[:, base + 2 * third : base + 2 * third + LANES]
            out = None
            for i, mask in enumerate(masks):
                scores = nt_dot(key, query * mask) * (1.0 / math.sqrt(HEAD))
                top = jnp.max(scores, axis=0, keepdims=True)
                raised = jnp.exp(scores - top)
                total = row_sum(raised)
                probs = (raised * (1.0 / total)).astype(jnp.bfloat16)
                head = (p * third + pair * LANES) // HEAD + i
                lse[0, head : head + 1, :] = top + jnp.log(total)
                term = tn_dot(probs, val * mask)
                out = term if out is None else out + term
            att[:, p * third + pair * LANES : p * third + (pair + 1) * LANES] = out.astype(jnp.bfloat16)
    total = None
    for p in range(tp):
        term = nt_dot(att[:, p * third : (p + 1) * third], weight[p, :, columns:])
        total = term if total is None else total + term
    branch[...] = total.astype(jnp.bfloat16)
    after = value + mods[0, 2:3, :] * (total + bias[...])
    mid[...] = after
    normed, _ = norm_parts(after)
    seq_m[...] = (normed * (1.0 + mods[0, 4:5, :]) + mods[0, 3:4, :]).astype(jnp.bfloat16)


def gelu_parts(value):
    square = value * value
    inner = GELU_A * (value + GELU_B * (square * value))
    return jnp.tanh(inner), square


def mlp_forward_kernel(info, chunk, seq_m, mid, mods, expand_bias, reduce_bias, *rest):
    parts_e, parts_r, pre, acted, branch, stream, w_expand, w_reduce, sems = rest
    tp, _, columns = w_expand.shape

    @pl.when(pl.program_id(0) == 0)
    def _():
        run_copies(
            column_copy(info[0], parts_e, w_expand, sems.at[0]),
            column_copy(info[1], parts_r, w_reduce, sems.at[1]),
        )

    for p in range(tp):
        for start in range(0, columns, chunk):
            cols = slice(p * columns + start, p * columns + start + chunk)
            value = nn_dot(seq_m[...], w_expand[p, :, start : start + chunk]) + expand_bias[:, cols]
            pre[:, cols] = value
            bent, _ = gelu_parts(value)
            acted[:, cols] = (0.5 * value * (1.0 + bent)).astype(jnp.bfloat16)
    total = None
    for p in range(tp):
        term = nt_dot(acted[:, p * columns : (p + 1) * columns], w_reduce[p])
        total = term if total is None else total + term
    branch[...] = total.astype(jnp.bfloat16)
    stream[...] = mid[...] + mods[0, 5:6, :] * (total + reduce_bias[...])


def mlp_backward_kernel(info, chunk, grad_out, branch_m, pre, mid, branch_a, mods, reduce_bias, out_bias, *rest):
    parts_e, parts_r, seq_grad_m, grad_pre, grad_mid, seq_grad_a = rest[:6]
    mod_grads, d_out, d_expand, d_reduce, w_expand, w_reduce, sems = rest[6:]
    tp, _, columns = w_expand.shape

    @pl.when(pl.program_id(0) == 0)
    def _():
        run_copies(
            column_copy(info[0], parts_e, w_expand, sems.at[0]),
            column_copy(info[1], parts_r, w_reduce, sems.at[1]),
        )
        d_out[...] = jnp.zeros_like(d_out)
        d_expand[...] = jnp.zeros_like(d_expand)
        d_reduce[...] = jnp.zeros_like(d_reduce)

    grad = grad_out[...]
    carried = mods[0, 5:6, :] * grad
    d_reduce[...] += row_sum(carried)
    mod_grads[0, 5:6, :] = row_sum(grad * (branch_m[...].astype(jnp.float32) + reduce_bias[...]))
    seq_grad_m[...] = carried.astype(jnp.bfloat16)
    spans = [(p, start) for p in range(tp) for start in range(0, columns, chunk)]

    def product(p, start):
        return nn_dot(seq_grad_m[...], w_reduce[p, :, start : start + chunk])

    total = None
    ahead = product(*spans[0])
    for i, (p, start) in enumerate(spans):
        back = ahead
        if i + 1 < len(spans):
            ahead = product(*spans[i + 1])
        cols = slice(p * columns + start, p * columns + start + chunk)
        value = pre[:, cols]
        bent, square = gelu_parts(value)
        slope = 0.5 * (1.0 + bent) + (0.5 * GELU_A) * value * (1.0 - bent * bent) * (
            1.0 + (3.0 * GELU_B) * square
        )
        low = (back * slope).astype(jnp.bfloat16)
        grad_pre[:, cols] = low
        d_expand[:, cols] += row_sum(low.astype(jnp.float32))
        term = nt_dot(low, w_expand[p, :, start : start + chunk])
        total = term if total is None else total + term
    normed, inverse = norm_parts(mid[...])
    mod_grads[0, 3:4, :] = row_sum(total)
    mod_grads[0, 4:5, :] = row_sum(total * normed)
    after = grad_out[...] + norm_back(normed, inverse, total * (1.0 + mods[0, 4:5, :]))
    grad_mid[...] = after
    mod_grads[0, 2:3, :] = row_sum(after * (branch_a[...].astype(jnp.float32) + out_bias[...]))
    carried = mods[0, 2:3, :] * after
    d_out[...] += row_sum(carried)
    seq_grad_a[...] = carried.astype(jnp.bfloat16)
    mod_grads[0, 0:2, :] = jnp.zeros((2, mod_grads.shape[2]), jnp.float32)


def attn_backward_kernel(info, columns, seq_grad, qkv, lse, stream, grad_mid, mods, *rest):
    parts, (grad_qkv, grad_in, mod_grads, back, weight, sems) = (rest[0], rest[1:])
    tp = weight.shape[0]
    third = columns // 3

    @pl.when(pl.program_id(0) == 0)
    def _():
        run_copies(column_copy(info, parts, weight, sems))

    masks = lane_masks(jnp.bfloat16)
    for p in range(tp):
        back[:, p * third : (p + 1) * third] = nn_dot(
            seq_grad[...], weight[p, :, columns:]
        ).astype(jnp.bfloat16)
    scale = 1.0 / math.sqrt(HEAD)
    for p in range(tp):
        for pair in range(third // LANES):
            base = p * columns + pair * LANES
            query = qkv[:, base : base + LANES]
            key = qkv[:, base + third : base + third + LANES]
            val = qkv[:, base + 2 * third : base + 2 * third + LANES]
            grad = back[:, p * third + pair * LANES : p * third + (pair + 1) * LANES]
            d_query, d_key, d_val = (None, None, None)
            for i, mask in enumerate(masks):
                head = (p * third + pair * LANES) // HEAD + i
                query_i, key_i, grad_i = (query * mask, key * mask, grad * mask)
                scores = nt_dot(key, query_i) * scale
                probs = jnp.exp(scores - lse[0, head : head + 1, :])
                d_probs = nt_dot(val, grad_i)
                d_scores = probs * (d_probs - row_sum(d_probs * probs))
                d_scores = d_scores.astype(jnp.bfloat16)
                terms = (
                    tn_dot(d_scores, key_i),
                    nn_dot(d_scores, query_i),
                    nn_dot(probs.astype(jnp.bfloat16), grad_i),
                )
                if i == 0:
                    d_query, d_key, d_val = terms
                else:
                    d_query, d_key, d_val = (d_query + terms[0], d_key + terms[1], d_val + terms[2])
            grad_qkv[:, base : base + LANES] = (d_query * scale).astype(jnp.bfloat16)
            grad_qkv[:, base + third : base + third + LANES] = (d_key * scale).astype(jnp.bfloat16)
            grad_qkv[:, base + 2 * third : base + 2 * third + LANES] = d_val.astype(jnp.bfloat16)
    total = None
    for p in range(tp):
        term = nt_dot(grad_qkv[:, p * columns : (p + 1) * columns], weight[p, :, :columns])
        total = term if total is None else total + term
    normed, inverse = norm_parts(stream[...])
    mod_grads[0, 0:1, :] = row_sum(total)
    mod_grads[0, 1:2, :] = row_sum(total * normed)
    grad_in[...] = grad_mid[...] + norm_back(normed, inverse, total * (1.0 + mods[0, 1:2, :]))


def final_kernel(scale_pred, stream, mods, noise, patch_out, grad_stream, mod_grads, d_patch, loss):
    @pl.when(pl.program_id(0) == 0)
    def _():
        d_patch[...] = jnp.zeros_like(d_patch)
        loss[...] = jnp.zeros_like(loss)

    normed, inverse = norm_parts(stream[...])
    final = (normed * (1.0 + mods[0, 1:2, :]) + mods[0, 0:1, :]).astype(jnp.bfloat16)
    error = nt_dot(final, patch_out[...]) - noise[0]
    loss[...] += row_sum(error * error)
    grad_pred = (error * scale_pred).astype(jnp.bfloat16)
    d_patch[...] += tn_dot(grad_pred, final)
    grad_final = nn_dot(grad_pred, patch_out[...])
    mod_grads[0, 0:1, :] = row_sum(grad_final)
    mod_grads[0, 1:2, :] = row_sum(grad_final * normed)
    grad_stream[...] = norm_back(normed, inverse, grad_final * (1.0 + mods[0, 1:2, :]))


def weight_grad_kernel(count, groups, place, left, right, *refs):
    turned = refs[-1]
    depth = turned.shape[0]
    rows = depth // count

    @pl.when((pl.program_id(0) == 0) & (pl.program_id(1) == 0))
    def _():
        for start in range(0, depth, LANES):
            block = jnp.transpose(left[:, start : start + LANES])
            for i in range(LANES // rows):
                k = place[0] ^ (start // rows + i)
                slot = (k % 2) * (count // 2) + k // 2
                turned[pl.ds(pl.multiple_of(slot * rows, rows), rows), :] = block[i * rows : (i + 1) * rows]

    half = depth // 2
    steps = pl.num_programs(1) // groups
    for group in range(groups):
        keep, send = refs[2 * group : 2 * group + 2]

        @pl.when(pl.program_id(1) // steps == group)
        def _():
            send[0] = nn_dot(turned[half:, :], right[...]).astype(jnp.bfloat16)
            keep[0] = nn_dot(turned[:half, :], right[...]).astype(jnp.bfloat16)


def params(semantics=1):
    return pltpu.CompilerParams(
        dimension_semantics=("arbitrary",) * semantics, vmem_limit_bytes=VMEM_BYTES
    )


ANY = pl.BlockSpec(memory_space=pl.ANY)
F32, BF16 = (jnp.float32, jnp.bfloat16)


def cost(flops, nbytes):
    return pl.CostEstimate(flops=int(flops), bytes_accessed=int(nbytes), transcendentals=0)


def hold(value, *after):
    def body(*refs):
        pass

    return pl.pallas_call(
        body,
        in_specs=[ANY] * (1 + len(after)),
        out_specs=ANY,
        out_shape=jax.ShapeDtypeStruct(value.shape, value.dtype),
        input_output_aliases={0: 0},
        cost_estimate=cost(0, 0),
    )(value, *after)


def token_rows(width, dtype):
    return ("token", (width,), dtype)


def latent_rows(dims, dtype):
    return ("latent", dims, dtype)


def one_sum(width):
    return ("sum", (1, width), F32)


def call_part(kernel, part, parts, latents, ins, anys, outs, scratch, estimate, after, before):
    count = latents // parts
    first = part * count

    def spec(kind, dims):
        if kind == "token":
            return pl.BlockSpec((TOK_LAT, dims[-1]), lambda i: (i + first, 0))
        if kind == "latent":
            return pl.BlockSpec((1,) + dims, lambda i: (i + first,) + (0,) * len(dims))
        return pl.BlockSpec(dims, lambda i: (0,) * len(dims))

    def dims_of(kind, array):
        return array.shape[1:] if kind == "latent" else array.shape

    out_shape = []
    for kind, dims, dtype in outs:
        lead = {"token": (latents * TOK_LAT,), "latent": (latents,), "sum": ()}[kind]
        out_shape.append(jax.ShapeDtypeStruct(lead + dims, dtype))
    filled = [i for i, (kind, _, _) in enumerate(outs) if kind != "sum"] if before else []
    head = len(ins) + len(anys)
    unused = len(filled) + len(after)

    def body(*refs):
        kernel(*refs[:head], *refs[head + unused :])

    return pl.pallas_call(
        body,
        grid=(count,),
        in_specs=[spec(kind, dims_of(kind, array)) for kind, array in ins] + [ANY] * (len(anys) + unused),
        out_specs=[spec(kind, dims) for kind, dims, _ in outs],
        out_shape=out_shape,
        scratch_shapes=scratch,
        input_output_aliases={head + j: i for j, i in enumerate(filled)},
        compiler_params=params(),
        cost_estimate=cost(estimate[0] / parts, estimate[1] / parts),
    )(*[array for _, array in ins], *anys, *[before[i] for i in filled], *after)


def call_parts(kernel, latents, ins, anys, outs, scratch, estimate, afters):
    parts = 2 if afters and latents % 2 == 0 else 1
    afters = afters or [lambda done: []] * 2
    result, sums = (None, None)
    for part in range(parts):
        after = afters[part](result) if parts > 1 else afters[0](None) + afters[1](None)
        result = call_part(
            kernel, part, parts, latents, ins, anys, outs, scratch, estimate, after, result
        )
        own = [value for value, (kind, _, _) in zip(result, outs) if kind == "sum"]
        sums = own if sums is None else [a + b for a, b in zip(sums, own)]
    sums = iter(sums)
    return [next(sums) if kind == "sum" else value for value, (kind, _, _) in zip(result, outs)]


def run_attn_forward(stream, mods, out_bias, pieces, columns, afters):
    total, depth = stream.shape
    latents = total // TOK_LAT
    tp = lax.axis_size(TP)
    third = columns // 3
    width = columns + third
    return call_parts(
        functools.partial(attn_forward_kernel, pieces[1], columns),
        latents,
        [("token", stream), ("latent", mods), ("whole", out_bias)],
        [pieces[0]],
        [
            token_rows(depth, BF16),
            token_rows(tp * columns, BF16),
            latent_rows((tp * third // HEAD, TOK_LAT), F32),
            token_rows(tp * third, BF16),
            token_rows(depth, BF16),
            token_rows(depth, F32),
            token_rows(depth, BF16),
        ],
        [pltpu.VMEM((tp, depth, width), BF16), pltpu.SemaphoreType.DMA],
        (2 * total * depth * width * tp * 2.5, total * depth * 24),
        afters,
    )


def mlp_scratch(pieces_e, pieces_r, depth):
    tp = lax.axis_size(TP)
    columns = pieces_e[2]
    return [
        pltpu.VMEM((tp, depth, columns), BF16),
        pltpu.VMEM((tp, depth, columns), BF16),
        pltpu.SemaphoreType.DMA((2,)),
    ]


def run_mlp_forward(seq_m, mid, mods, expand_bias, reduce_bias, pieces_e, pieces_r, afters):
    total, depth = mid.shape
    hidden = expand_bias.shape[1]
    chunk = hidden // lax.axis_size(TP)
    return call_parts(
        functools.partial(mlp_forward_kernel, (pieces_e[1], pieces_r[1]), chunk),
        total // TOK_LAT,
        [("token", seq_m), ("token", mid), ("latent", mods), ("whole", expand_bias), ("whole", reduce_bias)],
        [pieces_e[0], pieces_r[0]],
        [
            token_rows(hidden, F32),
            token_rows(hidden, BF16),
            token_rows(depth, BF16),
            token_rows(depth, F32),
        ],
        mlp_scratch(pieces_e, pieces_r, depth),
        (6 * total * depth * hidden, total * hidden * 6),
        afters,
    )


def run_mlp_backward(
    grad_out, branch_m, pre, mid, branch_a, mods, reduce_bias, out_bias, pieces_e, pieces_r, afters
):
    total, depth = mid.shape
    hidden = pre.shape[1]
    chunk = min(hidden // lax.axis_size(TP), 256)
    return call_parts(
        functools.partial(mlp_backward_kernel, (pieces_e[1], pieces_r[1]), chunk),
        total // TOK_LAT,
        [
            ("token", grad_out),
            ("token", branch_m),
            ("token", pre),
            ("token", mid),
            ("token", branch_a),
            ("latent", mods),
            ("whole", reduce_bias),
            ("whole", out_bias),
        ],
        [pieces_e[0], pieces_r[0]],
        [
            token_rows(depth, BF16),
            token_rows(hidden, BF16),
            token_rows(depth, F32),
            token_rows(depth, BF16),
            latent_rows((6, depth), F32),
            one_sum(depth),
            one_sum(hidden),
            one_sum(depth),
        ],
        mlp_scratch(pieces_e, pieces_r, depth),
        (6 * total * depth * hidden, total * hidden * 6),
        afters,
    )


def run_attn_backward(seq_grad, qkv, lse, stream, grad_mid, mods, pieces, columns, afters):
    total, depth = stream.shape
    tp = lax.axis_size(TP)
    third = columns // 3
    width = columns + third
    return call_parts(
        functools.partial(attn_backward_kernel, pieces[1], columns),
        total // TOK_LAT,
        [
            ("token", seq_grad),
            ("token", qkv),
            ("latent", lse),
            ("token", stream),
            ("token", grad_mid),
            ("latent", mods),
        ],
        [pieces[0]],
        [token_rows(tp * columns, BF16), token_rows(depth, F32), latent_rows((2, depth), F32)],
        [
            pltpu.VMEM((TOK_LAT, tp * third), BF16),
            pltpu.VMEM((tp, depth, width), BF16),
            pltpu.SemaphoreType.DMA,
        ],
        (2 * total * depth * width * tp * 3, total * depth * 24),
        afters,
    )


def run_final(stream, mods, noise, patch_out, scale_pred):
    total, depth = stream.shape
    return call_part(
        functools.partial(final_kernel, scale_pred),
        0,
        1,
        total // TOK_LAT,
        [("token", stream), ("latent", mods), ("latent", noise), ("whole", patch_out)],
        [],
        [
            token_rows(depth, F32),
            latent_rows((2, depth), F32),
            ("sum", (CH, depth), F32),
            one_sum(CH),
        ],
        [],
        (6 * total * depth * LANES, total * depth * 8),
        [],
        None,
    )


def start_sums(left, right, columns, firsts, after):
    total, depth = left.shape
    tp, count = (lax.axis_size(TP), lax.axis_size(FSDP))
    groups = len(firsts)
    width = columns // groups
    chunk = next(size for size in (768, 512, 384, 256, 128) if width % size == 0)
    steps = columns // chunk
    each = width // chunk
    place = jnp.stack([lax.axis_index(FSDP), lax.axis_index(TP)]).astype(jnp.int32)

    def out(group):
        return pl.BlockSpec(
            (1, depth // 2, chunk),
            lambda p, j, place: (p, 0, jnp.clip(j - group * each, 0, each - 1)),
        )

    def body(place, left, right, *rest):
        weight_grad_kernel(count, groups, place, left, right, *rest[len(after) :])

    results = pl.pallas_call(
        body,
        grid_spec=pltpu.PrefetchScalarGridSpec(
            num_scalar_prefetch=1,
            grid=(tp, steps),
            in_specs=[
                pl.BlockSpec((total, depth), lambda p, j, place: (0, 0)),
                pl.BlockSpec((total, chunk), lambda p, j, place: (0, (p ^ place[1]) * steps + j)),
            ]
            + [ANY] * len(after),
            out_specs=[out(i // 2) for i in range(2 * groups)],
            scratch_shapes=[pltpu.VMEM((depth, total), BF16)],
        ),
        out_shape=[jax.ShapeDtypeStruct((tp, depth // 2, width), BF16)] * (2 * groups),
        compiler_params=params(2),
        cost_estimate=cost(2.5 * total * depth * columns * tp, total * (depth + columns * tp) * 2),
    )(place, left, right, *after)
    return [GradientSum(*results[2 * i : 2 * i + 2], first) for i, first in enumerate(firsts)]


def heads_apart(matrix):
    rows, columns = matrix.shape
    return matrix.reshape(rows, columns // (3 * HEAD), 3, HEAD).swapaxes(1, 2).reshape(rows, columns)


def heads_together(matrix):
    rows, columns = matrix.shape
    return matrix.reshape(rows, 3, columns // (3 * HEAD), HEAD).swapaxes(1, 2).reshape(rows, columns)


def adam(weight, first, second, grad, factor):
    grad = grad * factor
    new_first = BETA_ONE * first + (1.0 - BETA_ONE) * grad
    new_second = BETA_TWO * second + (1.0 - BETA_TWO) * grad * grad
    first_hat = new_first / (1.0 - BETA_ONE**STEP)
    second_hat = new_second / (1.0 - BETA_TWO**STEP)
    new_weight = weight - RATE * (first_hat / (jnp.sqrt(second_hat) + ADAM_EPS) + DECAY * weight)
    return (new_first, new_second, new_weight)


def per_device(
    clean_patches,
    noise_patches,
    timesteps,
    labels,
    qkv_weight,
    out_weight,
    expand_weight,
    reduce_weight,
    modulate_weight,
    embed_weight,
    bias_vector,
    qkv_first,
    out_first,
    expand_first,
    reduce_first,
    modulate_first,
    embed_first,
    bias_first,
    qkv_second,
    out_second,
    expand_second,
    reduce_second,
    modulate_second,
    embed_second,
    bias_second,
):
    tp_count, fsdp_count = (lax.axis_size(TP), lax.axis_size(FSDP))
    tp_rank, fsdp_rank = (lax.axis_index(TP), lax.axis_index(FSDP))
    everywhere = (FSDP, TP)
    rank = lax.axis_index(everywhere)
    own, length, _ = clean_patches.shape
    latents = own * fsdp_count * tp_count
    depth, columns = (embed_weight.shape[0] - FREQ - 2 * CH - CLASSES, embed_weight.shape[1])
    cols_qkv = qkv_weight.shape[2]

    step_in_own, step_out_own, patch_in_own, table_own, patch_out_own = split_embed(
        embed_weight.astype(BF16)
    )
    group = timesteps.shape[0]
    vector = jnp.concatenate(
        [
            timesteps.astype(F32),
            labels.astype(F32),
            bias_vector,
            patch_in_own.astype(F32).reshape(-1),
            patch_out_own.astype(F32).reshape(-1),
        ]
    )
    def shard(name, layer):
        if name == "attn":
            parts = [heads_apart(qkv_weight[layer].astype(BF16)), out_weight[layer].T.astype(BF16)]
            return jnp.concatenate(parts, axis=1)
        if name == "expand":
            return expand_weight[layer].astype(BF16)
        return reduce_weight[layer].T.astype(BF16)

    low_modulate = modulate_weight.astype(BF16)
    cond_columns = jnp.concatenate([step_out_own, table_own], axis=0).reshape(-1, LANES)
    cond_rows = cond_columns.shape[0]
    cond_columns = jnp.pad(cond_columns, ((0, -cond_rows % 16), (0, 0)))
    packed, step_in, near_columns, near_modulate, matrix = run_head(
        padded(vector), step_in_own.reshape(-1, LANES), cond_columns, low_modulate, shard("attn", 0), 0
    )
    near_modulate = near_modulate.reshape(-1, modulate_weight.shape[1])
    near_columns = near_columns[:, :cond_rows].reshape(-1, depth + CLASSES, columns)
    near_columns = near_columns.swapaxes(0, 1).reshape(depth + CLASSES, -1)
    packed = packed.reshape(packed.shape[0], -1)[:, : vector.shape[0]]
    step_in = step_in.reshape(-1, FREQ, columns)
    first_of_tp = packed.reshape(fsdp_count, tp_count, -1)[:, 0]
    steps_all = first_of_tp[:, :group].reshape(-1).astype(jnp.int32)
    labels_all = first_of_tp[:, group : 2 * group].reshape(-1).astype(jnp.int32)
    at = 2 * group + bias_vector.shape[0]
    bias = packed[:, 2 * group : at].reshape(-1)

    def rows_of(block):
        return block.reshape(-1, CH, columns).swapaxes(0, 1).reshape(CH, -1).astype(BF16)

    patch_in_low = rows_of(packed[:, at : at + CH * columns])
    patch_out_low = rows_of(packed[:, at + CH * columns :])
    step_in_low = step_in.swapaxes(0, 1).reshape(FREQ, -1)
    ada_bias, layer_bias, step_in_bias, step_out_bias, patch_bias = split_bias(bias)

    def gather(shards):
        packed = jnp.concatenate(shards, axis=1)
        whole = lax.all_gather(packed, (TP, FSDP), axis=0, tiled=True)
        return whole.reshape(tp_count, -1, packed.shape[1])

    hidden = expand_weight.shape[2]
    width = hidden + cols_qkv + out_weight.shape[1]
    first_half = gather([shard("expand", 0), shard("reduce", 0)])
    second_attn = gather([hold(shard("attn", 1), matrix)])
    attn_width = width - hidden
    pieces = {
        ("attn", 0): (matrix, 0, attn_width),
        ("expand", 0): (first_half, 0, hidden),
        ("reduce", 0): (first_half, hidden, hidden),
        ("attn", 1): (second_attn, 0, attn_width),
    }

    features = step_features(steps_all).astype(BF16)
    step_pre = contract(features, step_in_low, "gf,fd->gd") + step_in_bias
    step_hidden = jax.nn.silu(step_pre).astype(BF16)
    onehot = (labels_all[:, None] == jnp.arange(CLASSES, dtype=jnp.int32)[None, :]).astype(F32)
    wide = tp_count * columns
    near_bias = jnp.take(
        step_out_bias.reshape(-1, 4 * wide), fsdp_rank // 4, axis=0
    )
    cond_near = (
        contract(step_hidden, near_columns[:depth], "gd,de->ge")
        + near_bias
        + contract(onehot.astype(BF16), near_columns[depth:], "gc,cd->gd")
    )
    place = (fsdp_rank % 4) * wide
    act_near = jax.nn.silu(cond_near).astype(BF16)
    act_own = lax.dynamic_slice_in_dim(act_near, place, wide, axis=1)
    far = far_flips()
    far_order = jnp.array([flip[0] for flip in far]) ^ fsdp_rank
    act_far = jnp.take(act_near.reshape(fsdp_count, group, -1), far_order, axis=0)
    mod_part = contract(
        act_far.reshape(len(far) * group, -1), near_modulate, "gd,de->ge"
    ).reshape(len(far), group, -1)
    mod_sum = mod_part[0]
    for k, flip in list(enumerate(far))[1:]:
        mod_sum = mod_sum + swap(mod_part[k].astype(BF16), flip).astype(F32)
    mods = exchange_tp(mod_sum.reshape(tp_count, own, -1)).swapaxes(0, 1).reshape(own, -1) + ada_bias
    mods = mods.reshape(own, 6 * LAYERS + 2, -1)
    steps_own = lax.dynamic_slice_in_dim(timesteps, tp_rank * own, own)
    signal, spread_level = noise_levels(steps_own)
    noisy = (
        signal[:, None, None] * clean_patches + spread_level[:, None, None] * noise_patches
    ).astype(BF16)
    stream = contract(noisy, patch_in_low, "gtc,cd->gtd") + patch_bias + place_table()[None]
    stream = stream.reshape(-1, depth)
    kept = [None] * LAYERS

    for layer in range(LAYERS):
        modulation = mods[:, 6 * layer : 6 * layer + 6]
        out_bias, expand_bias, reduce_bias = [value[None] for value in layer_bias[layer]]
        seq_a, qkv, lse, att, branch_a, mid, seq_m = run_attn_forward(
            stream, modulation, out_bias, pieces["attn", layer], cols_qkv, None
        )
        pre, acted, branch_m, after = run_mlp_forward(
            seq_m,
            mid,
            modulation,
            expand_bias,
            reduce_bias,
            pieces["expand", layer],
            pieces["reduce", layer],
            None,
        )
        if layer == 0:
            second_half = jnp.concatenate([shard("expand", 1), shard("reduce", 1)], axis=1)
            second_half = gather([hold(second_half, att)])
            pieces["expand", 1] = (second_half, 0, hidden)
            pieces["reduce", 1] = (second_half, hidden, hidden)
        kept[layer] = (stream, seq_a, qkv, lse, att, branch_a, mid, seq_m, pre, acted, branch_m)
        stream = after
    cond_matrix = jnp.concatenate([step_out_own, table_own], axis=0).T
    total = float(latents * length * CH)
    grad_stream, grad_final_mod, grad_patch_out, loss_rows = run_final(
        stream, mods[:, 6 * LAYERS :], noise_patches, patch_out_low, 2.0 / total
    )
    loss_local = jnp.sum(loss_rows)

    sums, reduced = ({}, {})

    def step(*wanted):
        return lambda done=None: [sent for key in wanted for sent in sums[key].step()]

    def finish(keys, array):
        if array is not None:
            wait_for(keys, array)
        return [sums[key].finish() for key in keys]

    def in_turn(steps, finished):
        return lambda done=None: steps() + finish(finished, None if done is None else done[0])

    def mlp_backward(layer, grad, afters):
        stream, seq_a, qkv, lse, att, branch_a, mid, seq_m, pre, acted, branch_m = kept[layer]
        out_bias, expand_bias, reduce_bias = [value[None] for value in layer_bias[layer]]
        return run_mlp_backward(
            grad,
            branch_m,
            pre,
            mid,
            branch_a,
            mods[:, 6 * layer : 6 * layer + 6],
            reduce_bias,
            out_bias,
            pieces["expand", layer],
            pieces["reduce", layer],
            afters,
        )

    mod_grads = [None] * LAYERS
    layer_bias_grads = [None] * LAYERS
    cols_out = out_weight.shape[1]
    halves = 2 if cols_qkv // 2 % LANES == 0 else 1
    qkv_keys = [[("qkv", layer, i) for i in range(halves)] for layer in range(LAYERS)]
    rest_keys = [[("reduce", layer, 0), ("expand", layer, 0), ("out", layer, 0)] for layer in range(LAYERS)]
    mlp_afters = [
        (step(*rest_keys[1]), in_turn(step(*qkv_keys[1], *rest_keys[1][1:]), rest_keys[1][:1])),
        None,
    ]
    grad_afters = [[step(), step(*qkv_keys[1]), step(*qkv_keys[1])], [step()] * 3]

    attn_afters = [
        (step(*rest_keys[0][:2]), in_turn(step(rest_keys[0][2]), qkv_keys[1])),
        (step(rest_keys[1][0]), step(rest_keys[1][1])),
    ]

    def wait_for(keys, array):
        for key in keys:
            sums[key].keep = hold(sums[key].keep, array)

    def start(name, layer, left, right, width, firsts, after):
        started = start_sums(left, right, width, firsts, list(after))
        for i, total_sum in enumerate(started):
            sums[name, layer, i] = total_sum

    for layer in reversed(range(LAYERS)):
        stream, seq_a, qkv, lse, att, branch_a, mid, seq_m, pre, acted, branch_m = kept[layer]
        seq_grad_m, grad_pre, grad_mid, seq_grad_a, mod_late, d_out, d_expand, d_reduce = mlp_backward(
            layer, grad_stream, mlp_afters[layer]
        )
        after = grad_afters[layer]
        if layer == LAYERS - 1:
            cond_matrix = lax.all_gather(hold(cond_matrix, seq_grad_m), everywhere, axis=0, tiled=True)
        if layer == 0:
            mod_known = [jnp.zeros_like(mod_late[:, :2]), mod_late[:, 2:]] + mod_grads[1:]
            mod_known = jnp.concatenate(mod_known + [grad_final_mod], axis=1).reshape(own, -1)
            mod_known = mod_known.astype(BF16)
            known_columns = mod_known.reshape(own, tp_count, -1).swapaxes(0, 1)
            known_columns = exchange_tp(known_columns).reshape(group, -1)
            known_columns = lax.all_gather(known_columns, FSDP, axis=0, tiled=True)
        start("reduce", layer, seq_grad_m, acted, hidden, [FSDP], after[0]())
        first = [sums["reduce", layer, 0].sent]
        start("expand", layer, seq_m, grad_pre, hidden, [TP], after[1]() + first)
        first = [sums["expand", layer, 0].sent]
        if layer == 0:
            first += finish(rest_keys[1][1:], first[0])
        start("out", layer, seq_grad_a, att, cols_out, [FSDP], after[2]() + first)
        grad_qkv, grad_stream, mod_early = run_attn_backward(
            seq_grad_a,
            qkv,
            lse,
            stream,
            grad_mid,
            mods[:, 6 * layer : 6 * layer + 6],
            pieces["attn", layer],
            cols_qkv,
            attn_afters[layer],
        )
        after = step(*(rest_keys[layer] if layer == 0 else rest_keys[layer][::2]))()
        start("qkv", layer, seq_a, grad_qkv, cols_qkv, [TP, FSDP][:halves], after)
        mod_grads[layer] = jnp.concatenate([mod_early, mod_late[:, 2:]], axis=1)
        layer_bias_grads[layer] = (d_out[0], d_expand[0], d_reduce[0])
    last_sent = [sums[key].sent for key in qkv_keys[0]]
    mod_columns = modulate_weight.shape[1]
    mod_early, grad_stream = (hold(mod_early, *last_sent), hold(grad_stream, *last_sent))
    mod_last = mod_early.reshape(own, -1).astype(BF16)
    last_columns = push([mod_last.reshape(-1, LANES)], [-(-mod_last.shape[1] // mod_columns) + 1], 3)[0]
    wait_for(qkv_keys[0] + rest_keys[0], last_columns)
    step(*qkv_keys[0], *rest_keys[0])()
    last_columns = last_columns.reshape(latents, -1)
    grad_embedded = grad_stream.astype(BF16)
    grad_patch_in = contract(noisy.reshape(-1, CH), grad_embedded, "tc,td->cd")
    grad_patch_bias = jnp.sum(grad_embedded.astype(F32), axis=0)

    last_columns = jnp.pad(last_columns, ((0, 0), (0, modulate_weight.shape[1] * tp_count - last_columns.shape[1])))
    grad_columns = known_columns + lax.dynamic_slice_in_dim(
        last_columns, tp_rank * modulate_weight.shape[1], modulate_weight.shape[1], axis=1
    )
    grad_ada = contract(act_own, grad_columns, "gd,ge->de")
    act_part = contract(grad_columns, low_modulate, "ge,de->gd").reshape(-1, own, low_modulate.shape[0])
    act_part = jnp.pad(act_part, ((0, 0), (0, -own % 8), (0, -act_part.shape[2] % LANES)))
    act_part = push([act_part], [1], 4)[0]
    act_part = act_part[:, :own, : low_modulate.shape[0]]
    act_part = jnp.sum(act_part.reshape(fsdp_count, tp_count, own, -1), axis=1).swapaxes(0, 1).reshape(own, -1)

    def of_own(value):
        return lax.dynamic_slice_in_dim(value, rank * own, own)

    cond_mine = (
        contract(of_own(step_hidden), cond_matrix[:, :depth], "gd,ed->ge")
        + step_out_bias
        + contract(of_own(onehot).astype(BF16), cond_matrix[:, depth:], "gc,dc->gd")
    )
    grad_cond = local_back(jax.nn.silu, cond_mine, act_part)
    grad_hidden = exact_dot(grad_cond, cond_matrix[:, :depth].astype(F32))
    grad_step_pre = local_back(jax.nn.silu, of_own(step_pre), grad_hidden)
    both_grads = jnp.concatenate([grad_cond, grad_step_pre], axis=0).reshape(2 * own, -1, columns)
    both_grads = jnp.pad(
        both_grads.swapaxes(0, 1), ((0, 0), (0, -2 * own % 8), (0, -columns % LANES))
    )

    pieces_bias = [
        jnp.sum(mod_known.astype(F32), axis=0)
        + jnp.pad(jnp.sum(mod_last.astype(F32), axis=0), (0, mod_known.shape[1] - mod_last.shape[1]))
    ]
    for layer in range(LAYERS):
        pieces_bias += layer_bias_grads[layer]
    pieces_bias += [jnp.zeros((2 * depth,), F32), grad_patch_bias]
    chunk = bias_vector.shape[0]
    small = jnp.concatenate(
        [
            jnp.concatenate(pieces_bias).reshape(-1, chunk),
            jnp.concatenate([grad_patch_in, grad_patch_out])
            .reshape(2 * CH, -1, columns)
            .swapaxes(0, 1)
            .reshape(-1, 2 * CH * columns),
        ],
        axis=1,
    )
    width = small.shape[1]
    small = jnp.pad(small, ((0, 0), (0, -width % (8 * LANES)))).reshape(small.shape[0], -1, LANES)
    small, both_grads = push([small, both_grads], [1, 1], 1)
    for (name, layer, i), total_sum in sums.items():
        reduced.setdefault((name, layer), []).append(total_sum.finish())
    reduced = {key: jnp.concatenate(parts, axis=1) for key, parts in reduced.items()}
    for layer in range(LAYERS):
        reduced["qkv", layer] = heads_together(reduced["qkv", layer])
    small = jnp.sum(small, axis=0).reshape(-1)[:width]
    grad_cond = both_grads[:, :own, :columns].reshape(latents, columns)
    grad_step_pre = both_grads[:, own : 2 * own, :columns].reshape(latents, columns)
    grad_table = exact_dot(onehot.T, grad_cond)
    grad_step_out = exact_dot(step_hidden.astype(F32).T, grad_cond)
    grad_step_in = exact_dot(features.astype(F32).T, grad_step_pre)
    step_bias_grads = jnp.concatenate([jnp.sum(grad_step_pre, axis=0), jnp.sum(grad_cond, axis=0)])
    bias_grad = small[:chunk]
    patch_grads = small[chunk:].reshape(2 * CH, columns)
    embed_grad = jnp.concatenate(
        [grad_step_in, grad_step_out, patch_grads[:CH], grad_table, patch_grads[CH:]], axis=0
    )
    grads = (
        jnp.stack([reduced["qkv", i] for i in range(LAYERS)]),
        jnp.stack([reduced["out", i].T for i in range(LAYERS)]),
        jnp.stack([reduced["expand", i] for i in range(LAYERS)]),
        jnp.stack([reduced["reduce", i].T for i in range(LAYERS)]),
        grad_ada,
        embed_grad,
        bias_grad,
    )
    square = jnp.zeros((), jnp.float32)
    for grad in grads:
        square = square + jnp.sum(grad * grad)
    square = square + jnp.sum(step_bias_grads * step_bias_grads)
    last = push([padded(jnp.concatenate([square[None], loss_local[None], step_bias_grads]))], [0], 2)[0]
    last = last.reshape(last.shape[0], -1)
    square, loss_total = jnp.sum(last[:, 0]), jnp.sum(last[:, 1])
    step_biases = [last[:, 2 : 2 + columns].reshape(-1), last[:, 2 + columns : 2 + 2 * columns].reshape(-1)]
    before = jnp.zeros((bias.shape[0] - 3 * depth,), F32)
    step_biases = jnp.concatenate([before] + step_biases + [jnp.zeros((depth,), F32)])
    bias_grad = bias_grad + lax.dynamic_slice_in_dim(step_biases, rank * chunk, chunk)
    grads = grads[:-1] + (bias_grad,)
    grad_norm = jnp.sqrt(square)
    factor = CLIP_AT / jnp.maximum(grad_norm, CLIP_AT)
    params = (
        qkv_weight,
        out_weight,
        expand_weight,
        reduce_weight,
        modulate_weight,
        embed_weight,
        bias_vector,
    )
    firsts = (
        qkv_first,
        out_first,
        expand_first,
        reduce_first,
        modulate_first,
        embed_first,
        bias_first,
    )
    seconds = (
        qkv_second,
        out_second,
        expand_second,
        reduce_second,
        modulate_second,
        embed_second,
        bias_second,
    )
    news = [adam(w, f, s, g, factor) for w, f, s, g in zip(params, firsts, seconds, grads)]
    qkv_moment, qkv_square, qkv_master = news[0]
    out_moment, out_square, out_master = news[1]
    expand_moment, expand_square, expand_master = news[2]
    reduce_moment, reduce_square, reduce_master = news[3]
    modulate_moment, modulate_square, modulate_master = news[4]
    embed_moment, embed_square, embed_master = news[5]
    bias_moment, bias_square, bias_master = news[6]
    return (
        loss_total,
        grad_norm,
        qkv_moment,
        qkv_square,
        qkv_master,
        out_moment,
        out_square,
        out_master,
        expand_moment,
        expand_square,
        expand_master,
        reduce_moment,
        reduce_square,
        reduce_master,
        modulate_moment,
        modulate_square,
        modulate_master,
        embed_moment,
        embed_square,
        embed_master,
        bias_moment,
        bias_square,
        bias_master,
        qkv_master.astype(jnp.bfloat16),
        out_master.astype(jnp.bfloat16),
        expand_master.astype(jnp.bfloat16),
        reduce_master.astype(jnp.bfloat16),
        modulate_master.astype(jnp.bfloat16),
        embed_master.astype(jnp.bfloat16),
    )


def solution(mesh):
    return jax.shard_map(
        per_device,
        mesh=mesh,
        in_specs=(
            P((FSDP, TP), None, None),
            P((FSDP, TP), None, None),
            P(FSDP),
            P(FSDP),
            P(None, FSDP, TP),
            P(None, TP, FSDP),
            P(None, FSDP, TP),
            P(None, TP, FSDP),
            P(FSDP, TP),
            P(None, (FSDP, TP)),
            P((FSDP, TP)),
            P(None, FSDP, TP),
            P(None, TP, FSDP),
            P(None, FSDP, TP),
            P(None, TP, FSDP),
            P(FSDP, TP),
            P(None, (FSDP, TP)),
            P((FSDP, TP)),
            P(None, FSDP, TP),
            P(None, TP, FSDP),
            P(None, FSDP, TP),
            P(None, TP, FSDP),
            P(FSDP, TP),
            P(None, (FSDP, TP)),
            P((FSDP, TP)),
        ),
        out_specs=(
            P(),
            P(),
            P(None, FSDP, TP),
            P(None, FSDP, TP),
            P(None, FSDP, TP),
            P(None, TP, FSDP),
            P(None, TP, FSDP),
            P(None, TP, FSDP),
            P(None, FSDP, TP),
            P(None, FSDP, TP),
            P(None, FSDP, TP),
            P(None, TP, FSDP),
            P(None, TP, FSDP),
            P(None, TP, FSDP),
            P(FSDP, TP),
            P(FSDP, TP),
            P(FSDP, TP),
            P(None, (FSDP, TP)),
            P(None, (FSDP, TP)),
            P(None, (FSDP, TP)),
            P((FSDP, TP)),
            P((FSDP, TP)),
            P((FSDP, TP)),
            P(None, FSDP, TP),
            P(None, TP, FSDP),
            P(None, FSDP, TP),
            P(None, TP, FSDP),
            P(FSDP, TP),
            P(None, (FSDP, TP)),
        ),
        check_vma=False,
    )
```
